128 devices in a mesh: tensor: 2 (over core), dp: 4 (over x), context: 16 (over z, y).
Axes of the slice: x: 4, y: 4, z: 4, core: 2. Of those that a mesh axis runs over, the one named last changes fastest.
Arguments:
- hidden_in: bfloat16 [16384, 1024], P(('dp', 'context'), 'tensor'), may hold values from -6 to 6
- segment_ids: int32 [16384], P(('dp', 'context')), may hold values from 0 to 2, as said below
- norm_gain: float32 [1024], replicated, may hold values from 0.25 to 1.75
- in_weight: bfloat16 [1024, 2, 2048], P(None, None, 'tensor'), may hold values from -0.1875 to 0.1875
- bc_weight: bfloat16 [1024, 2, 128], replicated, may hold values from -0.1875 to 0.1875
- step_weight: bfloat16 [1024, 32], P(None, 'tensor'), may hold values from -0.1875 to 0.1875
- conv_weight: float32 [4, 2048], P(None, 'tensor'), may hold values from -3 to 3
- conv_bias: float32 [2048], P('tensor'), may hold values from -3 to 3
- bc_conv_weight: float32 [4, 2, 128], replicated, may hold values from -3 to 3
- bc_conv_bias: float32 [2, 128], replicated, may hold values from -3 to 3
- step_bias: float32 [32], replicated, may hold values from -6.5 to -2.5
- decay_log: float32 [32], P('tensor'), may hold values from -1.5 to 2.5
- skip_gain: float32 [32], P('tensor'), may hold values from 0.5 to 2
- gate_gain: float32 [2048], P('tensor'), may hold values from 0.25 to 1.75
- out_weight: bfloat16 [2048, 1024], P('tensor'), may hold values from -0.125 to 0.125
- out_grad: bfloat16 [16384, 1024], P(('dp', 'context'), 'tensor'), may hold values from -6 to 6
Outputs:
- hidden_out: bfloat16 [16384, 1024], P(('dp', 'context'), 'tensor')
- hidden_grad: bfloat16 [16384, 1024], P(('dp', 'context'), 'tensor')
- grad_norm_gain: float32 [1024], P('tensor')
- grad_in_weight: float32 [1024, 2, 2048], P(None, None, 'tensor')
- grad_bc_weight: float32 [1024, 2, 128], P('tensor')
- grad_step_weight: float32 [1024, 32], P(None, 'tensor')
- grad_conv_weight: float32 [4, 2048], P(None, 'tensor')
- grad_conv_bias: float32 [2048], P('tensor')
- grad_bc_conv_weight: float32 [4, 2, 128], replicated
- grad_bc_conv_bias: float32 [2, 128], replicated
- grad_step_bias: float32 [32], P('tensor')
- grad_decay_log: float32 [32], P('tensor')
- grad_skip_gain: float32 [32], P('tensor')
- grad_gate_gain: float32 [2048], P('tensor')
- grad_out_weight: float32 [2048, 1024], P('tensor')
The draws below stay inside these ranges and needn't reach their ends.
Inputs may be any that keep to these rules, and one draw needn't show every extreme that they name: `segment_ids`: each group of 4096 tokens (one index of dp) holds three documents with ids 0, 1, 2 in order, never falling; the first and the last are each 1 to 128 tokens long, so the middle one starts in the group's first context piece and ends in its last.
All inputs are finite; a program needn't handle non-finite values.
Results may differ from the reference program's by a relative error of at most 0.013.
Values may be sent and summed in bfloat16 or wider, within the bound.
No kernel may reach another device: no remote copies, remote signals or barrier semaphores. Data moves between devices by JAX's collectives and lax.ppermute only.
A program may use at most 128 MiB of HBM per device.

```python
import jax
import jax.numpy as jnp
from jax import lax

D = 1024
HEADS = 32
HEAD = 64
STATE = 128
CONV = 4
BLOCK = 256
TOK_DEV = 256
INNER = 2048
GROUP = 4096
TOKENS = 16384


def draw_segment_ids(key, part):
    key = jax.random.fold_in(key, 7)
    first_key, second_key = jax.random.split(key)
    groups = TOKENS // GROUP
    first_end = jax.random.randint(first_key, (groups, 1), 1, TOK_DEV // 2 + 1)
    second_end = jax.random.randint(second_key, (groups, 1), GROUP - TOK_DEV // 2, GROUP)
    places = jnp.arange(GROUP, dtype=jnp.int32)[None, :]
    doc_ids = (places >= first_end).astype(jnp.int32) + (places >= second_end).astype(jnp.int32)
    return doc_ids.reshape(TOKENS)


def steps_of(stream_key, dims, shards, least, largest):
    gain = 1.0
    for position, parts in shards:
        steps = jax.random.uniform(jax.random.fold_in(jax.random.fold_in(stream_key, 6), position), (parts,), jnp.float32, least / len(shards), largest / len(shards))
        gain = gain * jnp.repeat(jnp.exp(steps), dims[position] // parts).reshape((-1,) + (1,) * (len(dims) - 1 - position))
    return gain


def gaussian(stream_key, extent, scale, bound, cuts=(), held_as=jnp.bfloat16):
    factor_of = steps_of(stream_key, extent, cuts, -0.22, 0.18) if cuts else 1.0
    entries = jax.random.normal(stream_key, extent, jnp.float32) * scale * factor_of
    return jnp.minimum(jnp.maximum(entries, -bound), bound).astype(held_as)


def setup_inputs(seed: int = 0) -> dict:
    splits = jax.random.split(jax.random.key(seed), 17)
    hidden_in = gaussian(splits[0], (TOKENS, D), 1.0, 6.0, ((0, 64), (1, 2)))
    segment_ids = draw_segment_ids(jax.random.fold_in(splits[16], 71), 0)
    norm_gain = jnp.clip(1.0 + 0.15 * jax.random.normal(splits[2], (D,), jnp.float32), 0.25, 1.75)
    in_weight = gaussian(splits[3], (D, 2, INNER), D ** -0.5, 0.1875, ((2, 2),))
    bc_weight = gaussian(splits[4], (D, 2, STATE), D ** -0.5, 0.1875)
    step_weight = gaussian(splits[5], (D, HEADS), D ** -0.5, 0.1875, ((1, 2),))
    conv_weight = gaussian(splits[6], (CONV, INNER), CONV ** -0.5, 3.0, ((1, 2),), jnp.float32)
    conv_bias = gaussian(splits[7], (INNER,), 0.5, 3.0, ((0, 2),), jnp.float32)
    bc_conv_weight = gaussian(splits[8], (CONV, 2, STATE), CONV ** -0.5, 3.0, (), jnp.float32)
    bc_conv_bias = gaussian(splits[9], (2, STATE), 0.5, 3.0, (), jnp.float32)
    step_bias = jnp.clip(jax.random.uniform(splits[10], (HEADS,), jnp.float32, -6.5, -2.5), -6.5, -2.5)
    decay_log = jnp.clip(-1.5 + 4.0 * jax.random.uniform(splits[11], (HEADS,), jnp.float32) ** steps_of(splits[11], (HEADS,), ((0, 2),), -0.2, 0.2), -1.5, 2.5)
    skip_gain = jnp.clip(0.5 + 1.5 * jax.random.uniform(splits[12], (HEADS,), jnp.float32) ** steps_of(splits[12], (HEADS,), ((0, 2),), -0.2, 0.2), 0.5, 2.0)
    gate_gain = jnp.clip(1.0 + 0.15 * jax.random.normal(splits[13], (INNER,), jnp.float32), 0.25, 1.75)
    out_weight = gaussian(splits[14], (INNER, D), INNER ** -0.5, 0.125, ((0, 2),))
    out_grad = gaussian(splits[15], (TOKENS, D), 1.0, 6.0, ((0, 64), (1, 2)))
    return {"hidden_in": hidden_in, "segment_ids": segment_ids, "norm_gain": norm_gain, "in_weight": in_weight, "bc_weight": bc_weight, "step_weight": step_weight, "conv_weight": conv_weight, "conv_bias": conv_bias, "bc_conv_weight": bc_conv_weight, "bc_conv_bias": bc_conv_bias, "step_bias": step_bias, "decay_log": decay_log, "skip_gain": skip_gain, "gate_gain": gate_gain, "out_weight": out_weight, "out_grad": out_grad}


@jax.custom_vjp
def low(v):
    return lax.optimization_barrier(v.astype(jnp.bfloat16)).astype(jnp.float32)

@jax.custom_vjp
def low_back(v):
    return v

def low_keep(v):
    return (low(v), None)

def low_pass(kept, grad):
    return (grad,)

def back_keep(v):
    return (v, None)

def back_low(kept, grad):
    return (low(grad),)
low.defvjp(low_keep, low_pass)
low_back.defvjp(back_keep, back_low)
epsilon = 1e-05
highest = lax.Precision.HIGHEST

def conv_layer(extended, weights, biases, ext_segs):
    row_count = extended.shape[0] - (CONV - 1)
    running = jnp.zeros((row_count, extended.shape[1]), jnp.float32) + biases[None, :]
    for offset in range(CONV):
        same_doc = (ext_segs[offset:offset + row_count] == ext_segs[CONV - 1:CONV - 1 + row_count]).astype(jnp.float32)
        running = running + weights[offset][None, :] * extended[offset:offset + row_count] * same_doc[:, None]
    return jax.nn.silu(running)

def rate_piece(raw_values, bias_values, log_rates):
    step_vals = jax.nn.softplus(raw_values + bias_values[None, :])
    return (step_vals, step_vals * (-jnp.exp(log_rates))[None, :])

def block_pieces(x_blocks, b_blocks, c_blocks, step_blocks, decay_blocks, block_segs, before_segs):
    block_len = x_blocks.shape[1]
    cumulative = jnp.cumsum(decay_blocks, axis=1)
    by_head = jnp.transpose(cumulative, (0, 2, 1))
    positions = jnp.arange(block_len)
    causal = positions[:, None] >= positions[None, :]
    pair_mask = ((block_segs[:, :, None] == block_segs[:, None, :]) & causal[None])[:, None]
    spread = by_head[:, :, :, None] - by_head[:, :, None, :]
    decay_pairs = jnp.where(pair_mask, jnp.exp(jnp.where(pair_mask, spread, 0.0)), 0.0)
    products_cb = jnp.einsum('kin,kjn->kij', c_blocks, b_blocks, precision=highest)
    scaled = x_blocks * step_blocks[..., None]
    within_block = jnp.einsum('khij,kjhp->kihp', decay_pairs * products_cb[:, None], scaled, precision=highest)
    end_weight = jnp.exp(cumulative[:, -1:, :] - cumulative) * (block_segs == block_segs[:, -1:]).astype(jnp.float32)[..., None]
    block_states = jnp.einsum('kjhp,kjn->khpn', scaled * end_weight[..., None], b_blocks, precision=highest)
    block_gains = jnp.exp(cumulative[:, -1, :]) * (block_segs[:, -1] == before_segs).astype(jnp.float32)[:, None]
    entry_decay = jnp.exp(cumulative) * (block_segs == before_segs[:, None]).astype(jnp.float32)[..., None]
    return (within_block, block_states, block_gains, entry_decay)

def block_starts(block_gains, block_states, start_state):

    def fold_step(carried, step_item):
        return (step_item[0][:, None, None] * carried + step_item[1], carried)
    return lax.scan(fold_step, start_state, (block_gains, block_states))[1]

def gate_input(within_block, entry_decay, c_blocks, starts, x_blocks, skip_vals, gate_z):
    from_state = jnp.einsum('kin,khpn->kihp', c_blocks, starts, precision=highest)
    mixed = within_block + entry_decay[..., None] * from_state + skip_vals[None, None, :, None] * x_blocks
    return mixed.reshape(gate_z.shape) * jax.nn.silu(gate_z)

def group_forward(params, hidden, seg_ids):
    norm_gain, in_weight, bc_weight, step_weight, conv_weight, conv_bias, bc_conv_weight, bc_conv_bias, step_bias, decay_log, skip_gain, gate_gain, out_weight = params
    token_count = hidden.shape[0]
    block_count = token_count // BLOCK
    mean_sq = lax.optimization_barrier(jnp.mean(hidden * hidden, axis=-1, keepdims=True))
    normed = low(hidden * lax.rsqrt(mean_sq + epsilon) * norm_gain[None, :])
    projected = low_back(jnp.dot(normed, in_weight.reshape(D, 2 * INNER), precision=highest))
    bc_raw = low_back(jnp.dot(normed, bc_weight.reshape(D, 2 * STATE), precision=highest))
    step_raw = low_back(jnp.dot(normed, step_weight, precision=highest))
    joined = jnp.concatenate([projected[:, :INNER], bc_raw], axis=1)
    seg_float = seg_ids.astype(jnp.float32) + 1.0
    extended = jnp.concatenate([jnp.zeros((CONV - 1, joined.shape[1]), jnp.float32), joined], axis=0)
    ext_segs = jnp.concatenate([jnp.zeros((CONV - 1,), jnp.float32), seg_float])
    weights = jnp.concatenate([conv_weight, bc_conv_weight.reshape(CONV, 2 * STATE)], axis=1)
    biases = jnp.concatenate([conv_bias, bc_conv_bias.reshape(2 * STATE)])
    activated = conv_layer(extended, weights, biases, ext_segs)
    step_vals, decay_vals = rate_piece(step_raw, step_bias, decay_log)
    x_blocks = activated[:, :INNER].reshape(block_count, BLOCK, HEADS, HEAD)
    b_blocks = activated[:, INNER:INNER + STATE].reshape(block_count, BLOCK, STATE)
    c_blocks = activated[:, INNER + STATE:].reshape(block_count, BLOCK, STATE)
    step_blocks = step_vals.reshape(block_count, BLOCK, HEADS)
    decay_blocks = decay_vals.reshape(block_count, BLOCK, HEADS)
    block_segs = seg_float.reshape(block_count, BLOCK)
    before_segs = jnp.concatenate([jnp.zeros((1,), jnp.float32), block_segs[:-1, -1]])
    within_block, block_states, block_gains, entry_decay = block_pieces(x_blocks, b_blocks, c_blocks, step_blocks, decay_blocks, block_segs, before_segs)
    zero_state = jnp.zeros((HEADS, HEAD, STATE), jnp.float32)
    starts = block_starts(block_gains, block_states, zero_state)
    gated_vals = gate_input(within_block, entry_decay, c_blocks, starts, x_blocks, skip_gain, projected[:, INNER:])
    mean_gate = lax.optimization_barrier(jnp.mean(gated_vals * gated_vals, axis=-1, keepdims=True))
    gnorm = low(gated_vals * lax.rsqrt(mean_gate + epsilon) * gate_gain[None, :])
    return hidden + jnp.dot(gnorm, out_weight, precision=highest)

def reference(hidden_in, segment_ids, norm_gain, in_weight, bc_weight, step_weight, conv_weight, conv_bias, bc_conv_weight, bc_conv_bias, step_bias, decay_log, skip_gain, gate_gain, out_weight, out_grad):
    params = tuple((weight_arg.astype(jnp.float32) for weight_arg in (norm_gain, in_weight, bc_weight, step_weight, conv_weight, conv_bias, bc_conv_weight, bc_conv_bias, step_bias, decay_log, skip_gain, gate_gain, out_weight)))
    group_total = TOKENS // GROUP
    hidden = hidden_in.astype(jnp.float32).reshape(group_total, GROUP, D)
    seg_groups = segment_ids.reshape(group_total, GROUP)
    checkpointed = jax.checkpoint(group_forward)

    def forward_all(weights_all, hidden_all):

        def one_group(group_pair):
            return checkpointed(weights_all, group_pair[0], group_pair[1])
        return lax.map(one_group, (hidden_all, seg_groups))
    result, pullback = jax.vjp(forward_all, params, hidden)
    gradients, d_hidden = pullback(out_grad.astype(jnp.float32).reshape(group_total, GROUP, D))
    return (result.reshape(TOKENS, D).astype(jnp.bfloat16), d_hidden.reshape(TOKENS, D).astype(jnp.bfloat16), gradients[0], gradients[1], gradients[2], gradients[3], gradients[4], gradients[5], gradients[6], gradients[7], gradients[8], gradients[9], gradients[10], gradients[11], gradients[12])
```

```python
import jax
import jax.numpy as jnp
from jax import lax
from jax.experimental import pallas as pl
from jax.experimental.pallas import tpu as pltpu
from jax.sharding import Mesh
from jax.sharding import PartitionSpec as P

D = 1024
HEAD = 64
STATE = 128
INNER = 2048
ROWS = 256
HEADS = 16
LOCAL = 1024
HALO = 16
EXT = ROWS + HALO
LANES = 128
PAIRS = LOCAL // LANES
CHUNK = 80
DEVICES = 64
CONTEXT = ("context_0", "context_1")
EVERYONE = ("dp", "context_0", "context_1")
EPSILON = 1e-05
f32 = jnp.float32
bf16 = jnp.bfloat16
HIGHEST = lax.Precision.HIGHEST


def mm(a, b):
    return lax.dot_general(a, b, (((1,), (0,)), ((), ())), preferred_element_type=f32)


def nt(a, b):
    return lax.dot_general(a, b, (((1,), (1,)), ((), ())), preferred_element_type=f32)


def tn(a, b):
    return lax.dot_general(a, b, (((0,), (0,)), ((), ())), preferred_element_type=f32)


def exact(a, b):
    return lax.dot_general(
        a, b, (((1,), (0,)), ((), ())), precision=HIGHEST, preferred_element_type=f32
    )


def whole(shape):
    return pl.BlockSpec(shape, lambda i: (0,) * len(shape), pipeline_mode=pl.Buffered(1))


def kernel_call(body, outs, args, scratch=(), flops=0, vmem=56):
    return pl.pallas_call(
        body,
        grid=(1,),
        out_shape=[jax.ShapeDtypeStruct(shape, kind) for shape, kind in outs],
        in_specs=[whole(a.shape) for a in args],
        out_specs=[whole(shape) for shape, _ in outs],
        scratch_shapes=list(scratch),
        compiler_params=pltpu.CompilerParams(vmem_limit_bytes=vmem * 1024 * 1024),
        cost_estimate=pl.CostEstimate(
            flops=flops,
            bytes_accessed=0,
            transcendentals=0,
        ),
    )(*args)


def lane_index(shape):
    return lax.broadcasted_iota(jnp.int32, shape, 1)


def row_index(shape):
    return lax.broadcasted_iota(jnp.int32, shape, 0)


def spread_pair(columns, pair):
    rows = columns.shape[0]
    first = jnp.broadcast_to(columns[:, 2 * pair : 2 * pair + 1], (rows, LANES))
    second = jnp.broadcast_to(columns[:, 2 * pair + 1 : 2 * pair + 2], (rows, LANES))
    return jnp.where(lane_index((rows, LANES)) < HEAD, first, second)


def pair_mask(documents, seg_row):
    shape = (ROWS, ROWS)
    causal = row_index(shape) >= lane_index(shape)
    columns = jnp.concatenate([documents, documents], axis=1)
    return jnp.where((columns == seg_row) & causal, 0.0, -1e30).astype(f32)


def decay_block(cum, cum_t, head, bias):
    return jnp.exp(cum[:, head : head + 1] - cum_t[head : head + 1, :] + bias)


def document_before():
    piece = lax.axis_index("context_0") * 4 + lax.axis_index("context_1")
    return jnp.where(piece > 0, 2.0, 0.0).astype(f32)


def documents_of(seg_ref):
    seg_row = seg_ref[...].astype(f32) + 1.0
    return seg_row, jnp.broadcast_to(seg_row, (LANES, ROWS)).T


def tap_masks_of(documents, ext_ref):
    ext_ref[:8, :] = jnp.full((8, LANES), document_before(), f32)
    ext_ref[8:, :] = documents
    return [(ext_ref[5 + k : 5 + k + ROWS, :] == documents).astype(f32) for k in range(3)]


def end_decay(cum, documents):
    last = (documents == documents[ROWS - 1 : ROWS, :]).astype(f32)
    return jnp.exp(cum[ROWS - 1 : ROWS, :] - cum) * last


def entry_decay(cum, documents):
    return jnp.exp(cum) * (documents == document_before()).astype(f32)


def to_lanes(values):
    rows, count = values.shape
    return jnp.concatenate([values, jnp.zeros((rows, LANES - count), f32)], axis=1)


def front_body(
    hidden_ref,
    halo_ref,
    gain_ref,
    win_ref,
    wbc_ref,
    wst_ref,
    taps_ref,
    bias_ref,
    bc_taps_ref,
    bc_bias_ref,
    seg_ref,
    step_bias_ref,
    decay_log_ref,
    normed_ref,
    joined_ref,
    pre_ref,
    gate_ref,
    b_ref,
    c_ref,
    step_ref,
    cum_ref,
    sig_ref,
    decay_ref,
    state_ref,
    ext_ref,
    wide_ref,
):
    gain = gain_ref[...]
    for source, start, rows in ((halo_ref, 0, HALO), (hidden_ref, HALO, ROWS)):
        values = source[...].astype(f32)
        scale = lax.rsqrt(jnp.sum(values * values, axis=1, keepdims=True) / D + EPSILON)
        normed_ref[start : start + rows, :] = (values * scale * gain).astype(bf16)
    normed_ext = normed_ref[...]
    normed = normed_ref[HALO:, :]
    joined_ref[:, :LOCAL] = mm(normed_ext, win_ref[:, :LOCAL])
    joined_ref[:, LOCAL:] = mm(normed_ext, wbc_ref[...])
    gate_ref[...] = mm(normed, win_ref[:, LOCAL:])
    wide_ref[...] = jnp.zeros_like(wide_ref)
    wide_ref[:, :HEADS] = wst_ref[...]
    both = step_bias_ref[...]
    first = lax.axis_index("tensor") == 0
    local_bias = jnp.where(first, both[:, :HEADS], both[:, HEADS:])
    raw = mm(normed, wide_ref[...]) + to_lanes(local_bias)
    step = jnp.maximum(raw, 0.0) + jnp.log1p(jnp.exp(-jnp.abs(raw)))
    decay = step * to_lanes(-jnp.exp(decay_log_ref[...]))
    tri = (row_index((ROWS, ROWS)) >= lane_index((ROWS, ROWS))).astype(f32)
    cum = exact(tri, decay)
    step_ref[...] = step
    cum_ref[...] = cum
    sig_ref[...] = jax.nn.sigmoid(raw)
    decay_ref[...] = decay
    _, documents = documents_of(seg_ref)
    tap_masks = tap_masks_of(documents, ext_ref)

    def conv(at, taps, bias):
        lanes = slice(at, at + LANES)
        total = jnp.broadcast_to(bias, (ROWS, LANES))
        for k in range(4):
            part = joined_ref[HALO - 3 + k : HALO - 3 + k + ROWS, lanes] * taps[k : k + 1]
            total = total + (part * tap_masks[k] if k < 3 else part)
        pre_ref[:, lanes] = total
        return total * jax.nn.sigmoid(total)

    b_low = conv(LOCAL, bc_taps_ref[:, :STATE], bc_bias_ref[:, :STATE]).astype(bf16)
    c_low = conv(LOCAL + STATE, bc_taps_ref[:, STATE:], bc_bias_ref[:, STATE:]).astype(bf16)
    b_ref[...] = b_low
    c_ref[...] = c_low
    gains = jnp.exp(cum[ROWS - 1 : ROWS, :])
    ended = step * end_decay(cum, documents)
    for pair in range(PAIRS):
        lanes = slice(pair * LANES, (pair + 1) * LANES)
        x = conv(pair * LANES, taps_ref[:, lanes], bias_ref[:, lanes])
        state = tn((x * spread_pair(ended, pair)).astype(bf16), b_low).astype(bf16)
        for side in range(2):
            head = 2 * pair + side
            state_ref[head, :HEAD, :] = state[side * HEAD : (side + 1) * HEAD, :]
            state_ref[head, HEAD:, :] = jnp.broadcast_to(
                gains[:, head : head + 1], (CHUNK - HEAD, STATE)
            ).astype(bf16)


def within_body(pre_ref, step_ref, cum_ref, b_ref, c_ref, seg_ref, skip_ref, within_ref):
    seg_row, documents = documents_of(seg_ref)
    products = nt(c_ref[...], b_ref[...])
    bias = pair_mask(documents, seg_row)
    step = step_ref[...]
    cum = cum_ref[...]
    cum_t = cum.T
    skip = skip_ref[...]
    first_half = lane_index((ROWS, LANES)) < HEAD
    for pair in range(PAIRS):
        lanes = slice(pair * LANES, (pair + 1) * LANES)
        pre = pre_ref[:, lanes]
        x = pre * jax.nn.sigmoid(pre)
        xs_low = (x * spread_pair(step, pair)).astype(bf16)
        sums = []
        for head in (2 * pair, 2 * pair + 1):
            block = (decay_block(cum, cum_t, head, bias) * products).astype(bf16)
            sums.append(mm(block, xs_low))
        within_ref[:, lanes] = (
            jnp.where(first_half, sums[0], sums[1]) + spread_pair(skip, pair) * x
        )


def scan_body(pieces_ref, start_ref):
    state = jnp.zeros((HEAD, STATE), f32)
    for k in range(16):
        start_ref[k] = state.astype(bf16)
        if k < 15:
            gain = pieces_ref[k, HEAD : HEAD + 16, :].astype(f32)[0:1, :]
            state = state * gain + pieces_ref[k, :HEAD, :].astype(f32)


def scan_back_body(pieces_ref, grads_ref, adjoint_ref):
    state = jnp.zeros((HEAD, STATE), f32)
    for k in reversed(range(16)):
        adjoint_ref[k] = state.astype(bf16)
        if k > 0:
            gain = pieces_ref[k, HEAD : HEAD + 16, :].astype(f32)[0:1, :]
            state = state * gain + grads_ref[k].astype(f32)


def mixed_body(
    within_ref, start_ref, c_ref, cum_ref, seg_ref, gate_ref, dg_ref, gain_ref, mixed_ref, sums_ref
):
    entry = entry_decay(cum_ref[...], documents_of(seg_ref)[1])
    c_low = c_ref[...]
    squares = jnp.zeros((ROWS, LANES), f32)
    dots = jnp.zeros((ROWS, LANES), f32)
    for pair in range(PAIRS):
        lanes = slice(pair * LANES, (pair + 1) * LANES)
        carried = nt(c_low, start_ref[lanes, :])
        mixed = within_ref[:, lanes] + spread_pair(entry, pair) * carried
        mixed_ref[:, lanes] = mixed
        gate = gate_ref[:, lanes]
        gated = mixed * (gate * jax.nn.sigmoid(gate))
        squares = squares + gated * gated
        dots = dots + gated * gain_ref[:, lanes] * dg_ref[:, lanes]
    lane = lane_index((ROWS, LANES))
    sums_ref[...] = jnp.where(
        lane == 0,
        jnp.sum(squares, axis=1, keepdims=True),
        jnp.where(lane == 1, jnp.sum(dots, axis=1, keepdims=True), 0.0),
    )


def gate_body(
    sums_ref,
    other_ref,
    mixed_ref,
    gate_ref,
    dg_ref,
    gain_ref,
    c_ref,
    cum_ref,
    seg_ref,
    gnorm_ref,
    d_mixed_ref,
    d_gate_ref,
    grad_gain_ref,
    d_start_ref,
):
    sums = sums_ref[...] + other_ref[...]
    rate = lax.rsqrt(sums[:, 0:1] / INNER + EPSILON)
    back = rate * rate * rate * sums[:, 1:2] / INNER
    rate = jnp.broadcast_to(rate, (ROWS, LANES))
    back = jnp.broadcast_to(back, (ROWS, LANES))
    entry = entry_decay(cum_ref[...], documents_of(seg_ref)[1])
    c_low = c_ref[...]
    for pair in range(PAIRS):
        lanes = slice(pair * LANES, (pair + 1) * LANES)
        mixed = mixed_ref[:, lanes]
        gate = gate_ref[:, lanes]
        gain = gain_ref[:, lanes]
        dg = dg_ref[:, lanes]
        sig = jax.nn.sigmoid(gate)
        silu = gate * sig
        gated = mixed * silu
        scaled = gated * rate
        gnorm_ref[:, lanes] = (scaled * gain).astype(bf16)
        grad_gain_ref[:, lanes] = jnp.sum(dg * scaled, axis=0, keepdims=True)
        d_gated = rate * gain * dg - gated * back
        d_mixed = d_gated * silu
        d_mixed_ref[:, lanes] = d_mixed
        d_gate_ref[:, lanes] = (d_gated * mixed * (sig + silu * (1.0 - sig))).astype(bf16)
        d_state = tn((d_mixed * spread_pair(entry, pair)).astype(bf16), c_low).astype(bf16)
        for side in range(2):
            d_start_ref[2 * pair + side] = d_state[side * HEAD : (side + 1) * HEAD, :]


def head_sums(values, pair):
    shape = (LANES, LANES)
    into = lane_index(shape) == 2 * pair + (row_index(shape) >= HEAD).astype(jnp.int32)
    into = into.astype(bf16)
    high = values.astype(bf16)
    low = (values - high.astype(f32)).astype(bf16)
    return mm(high, into) + mm(low, into)


def conv_back(d_pre, joined_ref, source, lanes, taps, masks, pad_ref, into):
    total = None
    sums = []
    for k in range(4):
        joined = joined_ref[HALO - 3 + k : HALO - 3 + k + ROWS, source]
        part = d_pre * masks[k] if k < 3 else d_pre
        sums.append(jnp.sum(part * joined, axis=0, keepdims=True))
        pad_ref[k, 24 : 24 + ROWS, :] = part * taps[k : k + 1]
        moved = pad_ref[k, 24 - 13 - k : 24 - 13 - k + EXT, :]
        total = moved if total is None else total + moved
    sums.append(jnp.sum(d_pre, axis=0, keepdims=True))
    into[:, lanes] = jnp.concatenate(sums + [jnp.zeros((3, LANES), f32)], axis=0)
    return total


def back_body(
    d_mixed_ref,
    pre_ref,
    joined_ref,
    within_ref,
    start_ref,
    adjoint_ref,
    b_ref,
    c_ref,
    step_ref,
    cum_ref,
    sig_ref,
    decay_ref,
    seg_ref,
    decay_log_ref,
    skip_ref,
    taps_ref,
    d_bc_ref,
    d_ext_ref,
    d_step_ref,
    conv_ref,
    skip_grad_ref,
    small_ref,
    ext_ref,
    pad_ref,
):
    seg_row, documents = documents_of(seg_ref)
    tap_masks = tap_masks_of(documents, ext_ref)
    pad_ref[...] = jnp.zeros_like(pad_ref)
    skips = skip_ref[...]
    cum = cum_ref[...]
    cum_t = cum.T
    step = step_ref[...]
    b_low = b_ref[...]
    c_low = c_ref[...]
    products = nt(c_low, b_low)
    bias = pair_mask(documents, seg_row)
    end = end_decay(cum, documents)
    entry = entry_decay(cum, documents)
    gains = jnp.exp(cum[ROWS - 1 : ROWS, :])
    first_half = lane_index((ROWS, LANES)) < HEAD
    lane = lane_index((1, LANES))
    d_products = jnp.zeros((ROWS, ROWS), f32)
    d_b = jnp.zeros((ROWS, STATE), f32)
    d_c = jnp.zeros((ROWS, STATE), f32)
    d_cum = jnp.zeros((ROWS, LANES), f32)
    d_step = jnp.zeros((ROWS, LANES), f32)
    d_last = jnp.zeros((8, LANES), f32)
    d_whole = jnp.zeros((1, LANES), f32)
    for pair in range(PAIRS):
        lanes = slice(pair * LANES, (pair + 1) * LANES)
        pre = pre_ref[:, lanes]
        sig = jax.nn.sigmoid(pre)
        x = pre * sig
        steps = spread_pair(step, pair)
        ends = spread_pair(end, pair)
        entries = spread_pair(entry, pair)
        skip = spread_pair(skips, pair)
        xs = x * steps
        xs_low = xs.astype(bf16)
        d_mixed = d_mixed_ref[:, lanes]
        dy_low = d_mixed.astype(bf16)
        zero = jnp.zeros_like(dy_low)
        parts = []
        for side in range(2):
            head = 2 * pair + side
            own = jnp.where(first_half if side == 0 else ~first_half, dy_low, zero)
            decays = decay_block(cum, cum_t, head, bias)
            d_products = d_products + decays * nt(own, xs_low)
            parts.append(tn((decays * products).astype(bf16), dy_low))
        d_xs = jnp.where(first_half, parts[0], parts[1])
        within = within_ref[:, lanes] - skip * x
        through = dy_low.astype(f32) * within - xs_low.astype(f32) * d_xs
        start_low = start_ref[lanes, :]
        adjoint_low = adjoint_ref[lanes, :]
        d_ended = nt(b_low, adjoint_low) * ends
        d_b = d_b + mm((xs * ends).astype(bf16), adjoint_low)
        at_end = xs * d_ended
        carried = nt(c_low, start_low) * entries
        d_c = d_c + mm((d_mixed * entries).astype(bf16), start_low)
        d_cum = d_cum + head_sums(through + d_mixed * carried - at_end, pair)
        d_xs = d_xs + d_ended
        d_step = d_step + head_sums(x * d_xs, pair)
        end_sum = jnp.sum(at_end, axis=0, keepdims=True)
        d_last = d_last + head_sums(jnp.broadcast_to(end_sum, (8, LANES)), pair)
        meeting = start_low.astype(f32) * adjoint_low.astype(f32)
        for side in range(2):
            whole = jnp.sum(
                jnp.sum(meeting[side * HEAD : (side + 1) * HEAD, :], axis=0, keepdims=True),
                axis=1,
                keepdims=True,
            )
            d_whole = d_whole + jnp.where(lane == 2 * pair + side, whole, 0.0)
        skip_grad_ref[:, lanes] = jnp.sum(d_mixed * x, axis=0, keepdims=True)
        d_pre = (steps * d_xs + skip * d_mixed) * (sig + x * (1.0 - sig))
        d_ext_ref[:, lanes] = conv_back(
            d_pre, joined_ref, lanes, lanes, taps_ref[:, lanes], tap_masks, pad_ref, conv_ref
        ).astype(bf16)
    d_products = d_products.astype(bf16)
    d_bc_ref[:, :STATE] = (d_b + tn(d_products, c_low)).astype(bf16)
    d_bc_ref[:, STATE:] = (d_c + mm(d_products, b_low)).astype(bf16)
    tri = (row_index((ROWS, ROWS)) <= lane_index((ROWS, ROWS))).astype(f32)
    d_decay = exact(tri, d_cum) + (d_last[0:1, :] + gains * d_whole)
    d_raw = (d_step + d_decay * to_lanes(-jnp.exp(decay_log_ref[...]))) * sig_ref[...]
    d_step_ref[...] = d_raw.astype(bf16)
    small_ref[...] = jnp.concatenate(
        [
            jnp.sum(d_raw, axis=0, keepdims=True),
            jnp.sum(d_decay * decay_ref[...], axis=0, keepdims=True),
            jnp.zeros((6, LANES), f32),
        ],
        axis=0,
    )


def bc_back_body(
    own_ref, other_ref, pre_ref, joined_ref, seg_ref, taps_ref, d_ext_ref, conv_ref, ext_ref, pad_ref
):
    _, documents = documents_of(seg_ref)
    tap_masks = tap_masks_of(documents, ext_ref)
    pad_ref[...] = jnp.zeros_like(pad_ref)
    for half in range(2):
        lanes = slice(half * LANES, (half + 1) * LANES)
        source = slice(LOCAL + half * LANES, LOCAL + (half + 1) * LANES)
        pre = pre_ref[:, source]
        sig = jax.nn.sigmoid(pre)
        d_act = own_ref[:, lanes].astype(f32) + other_ref[:, lanes].astype(f32)
        d_pre = d_act * (sig + pre * sig * (1.0 - sig))
        d_ext_ref[:, lanes] = conv_back(
            d_pre, joined_ref, source, lanes, taps_ref[:, lanes], tap_masks, pad_ref, conv_ref
        ).astype(bf16)


def terms_body(dx_ref, dz_ref, dst_ref, dbc_ref, win_ref, wst_ref, wbc_ref, out_ref):
    first = lax.axis_index("tensor") == 0
    dbc = dbc_ref[...]
    wbc = wbc_ref[...]
    half = jnp.where(first, dbc[:, :STATE], dbc[:, STATE:])
    weights = jnp.where(first, wbc[:, :STATE], wbc[:, STATE:])
    both = nt(dx_ref[...], win_ref[:, :LOCAL]) + nt(half, weights)
    out_ref[:HALO, :] = both[:HALO, :].astype(bf16)
    own = nt(dz_ref[...], win_ref[:, LOCAL:]) + nt(dst_ref[:, :HEADS], wst_ref[...])
    out_ref[HALO:, :] = (both[HALO:, :] + own).astype(bf16)


def hidden_body(
    hidden_ref, terms_ref, other_ref, returned_ref, gain_ref, out_grad_ref, grad_ref, gain_grad_ref
):
    values = hidden_ref[...].astype(f32)
    scale = lax.rsqrt(jnp.sum(values * values, axis=1, keepdims=True) / D + EPSILON)
    d_normed = terms_ref[HALO:, :].astype(f32) + other_ref[HALO:, :].astype(f32)
    tail = jnp.concatenate(
        [jnp.zeros((ROWS - HALO, D), f32), returned_ref[...].astype(f32)], axis=0
    )
    d_normed = d_normed + tail
    first = lax.axis_index("tensor") == 0
    half = D // 2
    grads = jnp.sum(d_normed * values * scale, axis=0, keepdims=True)
    gain_grad_ref[...] = jnp.where(first, grads[:, :half], grads[:, half:])
    scaled = d_normed * gain_ref[...]
    dots = jnp.sum(values * scaled, axis=1, keepdims=True)
    result = scale * scaled - values * (scale * scale * scale * dots / D)
    own = jnp.where(first, result[:, :half], result[:, half:])
    grad_ref[...] = (out_grad_ref[...].astype(f32) + own).astype(bf16)


def bundle_body(
    normed_ref,
    dx_ref,
    dbc_ref,
    dst_ref,
    conv_ref,
    bc_conv_ref,
    gate_gain_ref,
    norm_gain_ref,
    skip_ref,
    small_ref,
    bundle_ref,
):
    half = D // 2
    bundle_ref[:, :LOCAL] = tn(normed_ref[...], dx_ref[...]).astype(bf16)
    first = lax.axis_index("tensor") == 0
    share = jnp.where(first, normed_ref[:, :half], normed_ref[:, half:])
    bundle_ref[:half, LOCAL:] = tn(share, dbc_ref[...]).astype(bf16)
    steps = tn(dst_ref[...], normed_ref[HALO:, :])
    for part in range(4):
        at = half + part * HEADS
        bundle_ref[at : at + HEADS, LOCAL:] = steps[:HEADS, part * 256 : part * 256 + 256].astype(bf16)
    row = half + 4 * HEADS
    pieces = []
    for part in range(4):
        pieces.append(conv_ref[:, part * 256 : part * 256 + 256])
    pieces.append(bc_conv_ref[...])
    lone = [gate_gain_ref[:, part * 256 : part * 256 + 256] for part in range(4)]
    lone += [norm_gain_ref[:, part * 256 : part * 256 + 256] for part in range(2)]
    lone += [jnp.concatenate([small_ref[0:1, :], small_ref[1:2, :]], axis=1)]
    lone += [jnp.zeros((1, 256), f32)]
    pieces.append(jnp.concatenate(lone, axis=0))
    skips = skip_ref[...]
    pieces.append(
        jnp.concatenate(
            [skips[:, part * 256 : part * 256 + 256] for part in range(4)]
            + [jnp.zeros((4, 256), f32)],
            axis=0,
        )
    )
    pieces.append(jnp.zeros((8, 256), f32))
    bundle_ref[row : row + 64, LOCAL:] = jnp.concatenate(pieces, axis=0).astype(bf16)
    bundle_ref[row + 64 :, LOCAL:] = jnp.zeros((half - 4 * HEADS - 64, 256), bf16)


def total_body(received_ref, out_ref):
    total = jnp.zeros(received_ref.shape[1:], f32)
    for k in range(DEVICES):
        total = total + received_ref[k].astype(f32)
    total = total.astype(bf16)
    for k in range(DEVICES):
        out_ref[k] = total


def few_body(
    final_ref,
    bc_ref,
    step_ref,
    conv_ref,
    conv_bias_ref,
    bc_conv_ref,
    bc_conv_bias_ref,
    gate_gain_ref,
    norm_gain_ref,
    skip_ref,
    step_bias_ref,
    decay_log_ref,
):
    half = D // 2
    grads = final_ref[:half, LOCAL:].astype(f32)
    bc_ref[:, 0, :] = grads[:, :STATE]
    bc_ref[:, 1, :] = grads[:, STATE:]
    rest = final_ref[half : half + 128, LOCAL:].astype(f32)
    steps = jnp.concatenate([rest[part * HEADS : (part + 1) * HEADS] for part in range(4)], axis=1)
    steps = jnp.concatenate([steps, jnp.zeros((LANES - HEADS, D), f32)], axis=0)
    step_ref[...] = steps.T[:, :HEADS]
    conv = jnp.concatenate([rest[64 + part * 8 : 72 + part * 8] for part in range(4)], axis=1)
    conv_ref[...] = conv[:4]
    conv_bias_ref[...] = conv[4:5]
    bc = rest[96:104]
    for side in range(2):
        lanes = slice(side * STATE, (side + 1) * STATE)
        bc_conv_ref[:, side, :] = bc[:4, lanes]
        bc_conv_bias_ref[side : side + 1, :] = bc[4:5, lanes]
    lone = rest[104:112]
    gate_gain_ref[...] = jnp.concatenate([lone[part : part + 1] for part in range(4)], axis=1)
    norm_gain_ref[...] = jnp.concatenate([lone[part : part + 1] for part in range(4, 6)], axis=1)
    step_bias_ref[...] = lone[6:7, :HEADS]
    decay_log_ref[...] = lone[6:7, LANES : LANES + HEADS]
    skips = rest[112:116]
    total = jnp.zeros((1, LANES), f32)
    lane = lane_index((1, LANES))
    for head in range(HEADS):
        at = (head % 4) * HEAD
        own = jnp.sum(
            skips[head // 4 : head // 4 + 1, at : at + HEAD], axis=1, keepdims=True
        )
        total = total + jnp.where(lane == head, own, 0.0)
    skip_ref[...] = total[:, :HEADS]


def large_body(final_ref, gate_ref, grad_in_ref):
    grad_in_ref[:, 0, :] = final_ref[:, :LOCAL].astype(f32)
    grad_in_ref[:, 1, :] = gate_ref[...]


def swapped(values):
    return lax.ppermute(values, "tensor", [(0, 1), (1, 0)])


def shards(
    hidden_in,
    segment_ids,
    norm_gain,
    in_weight,
    bc_weight,
    step_weight,
    conv_weight,
    conv_bias,
    bc_conv_weight,
    bc_conv_bias,
    step_bias,
    decay_log,
    skip_gain,
    gate_gain,
    out_weight,
    out_grad,
):
    side = lax.axis_index("tensor")
    width = hidden_in.shape[1]
    gathered = lax.all_gather(hidden_in, "tensor", axis=1, tiled=True)
    halo = lax.ppermute(gathered[ROWS - HALO :], CONTEXT, [(i, i + 1) for i in range(15)])
    cotangent = lax.all_gather(out_grad, "tensor", axis=1, tiled=True)
    win = in_weight.reshape(D, 2 * LOCAL)
    wbc = bc_weight.reshape(D, 2 * STATE)
    bc_taps = bc_conv_weight.reshape(4, 2 * STATE)
    segs = segment_ids[None]
    skip = skip_gain[None]
    gain_row = gate_gain[None]
    dg = nt(cotangent, out_weight)
    ext_scratch = pltpu.VMEM((ROWS + 8, LANES), f32)
    pad_scratch = pltpu.VMEM((4, ROWS + 48, LANES), f32)
    (
        normed_ext,
        joined,
        pre,
        gate,
        b_low,
        c_low,
        step,
        cum,
        sig,
        decay,
        state,
    ) = kernel_call(
        front_body,
        [
            ((EXT, D), bf16),
            ((EXT, LOCAL + 2 * STATE), f32),
            ((ROWS, LOCAL + 2 * STATE), f32),
            ((ROWS, LOCAL), f32),
            ((ROWS, STATE), bf16),
            ((ROWS, STATE), bf16),
            ((ROWS, LANES), f32),
            ((ROWS, LANES), f32),
            ((ROWS, LANES), f32),
            ((ROWS, LANES), f32),
            ((HEADS, CHUNK, STATE), bf16),
        ],
        (
            gathered,
            halo,
            norm_gain[None],
            win,
            wbc,
            step_weight,
            conv_weight,
            conv_bias[None],
            bc_taps,
            bc_conv_bias.reshape(1, 2 * STATE),
            segs,
            step_bias[None],
            decay_log[None],
        ),
        scratch=[ext_scratch, pltpu.VMEM((D, LANES), bf16)],
    )
    pieces = lax.all_to_all(state, CONTEXT, 0, 0, tiled=True)
    (within,) = kernel_call(
        within_body,
        [((ROWS, LOCAL), f32)],
        (pre, step, cum, b_low, c_low, segs, skip),
    )
    (starts,) = kernel_call(scan_body, [((16, HEAD, STATE), bf16)], (pieces,))
    start = lax.all_to_all(starts, CONTEXT, 0, 0, tiled=True).reshape(LOCAL, STATE)
    mixed, sums = kernel_call(
        mixed_body,
        [((ROWS, LOCAL), f32), ((ROWS, LANES), f32)],
        (within, start, c_low, cum, segs, gate, dg, gain_row),
    )
    gnorm, d_mixed, d_gate, grad_gate_gain, d_start = kernel_call(
        gate_body,
        [
            ((ROWS, LOCAL), bf16),
            ((ROWS, LOCAL), f32),
            ((ROWS, LOCAL), bf16),
            ((1, LOCAL), f32),
            ((HEADS, HEAD, STATE), bf16),
        ],
        (sums, swapped(sums), mixed, gate, dg, gain_row, c_low, cum, segs),
    )
    normed = normed_ext[HALO:]
    grad_out, grad_gate, d_start = lax.optimization_barrier(
        (tn(gnorm, cotangent), tn(normed, d_gate), d_start)
    )
    grad_out, grad_gate = lax.psum((grad_out, grad_gate), EVERYONE)
    received = lax.all_to_all(d_start, CONTEXT, 0, 0, tiled=True)
    (adjoints,) = kernel_call(
        scan_back_body, [((16, HEAD, STATE), bf16)], (pieces, received)
    )
    adjoint = lax.all_to_all(adjoints, CONTEXT, 0, 0, tiled=True).reshape(LOCAL, STATE)
    out_terms = mm(gnorm, out_weight).astype(bf16)
    kept = lax.dynamic_slice_in_dim(out_terms, side * width, width, 1)
    given = lax.dynamic_slice_in_dim(out_terms, (1 - side) * width, width, 1)
    hidden_out = (
        hidden_in.astype(f32) + kept.astype(f32) + swapped(given).astype(f32)
    ).astype(bf16)
    d_bc, d_ext, d_step, conv_grads, skip_grads, small = kernel_call(
        back_body,
        [
            ((ROWS, 2 * STATE), bf16),
            ((EXT, LOCAL), bf16),
            ((ROWS, LANES), bf16),
            ((8, LOCAL), f32),
            ((1, LOCAL), f32),
            ((8, LANES), f32),
        ],
        (
            d_mixed,
            pre,
            joined,
            within,
            start,
            adjoint,
            b_low,
            c_low,
            step,
            cum,
            sig,
            decay,
            segs,
            decay_log[None],
            skip,
            conv_weight,
        ),
        scratch=[ext_scratch, pad_scratch],
    )
    d_bc_ext, bc_conv_grads = kernel_call(
        bc_back_body,
        [((EXT, 2 * STATE), bf16), ((8, 2 * STATE), f32)],
        (d_bc, swapped(d_bc), pre, joined, segs, bc_taps),
        scratch=[ext_scratch, pad_scratch],
    )
    (terms,) = kernel_call(
        terms_body,
        [((EXT, D), bf16)],
        (d_ext, d_gate, d_step, d_bc_ext, win, step_weight, wbc),
    )
    other_terms = swapped(terms)
    halo_terms = (terms[:HALO].astype(f32) + other_terms[:HALO].astype(f32)).astype(bf16)
    returned = lax.ppermute(halo_terms, CONTEXT, [(i + 1, i) for i in range(15)])
    hidden_grad, grad_norm = kernel_call(
        hidden_body,
        [((ROWS, width), bf16), ((1, width), f32)],
        (gathered, terms, other_terms, returned, norm_gain[None], out_grad),
    )
    (bundle,) = kernel_call(
        bundle_body,
        [((D, LOCAL + 256), bf16)],
        (
            normed_ext,
            d_ext,
            d_bc_ext,
            d_step,
            conv_grads,
            bc_conv_grads,
            grad_gate_gain,
            grad_norm,
            skip_grads,
            small,
        ),
    )
    scattered = lax.all_to_all(
        bundle.reshape(DEVICES, 16, LOCAL + 256), EVERYONE, 0, 0, tiled=True
    )
    (spread,) = kernel_call(total_body, [(scattered.shape, bf16)], (scattered,))
    final = lax.all_to_all(spread, EVERYONE, 0, 0, tiled=True).reshape(D, LOCAL + 256)
    half = D // 2
    (
        grad_bc,
        grad_step,
        grad_conv,
        grad_conv_bias,
        grad_bc_conv,
        grad_bc_conv_bias,
        total_gate_gain,
        total_norm_gain,
        grad_skip,
        grad_step_bias,
        grad_decay_log,
    ) = kernel_call(
        few_body,
        [
            ((half, 2, STATE), f32),
            ((D, HEADS), f32),
            ((4, LOCAL), f32),
            ((1, LOCAL), f32),
            ((4, 2, STATE), f32),
            ((2, STATE), f32),
            ((1, LOCAL), f32),
            ((1, half), f32),
            ((1, HEADS), f32),
            ((1, HEADS), f32),
            ((1, HEADS), f32),
        ],
        (final,),
    )
    (grad_in,) = kernel_call(large_body, [((D, 2, LOCAL), f32)], (final, grad_gate))
    return (
        hidden_out,
        hidden_grad,
        total_norm_gain[0],
        grad_in,
        grad_bc,
        grad_step,
        grad_conv,
        grad_conv_bias[0],
        grad_bc_conv,
        grad_bc_conv_bias,
        grad_step_bias[0],
        grad_decay_log[0],
        grad_skip[0],
        total_gate_gain[0],
        grad_out,
    )


def solution(mesh):
    torus = Mesh(
        mesh.devices.reshape(mesh.shape["tensor"], mesh.shape["dp"], 4, 4),
        ("tensor", "dp", "context_0", "context_1"),
    )
    rows = ("dp", "context_0", "context_1")
    in_specs = (
        P(rows, "tensor"),
        P(rows),
        P(),
        P(None, None, "tensor"),
        P(),
        P(None, "tensor"),
        P(None, "tensor"),
        P("tensor"),
        P(),
        P(),
        P(),
        P("tensor"),
        P("tensor"),
        P("tensor"),
        P("tensor", None),
        P(rows, "tensor"),
    )
    out_specs = (
        P(rows, "tensor"),
        P(rows, "tensor"),
        P("tensor"),
        P(None, None, "tensor"),
        P("tensor", None, None),
        P(None, "tensor"),
        P(None, "tensor"),
        P("tensor"),
        P(),
        P(),
        P("tensor"),
        P("tensor"),
        P("tensor"),
        P("tensor"),
        P("tensor", None),
    )
    return jax.shard_map(
        shards, mesh=torus, in_specs=in_specs, out_specs=out_specs, check_vma=False
    )
```

```python
import jax
import jax.numpy as jnp
from jax import lax
from jax.experimental import pallas as pl
from jax.experimental.pallas import tpu as pltpu
from jax.sharding import Mesh
from jax.sharding import PartitionSpec as P

D = 1024
HEAD = 64
STATE = 128
INNER = 2048
ROWS = 256
HEADS = 16
LOCAL = 1024
HALO = 16
EXT = ROWS + HALO
LANES = 128
PAIRS = LOCAL // LANES
CHUNK = 80
DEVICES = 64
CONTEXT = ("context_0", "context_1")
EVERYONE = ("dp", "context_0", "context_1")
EPSILON = 1e-05
BC_COST = 10_000_000
TERMS_COST = 15_000_000
HIDDEN_COST = 9_000_000
BUNDLE_COST = 8_000_000
f32 = jnp.float32
bf16 = jnp.bfloat16
HIGHEST = lax.Precision.HIGHEST


def mm(a, b):
    return lax.dot_general(a, b, (((1,), (0,)), ((), ())), preferred_element_type=f32)


def nt(a, b):
    return lax.dot_general(a, b, (((1,), (1,)), ((), ())), preferred_element_type=f32)


def tn(a, b):
    return lax.dot_general(a, b, (((0,), (0,)), ((), ())), preferred_element_type=f32)


def exact(a, b):
    return lax.dot_general(
        a, b, (((1,), (0,)), ((), ())), precision=HIGHEST, preferred_element_type=f32
    )


def whole(shape, index=None):
    index = index or (0,) * len(shape)
    return pl.BlockSpec(shape, lambda i: index, pipeline_mode=pl.Buffered(1))


def kernel_call(body, outs, args, scratch=(), cost=0, vmem=56, blocks={}):
    return pl.pallas_call(
        body,
        grid=(1,),
        out_shape=[jax.ShapeDtypeStruct(shape, kind) for shape, kind in outs],
        in_specs=[whole(*blocks.get(i, (a.shape,))) for i, a in enumerate(args)],
        out_specs=[whole(shape) for shape, _ in outs],
        scratch_shapes=list(scratch),
        compiler_params=pltpu.CompilerParams(vmem_limit_bytes=vmem * 1024 * 1024),
        cost_estimate=pl.CostEstimate(flops=0, bytes_accessed=cost, transcendentals=0),
    )(*args)


def lane_index(shape):
    return lax.broadcasted_iota(jnp.int32, shape, 1)


def row_index(shape):
    return lax.broadcasted_iota(jnp.int32, shape, 0)


def spread_pair(columns, pair):
    rows = columns.shape[0]
    first = jnp.broadcast_to(columns[:, 2 * pair : 2 * pair + 1], (rows, LANES))
    second = jnp.broadcast_to(columns[:, 2 * pair + 1 : 2 * pair + 2], (rows, LANES))
    return jnp.where(lane_index((rows, LANES)) < HEAD, first, second)


def pair_mask(documents, seg_row):
    shape = (ROWS, ROWS)
    causal = row_index(shape) >= lane_index(shape)
    columns = jnp.concatenate([documents, documents], axis=1)
    return jnp.where((columns == seg_row) & causal, 0.0, -1e30).astype(f32)


def decay_block(cum, cum_t, head, bias):
    return jnp.exp(cum[:, head : head + 1] - cum_t[head : head + 1, :] + bias)


def document_before():
    piece = lax.axis_index("context_0") * 4 + lax.axis_index("context_1")
    return jnp.where(piece > 0, 2.0, 0.0).astype(f32)


def documents_of(seg_ref):
    seg_row = seg_ref[...].astype(f32) + 1.0
    return seg_row, jnp.broadcast_to(seg_row, (LANES, ROWS)).T


def tap_masks_of(documents, ext_ref):
    ext_ref[:8, :] = jnp.full((8, LANES), document_before(), f32)
    ext_ref[8:, :] = documents
    return [(ext_ref[5 + k : 5 + k + ROWS, :] == documents).astype(f32) for k in range(3)]


def end_decay(cum, documents):
    last = (documents == documents[ROWS - 1 : ROWS, :]).astype(f32)
    return jnp.exp(cum[ROWS - 1 : ROWS, :] - cum) * last


def entry_decay(cum, documents):
    return jnp.exp(cum) * (documents == document_before()).astype(f32)


def to_lanes(values):
    rows, count = values.shape
    return jnp.concatenate([values, jnp.zeros((rows, LANES - count), f32)], axis=1)


def front_body(
    hidden_ref,
    halo_ref,
    gain_ref,
    win_ref,
    wbc_ref,
    wst_ref,
    taps_ref,
    bias_ref,
    bc_taps_ref,
    bc_bias_ref,
    seg_ref,
    step_bias_ref,
    decay_log_ref,
    normed_ref,
    joined_ref,
    pre_ref,
    b_ref,
    c_ref,
    step_ref,
    cum_ref,
    sig_ref,
    decay_ref,
    state_ref,
    ext_ref,
    wide_ref,
):
    gain = gain_ref[...]
    for source, start, rows in ((halo_ref, 0, HALO), (hidden_ref, HALO, ROWS)):
        values = source[...].astype(f32)
        scale = lax.rsqrt(jnp.sum(values * values, axis=1, keepdims=True) / D + EPSILON)
        normed_ref[start : start + rows, :] = (values * scale * gain).astype(bf16)
    normed_ext = normed_ref[...]
    normed = normed_ref[HALO:, :]
    joined_ref[:, :LOCAL] = mm(normed_ext, win_ref[...])
    joined_ref[:, LOCAL:] = mm(normed_ext, wbc_ref[...])
    wide_ref[...] = jnp.zeros_like(wide_ref)
    wide_ref[:HEADS, :] = wst_ref[...]
    both = step_bias_ref[...]
    first = lax.axis_index("tensor") == 0
    local_bias = jnp.where(first, both[:, :HEADS], both[:, HEADS:])
    raw = nt(normed, wide_ref[...]) + to_lanes(local_bias)
    step = jnp.maximum(raw, 0.0) + jnp.log1p(jnp.exp(-jnp.abs(raw)))
    decay = step * to_lanes(-jnp.exp(decay_log_ref[...]))
    tri = (row_index((ROWS, ROWS)) >= lane_index((ROWS, ROWS))).astype(f32)
    cum = exact(tri, decay)
    step_ref[...] = step
    cum_ref[...] = cum
    sig_ref[...] = jax.nn.sigmoid(raw)
    decay_ref[...] = decay
    _, documents = documents_of(seg_ref)
    tap_masks = tap_masks_of(documents, ext_ref)

    def conv(at, taps, bias):
        lanes = slice(at, at + LANES)
        total = jnp.broadcast_to(bias, (ROWS, LANES))
        for k in range(4):
            part = joined_ref[HALO - 3 + k : HALO - 3 + k + ROWS, lanes] * taps[k : k + 1]
            total = total + (part * tap_masks[k] if k < 3 else part)
        pre_ref[:, lanes] = total
        return total * jax.nn.sigmoid(total)

    b_low = conv(LOCAL, bc_taps_ref[:, :STATE], bc_bias_ref[:, :STATE]).astype(bf16)
    c_low = conv(LOCAL + STATE, bc_taps_ref[:, STATE:], bc_bias_ref[:, STATE:]).astype(bf16)
    b_ref[...] = b_low
    c_ref[...] = c_low
    gains = jnp.exp(cum[ROWS - 1 : ROWS, :])
    ended = step * end_decay(cum, documents)
    for pair in range(PAIRS):
        lanes = slice(pair * LANES, (pair + 1) * LANES)
        x = conv(pair * LANES, taps_ref[:, lanes], bias_ref[:, lanes])
        state = tn((x * spread_pair(ended, pair)).astype(bf16), b_low).astype(bf16)
        for side in range(2):
            head = 2 * pair + side
            state_ref[head, :HEAD, :] = state[side * HEAD : (side + 1) * HEAD, :]
            state_ref[head, HEAD:, :] = jnp.broadcast_to(
                gains[:, head : head + 1], (CHUNK - HEAD, STATE)
            ).astype(bf16)


def gate_proj_body(normed_ref, win_ref, gate_ref):
    gate_ref[...] = mm(normed_ref[HALO:, :], win_ref[...])


def within_body(pre_ref, step_ref, cum_ref, b_ref, c_ref, seg_ref, skip_ref, within_ref):
    seg_row, documents = documents_of(seg_ref)
    products = nt(c_ref[...], b_ref[...])
    bias = pair_mask(documents, seg_row)
    step = step_ref[...]
    cum = cum_ref[...]
    cum_t = cum.T
    skip = skip_ref[...]
    first_half = lane_index((ROWS, LANES)) < HEAD
    for pair in range(PAIRS):
        lanes = slice(pair * LANES, (pair + 1) * LANES)
        pre = pre_ref[:, lanes]
        x = pre * jax.nn.sigmoid(pre)
        xs_low = (x * spread_pair(step, pair)).astype(bf16)
        sums = []
        for head in (2 * pair, 2 * pair + 1):
            block = (decay_block(cum, cum_t, head, bias) * products).astype(bf16)
            sums.append(mm(block, xs_low))
        within_ref[:, lanes] = (
            jnp.where(first_half, sums[0], sums[1]) + spread_pair(skip, pair) * x
        )


def scan_body(pieces_ref, start_ref):
    state = jnp.zeros((HEAD, STATE), f32)
    for k in range(16):
        start_ref[k] = state.astype(bf16)
        if k < 15:
            gain = pieces_ref[k, HEAD : HEAD + 16, :].astype(f32)[0:1, :]
            state = state * gain + pieces_ref[k, :HEAD, :].astype(f32)


def scan_back_body(pieces_ref, grads_ref, adjoint_ref):
    state = jnp.zeros((HEAD, STATE), f32)
    for k in reversed(range(16)):
        adjoint_ref[k] = state.astype(bf16)
        if k > 0:
            gain = pieces_ref[k, HEAD : HEAD + 16, :].astype(f32)[0:1, :]
            state = state * gain + grads_ref[k].astype(f32)


def mixed_body(
    within_ref, start_ref, c_ref, cum_ref, seg_ref, gate_ref, dg_ref, gain_ref, mixed_ref, sums_ref
):
    entry = entry_decay(cum_ref[...], documents_of(seg_ref)[1])
    c_low = c_ref[...]
    squares = jnp.zeros((ROWS, LANES), f32)
    dots = jnp.zeros((ROWS, LANES), f32)
    for pair in range(PAIRS):
        lanes = slice(pair * LANES, (pair + 1) * LANES)
        carried = nt(c_low, start_ref[lanes, :])
        mixed = within_ref[:, lanes] + spread_pair(entry, pair) * carried
        mixed_ref[:, lanes] = mixed
        gate = gate_ref[:, lanes]
        gated = mixed * (gate * jax.nn.sigmoid(gate))
        squares = squares + gated * gated
        dots = dots + gated * gain_ref[:, lanes] * dg_ref[:, lanes]
    lane = lane_index((ROWS, LANES))
    sums_ref[...] = jnp.where(
        lane == 0,
        jnp.sum(squares, axis=1, keepdims=True),
        jnp.where(lane == 1, jnp.sum(dots, axis=1, keepdims=True), 0.0),
    )


def gate_body(
    sums_ref,
    other_ref,
    mixed_ref,
    gate_ref,
    dg_ref,
    gain_ref,
    c_ref,
    cum_ref,
    seg_ref,
    gnorm_ref,
    d_mixed_ref,
    d_gate_ref,
    grad_gain_ref,
    d_start_ref,
):
    sums = sums_ref[...] + other_ref[...]
    rate = lax.rsqrt(sums[:, 0:1] / INNER + EPSILON)
    back = rate * rate * rate * sums[:, 1:2] / INNER
    rate = jnp.broadcast_to(rate, (ROWS, LANES))
    back = jnp.broadcast_to(back, (ROWS, LANES))
    entry = entry_decay(cum_ref[...], documents_of(seg_ref)[1])
    c_low = c_ref[...]
    for pair in range(PAIRS):
        lanes = slice(pair * LANES, (pair + 1) * LANES)
        mixed = mixed_ref[:, lanes]
        gate = gate_ref[:, lanes]
        gain = gain_ref[:, lanes]
        dg = dg_ref[:, lanes]
        sig = jax.nn.sigmoid(gate)
        silu = gate * sig
        gated = mixed * silu
        scaled = gated * rate
        gnorm_ref[:, lanes] = (scaled * gain).astype(bf16)
        grad_gain_ref[:, lanes] = jnp.sum(dg * scaled, axis=0, keepdims=True)
        d_gated = rate * gain * dg - gated * back
        d_mixed = d_gated * silu
        d_mixed_ref[:, lanes] = d_mixed
        d_gate_ref[:, lanes] = (d_gated * mixed * (sig + silu * (1.0 - sig))).astype(bf16)
        d_state = tn((d_mixed * spread_pair(entry, pair)).astype(bf16), c_low).astype(bf16)
        for side in range(2):
            d_start_ref[2 * pair + side] = d_state[side * HEAD : (side + 1) * HEAD, :]


def head_sums(values, pair):
    shape = (LANES, LANES)
    into = lane_index(shape) == 2 * pair + (row_index(shape) >= HEAD).astype(jnp.int32)
    into = into.astype(bf16)
    high = values.astype(bf16)
    low = (values - high.astype(f32)).astype(bf16)
    return mm(high, into) + mm(low, into)


def conv_back(d_pre, joined_ref, source, lanes, taps, masks, pad_ref, into):
    total = None
    sums = []
    for k in range(4):
        joined = joined_ref[HALO - 3 + k : HALO - 3 + k + ROWS, source]
        part = d_pre * masks[k] if k < 3 else d_pre
        sums.append(jnp.sum(part * joined, axis=0, keepdims=True))
        pad_ref[k, 24 : 24 + ROWS, :] = part * taps[k : k + 1]
        moved = pad_ref[k, 24 - 13 - k : 24 - 13 - k + EXT, :]
        total = moved if total is None else total + moved
    sums.append(jnp.sum(d_pre, axis=0, keepdims=True))
    into[:, lanes] = jnp.concatenate(sums + [jnp.zeros((3, LANES), f32)], axis=0)
    return total


def back_body(
    d_mixed_ref,
    pre_ref,
    within_ref,
    start_ref,
    b_ref,
    c_ref,
    step_ref,
    cum_ref,
    seg_ref,
    skip_ref,
    d_xs_ref,
    d_bc_ref,
    d_cum_ref,
    skip_grad_ref,
):
    seg_row, documents = documents_of(seg_ref)
    skips = skip_ref[...]
    cum = cum_ref[...]
    cum_t = cum.T
    step = step_ref[...]
    b_low = b_ref[...]
    c_low = c_ref[...]
    products = nt(c_low, b_low)
    bias = pair_mask(documents, seg_row)
    entry = entry_decay(cum, documents)
    first_half = lane_index((ROWS, LANES)) < HEAD
    d_products = jnp.zeros((ROWS, ROWS), f32)
    d_c = jnp.zeros((ROWS, STATE), f32)
    d_cum = jnp.zeros((ROWS, LANES), f32)
    for pair in range(PAIRS):
        lanes = slice(pair * LANES, (pair + 1) * LANES)
        pre = pre_ref[:, lanes]
        x = pre * jax.nn.sigmoid(pre)
        xs_low = (x * spread_pair(step, pair)).astype(bf16)
        d_mixed = d_mixed_ref[:, lanes]
        dy_low = d_mixed.astype(bf16)
        zero = jnp.zeros_like(dy_low)
        parts = []
        for side in range(2):
            head = 2 * pair + side
            own = jnp.where(first_half if side == 0 else ~first_half, dy_low, zero)
            decays = decay_block(cum, cum_t, head, bias)
            d_products = d_products + decays * nt(own, xs_low)
            parts.append(tn((decays * products).astype(bf16), dy_low))
        d_xs = jnp.where(first_half, parts[0], parts[1])
        d_xs_ref[:, lanes] = d_xs
        within = within_ref[:, lanes] - spread_pair(skips, pair) * x
        through = dy_low.astype(f32) * within - xs_low.astype(f32) * d_xs
        start_low = start_ref[lanes, :]
        carried = d_mixed * spread_pair(entry, pair)
        d_c = d_c + mm(carried.astype(bf16), start_low)
        d_cum = d_cum + head_sums(through + carried * nt(c_low, start_low), pair)
        skip_grad_ref[:, lanes] = jnp.sum(d_mixed * x, axis=0, keepdims=True)
    d_products = d_products.astype(bf16)
    d_bc_ref[:, :STATE] = tn(d_products, c_low)
    d_bc_ref[:, STATE:] = d_c + mm(d_products, b_low)
    d_cum_ref[...] = d_cum


def carry_back_body(
    d_mixed_ref,
    pre_ref,
    joined_ref,
    d_xs_ref,
    d_bc_in_ref,
    d_cum_ref,
    start_ref,
    adjoint_ref,
    b_ref,
    step_ref,
    cum_ref,
    sig_ref,
    decay_ref,
    seg_ref,
    decay_log_ref,
    skip_ref,
    taps_ref,
    d_bc_ref,
    d_ext_ref,
    d_step_ref,
    conv_ref,
    small_ref,
    ext_ref,
    pad_ref,
):
    _, documents = documents_of(seg_ref)
    tap_masks = tap_masks_of(documents, ext_ref)
    pad_ref[...] = jnp.zeros_like(pad_ref)
    skips = skip_ref[...]
    cum = cum_ref[...]
    step = step_ref[...]
    b_low = b_ref[...]
    end = end_decay(cum, documents)
    gains = jnp.exp(cum[ROWS - 1 : ROWS, :])
    lane = lane_index((1, LANES))
    d_b = d_bc_in_ref[:, :STATE]
    d_cum = d_cum_ref[...]
    d_step = jnp.zeros((ROWS, LANES), f32)
    d_last = jnp.zeros((8, LANES), f32)
    d_whole = jnp.zeros((1, LANES), f32)
    for pair in range(PAIRS):
        lanes = slice(pair * LANES, (pair + 1) * LANES)
        pre = pre_ref[:, lanes]
        sig = jax.nn.sigmoid(pre)
        x = pre * sig
        steps = spread_pair(step, pair)
        ends = spread_pair(end, pair)
        xs = x * steps
        adjoint_low = adjoint_ref[lanes, :]
        d_ended = nt(b_low, adjoint_low) * ends
        d_b = d_b + mm((xs * ends).astype(bf16), adjoint_low)
        at_end = xs * d_ended
        d_cum = d_cum - head_sums(at_end, pair)
        d_xs = d_xs_ref[:, lanes] + d_ended
        d_step = d_step + head_sums(x * d_xs, pair)
        end_sum = jnp.sum(at_end, axis=0, keepdims=True)
        d_last = d_last + head_sums(jnp.broadcast_to(end_sum, (8, LANES)), pair)
        meeting = start_ref[lanes, :].astype(f32) * adjoint_low.astype(f32)
        for side in range(2):
            whole_sum = jnp.sum(
                jnp.sum(meeting[side * HEAD : (side + 1) * HEAD, :], axis=0, keepdims=True),
                axis=1,
                keepdims=True,
            )
            d_whole = d_whole + jnp.where(lane == 2 * pair + side, whole_sum, 0.0)
        d_act = steps * d_xs + spread_pair(skips, pair) * d_mixed_ref[:, lanes]
        d_pre = d_act * (sig + x * (1.0 - sig))
        d_ext_ref[:, lanes] = conv_back(
            d_pre, joined_ref, lanes, lanes, taps_ref[:, lanes], tap_masks, pad_ref, conv_ref
        ).astype(bf16)
    d_bc_ref[:, :STATE] = d_b.astype(bf16)
    d_bc_ref[:, STATE:] = d_bc_in_ref[:, STATE:].astype(bf16)
    tri = (row_index((ROWS, ROWS)) <= lane_index((ROWS, ROWS))).astype(f32)
    d_decay = exact(tri, d_cum) + (d_last[0:1, :] + gains * d_whole)
    d_raw = (d_step + d_decay * to_lanes(-jnp.exp(decay_log_ref[...]))) * sig_ref[...]
    d_step_ref[...] = d_raw.astype(bf16)
    small_ref[...] = jnp.concatenate(
        [
            jnp.sum(d_raw, axis=0, keepdims=True),
            jnp.sum(d_decay * decay_ref[...], axis=0, keepdims=True),
            jnp.zeros((6, LANES), f32),
        ],
        axis=0,
    )


def bc_back_body(
    own_ref, other_ref, pre_ref, joined_ref, seg_ref, taps_ref, d_ext_ref, conv_ref, ext_ref, pad_ref
):
    _, documents = documents_of(seg_ref)
    tap_masks = tap_masks_of(documents, ext_ref)
    pad_ref[...] = jnp.zeros_like(pad_ref)
    for half in range(2):
        lanes = slice(half * LANES, (half + 1) * LANES)
        source = slice(LOCAL + half * LANES, LOCAL + (half + 1) * LANES)
        pre = pre_ref[:, source]
        sig = jax.nn.sigmoid(pre)
        d_act = own_ref[:, lanes].astype(f32) + other_ref[:, lanes].astype(f32)
        d_pre = d_act * (sig + pre * sig * (1.0 - sig))
        d_ext_ref[:, lanes] = conv_back(
            d_pre, joined_ref, source, lanes, taps_ref[:, lanes], tap_masks, pad_ref, conv_ref
        ).astype(bf16)


def terms_body(dx_ref, dz_ref, dst_ref, dbc_ref, win_ref, wst_ref, wbc_ref, out_ref):
    first = lax.axis_index("tensor") == 0
    dbc = dbc_ref[...]
    wbc = wbc_ref[...]
    half = jnp.where(first, dbc[:, :STATE], dbc[:, STATE:])
    weights = jnp.where(first, wbc[:, :STATE], wbc[:, STATE:])
    both = nt(dx_ref[...], win_ref[:, :LOCAL]) + nt(half, weights)
    out_ref[:HALO, :] = both[:HALO, :].astype(bf16)
    own = nt(dz_ref[...], win_ref[:, LOCAL:]) + mm(dst_ref[:, :HEADS], wst_ref[...])
    out_ref[HALO:, :] = (both[HALO:, :] + own).astype(bf16)


def hidden_body(
    hidden_ref, terms_ref, other_ref, returned_ref, gain_ref, out_grad_ref, grad_ref, gain_grad_ref
):
    values = hidden_ref[...].astype(f32)
    scale = lax.rsqrt(jnp.sum(values * values, axis=1, keepdims=True) / D + EPSILON)
    d_normed = terms_ref[HALO:, :].astype(f32) + other_ref[HALO:, :].astype(f32)
    tail = jnp.concatenate(
        [jnp.zeros((ROWS - HALO, D), f32), returned_ref[...].astype(f32)], axis=0
    )
    d_normed = d_normed + tail
    first = lax.axis_index("tensor") == 0
    half = D // 2
    grads = jnp.sum(d_normed * values * scale, axis=0, keepdims=True)
    gain_grad_ref[...] = jnp.where(first, grads[:, :half], grads[:, half:])
    scaled = d_normed * gain_ref[...]
    dots = jnp.sum(values * scaled, axis=1, keepdims=True)
    result = scale * scaled - values * (scale * scale * scale * dots / D)
    own = jnp.where(first, result[:, :half], result[:, half:])
    grad_ref[...] = (out_grad_ref[...].astype(f32) + own).astype(bf16)


def x_grad_body(normed_ref, dx_ref, grad_ref):
    grad_ref[...] = tn(normed_ref[...], dx_ref[...]).astype(bf16)


def bundle_body(
    normed_ref,
    dbc_ref,
    dst_ref,
    conv_ref,
    bc_conv_ref,
    gate_gain_ref,
    norm_gain_ref,
    skip_ref,
    small_ref,
    bundle_ref,
):
    half = D // 2
    first = lax.axis_index("tensor") == 0
    share = jnp.where(first, normed_ref[:, :half], normed_ref[:, half:])
    bundle_ref[:half, :] = tn(share, dbc_ref[...]).astype(bf16)
    steps = tn(dst_ref[...], normed_ref[HALO:, :])
    for part in range(4):
        at = half + part * HEADS
        bundle_ref[at : at + HEADS, :] = steps[:HEADS, part * 256 : part * 256 + 256].astype(bf16)
    row = half + 4 * HEADS
    pieces = []
    for part in range(4):
        pieces.append(conv_ref[:, part * 256 : part * 256 + 256])
    pieces.append(bc_conv_ref[...])
    lone = [gate_gain_ref[:, part * 256 : part * 256 + 256] for part in range(4)]
    lone += [norm_gain_ref[:, part * 256 : part * 256 + 256] for part in range(2)]
    lone += [jnp.concatenate([small_ref[0:1, :], small_ref[1:2, :]], axis=1)]
    lone += [jnp.zeros((1, 256), f32)]
    pieces.append(jnp.concatenate(lone, axis=0))
    skips = skip_ref[...]
    pieces.append(
        jnp.concatenate(
            [skips[:, part * 256 : part * 256 + 256] for part in range(4)]
            + [jnp.zeros((4, 256), f32)],
            axis=0,
        )
    )
    pieces.append(jnp.zeros((8, 256), f32))
    bundle_ref[row : row + 64, :] = jnp.concatenate(pieces, axis=0).astype(bf16)
    bundle_ref[row + 64 :, :] = jnp.zeros((half - 4 * HEADS - 64, 256), bf16)


def total_body(x_ref, few_ref, out_ref):
    for received_ref, lanes in ((x_ref, slice(0, LOCAL)), (few_ref, slice(LOCAL, LOCAL + 256))):
        total = jnp.zeros(received_ref.shape[1:], f32)
        for k in range(DEVICES):
            total = total + received_ref[k].astype(f32)
        total = total.astype(bf16)
        for k in range(DEVICES):
            out_ref[k, :, lanes] = total


def few_body(
    final_ref,
    bc_ref,
    step_ref,
    conv_ref,
    conv_bias_ref,
    bc_conv_ref,
    bc_conv_bias_ref,
    gate_gain_ref,
    norm_gain_ref,
    skip_ref,
    step_bias_ref,
    decay_log_ref,
):
    half = D // 2
    grads = final_ref[:half, LOCAL:].astype(f32)
    bc_ref[:, 0, :] = grads[:, :STATE]
    bc_ref[:, 1, :] = grads[:, STATE:]
    rest = final_ref[half : half + 128, LOCAL:].astype(f32)
    for part in range(4):
        step_ref[:, part * 256 : part * 256 + 256] = rest[part * HEADS : (part + 1) * HEADS]
    conv = jnp.concatenate([rest[64 + part * 8 : 72 + part * 8] for part in range(4)], axis=1)
    conv_ref[...] = conv[:4]
    conv_bias_ref[...] = conv[4:5]
    bc = rest[96:104]
    for side in range(2):
        lanes = slice(side * STATE, (side + 1) * STATE)
        bc_conv_ref[:, side, :] = bc[:4, lanes]
        bc_conv_bias_ref[side : side + 1, :] = bc[4:5, lanes]
    lone = rest[104:112]
    gate_gain_ref[...] = jnp.concatenate([lone[part : part + 1] for part in range(4)], axis=1)
    norm_gain_ref[...] = jnp.concatenate([lone[part : part + 1] for part in range(4, 6)], axis=1)
    step_bias_ref[...] = lone[6:7, :HEADS]
    decay_log_ref[...] = lone[6:7, LANES : LANES + HEADS]
    skips = rest[112:116]
    total = jnp.zeros((1, LANES), f32)
    lane = lane_index((1, LANES))
    for head in range(HEADS):
        at = (head % 4) * HEAD
        own = jnp.sum(
            skips[head // 4 : head // 4 + 1, at : at + HEAD], axis=1, keepdims=True
        )
        total = total + jnp.where(lane == head, own, 0.0)
    skip_ref[...] = total[:, :HEADS]


def large_body(final_ref, gate_ref, out_ref, grad_in_ref, grad_out_ref):
    grad_in_ref[:, 0, :] = final_ref[...].astype(f32)
    grad_in_ref[:, 1, :] = gate_ref[...].astype(f32)
    grad_out_ref[...] = out_ref[...].astype(f32)


def swapped(values):
    return lax.ppermute(values, "tensor", [(0, 1), (1, 0)])


def shards(
    hidden_in,
    segment_ids,
    norm_gain,
    in_weight,
    bc_weight,
    step_weight,
    conv_weight,
    conv_bias,
    bc_conv_weight,
    bc_conv_bias,
    step_bias,
    decay_log,
    skip_gain,
    gate_gain,
    out_weight,
    out_grad,
):
    side = lax.axis_index("tensor")
    width = hidden_in.shape[1]
    gathered = lax.all_gather(hidden_in, "tensor", axis=1, tiled=True)
    halo = lax.ppermute(gathered[ROWS - HALO :], CONTEXT, [(i, i + 1) for i in range(15)])
    cotangent = lax.all_gather(out_grad, "tensor", axis=1, tiled=True)
    win = in_weight.reshape(D, 2 * LOCAL)
    wbc = bc_weight.reshape(D, 2 * STATE)
    bc_taps = bc_conv_weight.reshape(4, 2 * STATE)
    segs = segment_ids[None]
    skip = skip_gain[None]
    step_rows = step_weight.T
    gain_row = gate_gain[None]
    dg = nt(cotangent, out_weight)
    ext_scratch = pltpu.VMEM((ROWS + 8, LANES), f32)
    pad_scratch = pltpu.VMEM((4, ROWS + 48, LANES), f32)
    (
        normed_ext,
        joined,
        pre,
        b_low,
        c_low,
        step,
        cum,
        sig,
        decay,
        state,
    ) = kernel_call(
        front_body,
        [
            ((EXT, D), bf16),
            ((EXT, LOCAL + 2 * STATE), f32),
            ((ROWS, LOCAL + 2 * STATE), f32),
            ((ROWS, STATE), bf16),
            ((ROWS, STATE), bf16),
            ((ROWS, LANES), f32),
            ((ROWS, LANES), f32),
            ((ROWS, LANES), f32),
            ((ROWS, LANES), f32),
            ((HEADS, CHUNK, STATE), bf16),
        ],
        (
            gathered,
            halo,
            norm_gain[None],
            win,
            wbc,
            step_rows,
            conv_weight,
            conv_bias[None],
            bc_taps,
            bc_conv_bias.reshape(1, 2 * STATE),
            segs,
            step_bias[None],
            decay_log[None],
        ),
        scratch=[ext_scratch, pltpu.VMEM((LANES, D), bf16)],
        blocks={3: ((D, LOCAL), (0, 0))},
    )
    pieces = lax.all_to_all(state, CONTEXT, 0, 0, tiled=True)
    (gate,) = kernel_call(
        gate_proj_body,
        [((ROWS, LOCAL), f32)],
        (normed_ext, win),
        blocks={1: ((D, LOCAL), (0, 1))},
    )
    (within,) = kernel_call(
        within_body,
        [((ROWS, LOCAL), f32)],
        (pre, step, cum, b_low, c_low, segs, skip),
        cost=12_000_000,
    )
    (starts,) = kernel_call(scan_body, [((16, HEAD, STATE), bf16)], (pieces,))
    start = lax.all_to_all(starts, CONTEXT, 0, 0, tiled=True).reshape(LOCAL, STATE)
    mixed, sums = kernel_call(
        mixed_body,
        [((ROWS, LOCAL), f32), ((ROWS, LANES), f32)],
        (within, start, c_low, cum, segs, gate, dg, gain_row),
    )
    gnorm, d_mixed, d_gate, grad_gate_gain, d_start = kernel_call(
        gate_body,
        [
            ((ROWS, LOCAL), bf16),
            ((ROWS, LOCAL), f32),
            ((ROWS, LOCAL), bf16),
            ((1, LOCAL), f32),
            ((HEADS, HEAD, STATE), bf16),
        ],
        (sums, swapped(sums), mixed, gate, dg, gain_row, c_low, cum, segs),
    )
    normed = normed_ext[HALO:]
    grad_out = tn(gnorm, cotangent).astype(bf16)
    grad_gate = tn(normed, d_gate).astype(bf16)
    grad_out, grad_gate = lax.psum((grad_out, grad_gate), EVERYONE)
    def later(
        d_start,
        gnorm,
        d_mixed,
        d_gate,
        grad_gate_gain,
        start,
        pieces,
        within,
        normed_ext,
        joined,
        pre,
        gathered,
        win,
    ):
        received = lax.all_to_all(d_start, CONTEXT, 0, 0, tiled=True)
        (adjoints,) = kernel_call(
            scan_back_body, [((16, HEAD, STATE), bf16)], (pieces, received)
        )
        adjoint = lax.all_to_all(adjoints, CONTEXT, 0, 0, tiled=True).reshape(LOCAL, STATE)
        out_terms = mm(gnorm, out_weight).astype(bf16)
        kept = lax.dynamic_slice_in_dim(out_terms, side * width, width, 1)
        given = lax.dynamic_slice_in_dim(out_terms, (1 - side) * width, width, 1)
        hidden_out = (
            hidden_in.astype(f32) + kept.astype(f32) + swapped(given).astype(f32)
        ).astype(bf16)
        d_xs, d_bc_part, d_cum, skip_grads = kernel_call(
            back_body,
            [
                ((ROWS, LOCAL), f32),
                ((ROWS, 2 * STATE), f32),
                ((ROWS, LANES), f32),
                ((1, LOCAL), f32),
            ],
            (d_mixed, pre, within, start, b_low, c_low, step, cum, segs, skip),
            cost=20_000_000,
        )
        d_bc, d_ext, d_step, conv_grads, small = kernel_call(
            carry_back_body,
            [
                ((ROWS, 2 * STATE), bf16),
                ((EXT, LOCAL), bf16),
                ((ROWS, LANES), bf16),
                ((8, LOCAL), f32),
                ((8, LANES), f32),
            ],
            (
                d_mixed,
                pre,
                joined,
                d_xs,
                d_bc_part,
                d_cum,
                start,
                adjoint,
                b_low,
                step,
                cum,
                sig,
                decay,
                segs,
                decay_log[None],
                skip,
                conv_weight,
            ),
            scratch=[ext_scratch, pad_scratch],
        )
        (grad_x,) = kernel_call(x_grad_body, [((D, LOCAL), bf16)], (normed_ext, d_ext))
        scattered_x = lax.all_to_all(
            grad_x.reshape(DEVICES, 16, LOCAL), EVERYONE, 0, 0, tiled=True
        )
        d_bc_ext, bc_conv_grads = kernel_call(
            bc_back_body,
            [((EXT, 2 * STATE), bf16), ((8, 2 * STATE), f32)],
            (d_bc, swapped(d_bc), pre, joined, segs, bc_taps),
            scratch=[ext_scratch, pad_scratch],
            cost=BC_COST,
        )
        (terms,) = kernel_call(
            terms_body,
            [((EXT, D), bf16)],
            (d_ext, d_gate, d_step, d_bc_ext, win, step_rows, wbc),
            cost=TERMS_COST,
        )
        other_terms = swapped(terms)
        halo_terms = (terms[:HALO].astype(f32) + other_terms[:HALO].astype(f32)).astype(bf16)
        returned = lax.ppermute(halo_terms, CONTEXT, [(i + 1, i) for i in range(15)])
        hidden_grad, grad_norm = kernel_call(
            hidden_body,
            [((ROWS, width), bf16), ((1, width), f32)],
            (gathered, terms, other_terms, returned, norm_gain[None], out_grad),
            cost=HIDDEN_COST,
        )
        (bundle,) = kernel_call(
            bundle_body,
            [((D, 256), bf16)],
            (
                normed_ext,
                d_bc_ext,
                d_step,
                conv_grads,
                bc_conv_grads,
                grad_gate_gain,
                grad_norm,
                skip_grads,
                small,
            ),
            cost=BUNDLE_COST,
        )
        bundle, scattered_x = lax.optimization_barrier((bundle, scattered_x))
        scattered = lax.all_to_all(
            bundle.reshape(DEVICES, 16, 256), EVERYONE, 0, 0, tiled=True
        )
        (spread,) = kernel_call(
            total_body, [((DEVICES, 16, LOCAL + 256), bf16)], (scattered_x, scattered)
        )
        final = lax.all_to_all(spread, EVERYONE, 0, 0, tiled=True).reshape(D, LOCAL + 256)
        return hidden_out, hidden_grad, final

    def nothing(*_):
        return (
            jnp.zeros((ROWS, width), bf16),
            jnp.zeros((ROWS, width), bf16),
            jnp.zeros((D, LOCAL + 256), bf16),
        )

    hidden_out, hidden_grad, final = lax.cond(
        segment_ids[0] >= 0,
        later,
        nothing,
        d_start,
        gnorm,
        d_mixed,
        d_gate,
        grad_gate_gain,
        start,
        pieces,
        within,
        normed_ext,
        joined,
        pre,
        gathered,
        win,
    )
    half = D // 2
    (
        grad_bc,
        grad_step,
        grad_conv,
        grad_conv_bias,
        grad_bc_conv,
        grad_bc_conv_bias,
        total_gate_gain,
        total_norm_gain,
        grad_skip,
        grad_step_bias,
        grad_decay_log,
    ) = kernel_call(
        few_body,
        [
            ((half, 2, STATE), f32),
            ((HEADS, D), f32),
            ((4, LOCAL), f32),
            ((1, LOCAL), f32),
            ((4, 2, STATE), f32),
            ((2, STATE), f32),
            ((1, LOCAL), f32),
            ((1, half), f32),
            ((1, HEADS), f32),
            ((1, HEADS), f32),
            ((1, HEADS), f32),
        ],
        (final,),
    )
    rows = pl.BlockSpec((D // 8, LOCAL), lambda i: (i, 0))
    grad_in, grad_out = pl.pallas_call(
        large_body,
        grid=(8,),
        out_shape=[
            jax.ShapeDtypeStruct((D, 2, LOCAL), f32),
            jax.ShapeDtypeStruct((LOCAL, D), f32),
        ],
        in_specs=[rows] * 3,
        out_specs=[pl.BlockSpec((D // 8, 2, LOCAL), lambda i: (i, 0, 0)), rows],
    )(final, grad_gate, grad_out)
    return (
        hidden_out,
        hidden_grad,
        total_norm_gain[0],
        grad_in,
        grad_bc,
        grad_step.T,
        grad_conv,
        grad_conv_bias[0],
        grad_bc_conv,
        grad_bc_conv_bias,
        grad_step_bias[0],
        grad_decay_log[0],
        grad_skip[0],
        total_gate_gain[0],
        grad_out,
    )


def solution(mesh):
    torus = Mesh(
        mesh.devices.reshape(mesh.shape["tensor"], mesh.shape["dp"], 4, 4),
        ("tensor", "dp", "context_0", "context_1"),
    )
    rows = ("dp", "context_0", "context_1")
    in_specs = (
        P(rows, "tensor"),
        P(rows),
        P(),
        P(None, None, "tensor"),
        P(),
        P(None, "tensor"),
        P(None, "tensor"),
        P("tensor"),
        P(),
        P(),
        P(),
        P("tensor"),
        P("tensor"),
        P("tensor"),
        P("tensor", None),
        P(rows, "tensor"),
    )
    out_specs = (
        P(rows, "tensor"),
        P(rows, "tensor"),
        P("tensor"),
        P(None, None, "tensor"),
        P("tensor", None, None),
        P(None, "tensor"),
        P(None, "tensor"),
        P("tensor"),
        P(),
        P(),
        P("tensor"),
        P("tensor"),
        P("tensor"),
        P("tensor"),
        P("tensor", None),
    )
    return jax.shard_map(
        shards, mesh=torus, in_specs=in_specs, out_specs=out_specs, check_vma=False
    )
```

```python
import jax
import jax.numpy as jnp
from jax import lax
from jax.experimental import pallas as pl
from jax.experimental.pallas import tpu as pltpu
from jax.sharding import Mesh
from jax.sharding import PartitionSpec as P

D = 1024
HEAD = 64
STATE = 128
INNER = 2048
ROWS = 256
HEADS = 16
LOCAL = 1024
HALO = 16
EXT = ROWS + HALO
LANES = 128
PAIRS = LOCAL // LANES
CHUNK = 80
DEVICES = 64
CONTEXT = ("context_0", "context_1")
EVERYONE = ("dp", "context_0", "context_1")
EPSILON = 1e-05
BC_COST = 10_000_000
TERMS_COST = 15_000_000
HIDDEN_COST = 9_000_000
BUNDLE_COST = 8_000_000
f32 = jnp.float32
bf16 = jnp.bfloat16
HIGHEST = lax.Precision.HIGHEST


def mm(a, b):
    return lax.dot_general(a, b, (((1,), (0,)), ((), ())), preferred_element_type=f32)


def nt(a, b):
    return lax.dot_general(a, b, (((1,), (1,)), ((), ())), preferred_element_type=f32)


def tn(a, b):
    return lax.dot_general(a, b, (((0,), (0,)), ((), ())), preferred_element_type=f32)


def exact(a, b):
    return lax.dot_general(
        a, b, (((1,), (0,)), ((), ())), precision=HIGHEST, preferred_element_type=f32
    )


def whole(shape, index=None):
    index = index or (0,) * len(shape)
    return pl.BlockSpec(shape, lambda i: index, pipeline_mode=pl.Buffered(1))


def kernel_call(body, outs, args, scratch=(), cost=0, vmem=56, blocks={}):
    return pl.pallas_call(
        body,
        grid=(1,),
        out_shape=[jax.ShapeDtypeStruct(shape, kind) for shape, kind in outs],
        in_specs=[whole(*blocks.get(i, (a.shape,))) for i, a in enumerate(args)],
        out_specs=[whole(shape) for shape, _ in outs],
        scratch_shapes=list(scratch),
        compiler_params=pltpu.CompilerParams(vmem_limit_bytes=vmem * 1024 * 1024),
        cost_estimate=pl.CostEstimate(flops=0, bytes_accessed=cost, transcendentals=0),
    )(*args)


def lane_index(shape):
    return lax.broadcasted_iota(jnp.int32, shape, 1)


def row_index(shape):
    return lax.broadcasted_iota(jnp.int32, shape, 0)


def spread_pair(columns, pair):
    rows = columns.shape[0]
    first = jnp.broadcast_to(columns[:, 2 * pair : 2 * pair + 1], (rows, LANES))
    second = jnp.broadcast_to(columns[:, 2 * pair + 1 : 2 * pair + 2], (rows, LANES))
    return jnp.where(lane_index((rows, LANES)) < HEAD, first, second)


def pair_mask(documents, seg_row):
    shape = (ROWS, ROWS)
    causal = row_index(shape) >= lane_index(shape)
    columns = jnp.concatenate([documents, documents], axis=1)
    return jnp.where((columns == seg_row) & causal, 0.0, -1e30).astype(f32)


def decay_block(cum, cum_t, head, bias):
    return jnp.exp(cum[:, head : head + 1] - cum_t[head : head + 1, :] + bias)


def document_before():
    piece = lax.axis_index("context_0") * 4 + lax.axis_index("context_1")
    return jnp.where(piece > 0, 2.0, 0.0).astype(f32)


def documents_of(seg_ref):
    seg_row = seg_ref[...].astype(f32) + 1.0
    return seg_row, jnp.broadcast_to(seg_row, (LANES, ROWS)).T


def tap_masks_of(documents, ext_ref):
    ext_ref[:8, :] = jnp.full((8, LANES), document_before(), f32)
    ext_ref[8:, :] = documents
    return [(ext_ref[5 + k : 5 + k + ROWS, :] == documents).astype(f32) for k in range(3)]


def end_decay(cum, documents):
    last = (documents == documents[ROWS - 1 : ROWS, :]).astype(f32)
    return jnp.exp(cum[ROWS - 1 : ROWS, :] - cum) * last


def entry_decay(cum, documents):
    return jnp.exp(cum) * (documents == document_before()).astype(f32)


def to_lanes(values):
    rows, count = values.shape
    return jnp.concatenate([values, jnp.zeros((rows, LANES - count), f32)], axis=1)


def front_body(
    hidden_ref,
    halo_ref,
    gain_ref,
    win_ref,
    wbc_ref,
    wst_ref,
    taps_ref,
    bias_ref,
    bc_taps_ref,
    bc_bias_ref,
    seg_ref,
    step_bias_ref,
    decay_log_ref,
    normed_ref,
    joined_ref,
    pre_ref,
    b_ref,
    c_ref,
    step_ref,
    cum_ref,
    sig_ref,
    decay_ref,
    state_ref,
    ext_ref,
    wide_ref,
):
    gain = gain_ref[...]
    for source, start, rows in ((halo_ref, 0, HALO), (hidden_ref, HALO, ROWS)):
        values = source[...].astype(f32)
        scale = lax.rsqrt(jnp.sum(values * values, axis=1, keepdims=True) / D + EPSILON)
        normed_ref[start : start + rows, :] = (values * scale * gain).astype(bf16)
    normed_ext = normed_ref[...]
    normed = normed_ref[HALO:, :]
    joined_ref[:, :LOCAL] = mm(normed_ext, win_ref[...])
    joined_ref[:, LOCAL:] = mm(normed_ext, wbc_ref[...])
    wide_ref[...] = jnp.zeros_like(wide_ref)
    wide_ref[:HEADS, :] = wst_ref[...]
    both = step_bias_ref[...]
    first = lax.axis_index("tensor") == 0
    local_bias = jnp.where(first, both[:, :HEADS], both[:, HEADS:])
    raw = nt(normed, wide_ref[...]) + to_lanes(local_bias)
    step = jnp.maximum(raw, 0.0) + jnp.log1p(jnp.exp(-jnp.abs(raw)))
    decay = step * to_lanes(-jnp.exp(decay_log_ref[...]))
    tri = (row_index((ROWS, ROWS)) >= lane_index((ROWS, ROWS))).astype(f32)
    cum = exact(tri, decay)
    step_ref[...] = step
    cum_ref[...] = cum
    sig_ref[...] = jax.nn.sigmoid(raw)
    decay_ref[...] = decay
    _, documents = documents_of(seg_ref)
    tap_masks = tap_masks_of(documents, ext_ref)

    def conv(at, taps, bias):
        lanes = slice(at, at + LANES)
        total = jnp.broadcast_to(bias, (ROWS, LANES))
        for k in range(4):
            part = joined_ref[HALO - 3 + k : HALO - 3 + k + ROWS, lanes] * taps[k : k + 1]
            total = total + (part * tap_masks[k] if k < 3 else part)
        pre_ref[:, lanes] = total
        return total * jax.nn.sigmoid(total)

    b_low = conv(LOCAL, bc_taps_ref[:, :STATE], bc_bias_ref[:, :STATE]).astype(bf16)
    c_low = conv(LOCAL + STATE, bc_taps_ref[:, STATE:], bc_bias_ref[:, STATE:]).astype(bf16)
    b_ref[...] = b_low
    c_ref[...] = c_low
    gains = jnp.exp(cum[ROWS - 1 : ROWS, :])
    ended = step * end_decay(cum, documents)
    for pair in range(PAIRS):
        lanes = slice(pair * LANES, (pair + 1) * LANES)
        x = conv(pair * LANES, taps_ref[:, lanes], bias_ref[:, lanes])
        state = tn((x * spread_pair(ended, pair)).astype(bf16), b_low).astype(bf16)
        for side in range(2):
            head = 2 * pair + side
            state_ref[head, :HEAD, :] = state[side * HEAD : (side + 1) * HEAD, :]
            state_ref[head, HEAD:, :] = jnp.broadcast_to(
                gains[:, head : head + 1], (CHUNK - HEAD, STATE)
            ).astype(bf16)


def gate_proj_body(normed_ref, win_ref, gate_ref):
    gate_ref[...] = mm(normed_ref[HALO:, :], win_ref[...])


def within_body(pre_ref, step_ref, cum_ref, b_ref, c_ref, seg_ref, skip_ref, within_ref):
    seg_row, documents = documents_of(seg_ref)
    products = nt(c_ref[...], b_ref[...])
    bias = pair_mask(documents, seg_row)
    step = step_ref[...]
    cum = cum_ref[...]
    cum_t = cum.T
    skip = skip_ref[...]
    first_half = lane_index((ROWS, LANES)) < HEAD
    for pair in range(PAIRS):
        lanes = slice(pair * LANES, (pair + 1) * LANES)
        pre = pre_ref[:, lanes]
        x = pre * jax.nn.sigmoid(pre)
        xs_low = (x * spread_pair(step, pair)).astype(bf16)
        sums = []
        for head in (2 * pair, 2 * pair + 1):
            block = (decay_block(cum, cum_t, head, bias) * products).astype(bf16)
            sums.append(mm(block, xs_low))
        within_ref[:, lanes] = (
            jnp.where(first_half, sums[0], sums[1]) + spread_pair(skip, pair) * x
        )


def scan_body(pieces_ref, start_ref):
    state = jnp.zeros((HEAD, STATE), f32)
    for k in range(16):
        start_ref[k] = state.astype(bf16)
        if k < 15:
            gain = pieces_ref[k, HEAD : HEAD + 16, :].astype(f32)[0:1, :]
            state = state * gain + pieces_ref[k, :HEAD, :].astype(f32)


def scan_back_body(pieces_ref, grads_ref, adjoint_ref):
    state = jnp.zeros((HEAD, STATE), f32)
    for k in reversed(range(16)):
        adjoint_ref[k] = state.astype(bf16)
        if k > 0:
            gain = pieces_ref[k, HEAD : HEAD + 16, :].astype(f32)[0:1, :]
            state = state * gain + grads_ref[k].astype(f32)


def mixed_body(
    within_ref, start_ref, c_ref, cum_ref, seg_ref, gate_ref, dg_ref, gain_ref, mixed_ref, sums_ref
):
    entry = entry_decay(cum_ref[...], documents_of(seg_ref)[1])
    c_low = c_ref[...]
    squares = jnp.zeros((ROWS, LANES), f32)
    dots = jnp.zeros((ROWS, LANES), f32)
    for pair in range(PAIRS):
        lanes = slice(pair * LANES, (pair + 1) * LANES)
        carried = nt(c_low, start_ref[lanes, :])
        mixed = within_ref[:, lanes] + spread_pair(entry, pair) * carried
        mixed_ref[:, lanes] = mixed
        gate = gate_ref[:, lanes]
        gated = mixed * (gate * jax.nn.sigmoid(gate))
        squares = squares + gated * gated
        dots = dots + gated * gain_ref[:, lanes] * dg_ref[:, lanes]
    lane = lane_index((ROWS, LANES))
    sums_ref[...] = jnp.where(
        lane == 0,
        jnp.sum(squares, axis=1, keepdims=True),
        jnp.where(lane == 1, jnp.sum(dots, axis=1, keepdims=True), 0.0),
    )


def gate_body(
    sums_ref,
    other_ref,
    mixed_ref,
    gate_ref,
    dg_ref,
    gain_ref,
    c_ref,
    cum_ref,
    seg_ref,
    cotangent_ref,
    normed_ref,
    gnorm_ref,
    d_mixed_ref,
    d_gate_ref,
    grad_gain_ref,
    d_start_ref,
    grad_out_ref,
    grad_gate_ref,
):
    normed_t = normed_ref[HALO:, :].T
    cotangent = cotangent_ref[...]
    sums = sums_ref[...] + other_ref[...]
    rate = lax.rsqrt(sums[:, 0:1] / INNER + EPSILON)
    back = rate * rate * rate * sums[:, 1:2] / INNER
    rate = jnp.broadcast_to(rate, (ROWS, LANES))
    back = jnp.broadcast_to(back, (ROWS, LANES))
    entry = entry_decay(cum_ref[...], documents_of(seg_ref)[1])
    c_low = c_ref[...]
    for pair in range(PAIRS):
        lanes = slice(pair * LANES, (pair + 1) * LANES)
        mixed = mixed_ref[:, lanes]
        gate = gate_ref[:, lanes]
        gain = gain_ref[:, lanes]
        dg = dg_ref[:, lanes]
        sig = jax.nn.sigmoid(gate)
        silu = gate * sig
        gated = mixed * silu
        scaled = gated * rate
        gnorm_ref[:, lanes] = (scaled * gain).astype(bf16)
        grad_gain_ref[:, lanes] = jnp.sum(dg * scaled, axis=0, keepdims=True)
        d_gated = rate * gain * dg - gated * back
        d_mixed = d_gated * silu
        d_mixed_ref[:, lanes] = d_mixed
        d_gate_ref[:, lanes] = (d_gated * mixed * (sig + silu * (1.0 - sig))).astype(bf16)
        d_state = tn((d_mixed * spread_pair(entry, pair)).astype(bf16), c_low).astype(bf16)
        for side in range(2):
            d_start_ref[2 * pair + side] = d_state[side * HEAD : (side + 1) * HEAD, :]
        if pair % 2 == 1:
            group = slice((pair - 1) * LANES, (pair + 1) * LANES)
            grad_out_ref[group, :] = tn(gnorm_ref[:, group], cotangent).astype(bf16)
            grad_gate_ref[:, group] = mm(normed_t, d_gate_ref[:, group]).astype(bf16)


def head_sums(values, pair):
    shape = (LANES, LANES)
    into = lane_index(shape) == 2 * pair + (row_index(shape) >= HEAD).astype(jnp.int32)
    into = into.astype(bf16)
    high = values.astype(bf16)
    low = (values - high.astype(f32)).astype(bf16)
    return mm(high, into) + mm(low, into)


def conv_back(d_pre, joined_ref, source, lanes, taps, masks, pad_ref, into):
    total = None
    sums = []
    for k in range(4):
        joined = joined_ref[HALO - 3 + k : HALO - 3 + k + ROWS, source]
        part = d_pre * masks[k] if k < 3 else d_pre
        sums.append(jnp.sum(part * joined, axis=0, keepdims=True))
        pad_ref[k, 24 : 24 + ROWS, :] = part * taps[k : k + 1]
        moved = pad_ref[k, 24 - 13 - k : 24 - 13 - k + EXT, :]
        total = moved if total is None else total + moved
    sums.append(jnp.sum(d_pre, axis=0, keepdims=True))
    into[:, lanes] = jnp.concatenate(sums + [jnp.zeros((3, LANES), f32)], axis=0)
    return total


def back_body(
    d_mixed_ref,
    pre_ref,
    within_ref,
    start_ref,
    b_ref,
    c_ref,
    step_ref,
    cum_ref,
    seg_ref,
    skip_ref,
    d_xs_ref,
    d_bc_ref,
    d_cum_ref,
    skip_grad_ref,
):
    seg_row, documents = documents_of(seg_ref)
    skips = skip_ref[...]
    cum = cum_ref[...]
    cum_t = cum.T
    step = step_ref[...]
    b_low = b_ref[...]
    c_low = c_ref[...]
    products = nt(c_low, b_low)
    bias = pair_mask(documents, seg_row)
    entry = entry_decay(cum, documents)
    first_half = lane_index((ROWS, LANES)) < HEAD
    d_products = jnp.zeros((ROWS, ROWS), f32)
    d_c = jnp.zeros((ROWS, STATE), f32)
    d_cum = jnp.zeros((ROWS, LANES), f32)
    for pair in range(PAIRS):
        lanes = slice(pair * LANES, (pair + 1) * LANES)
        pre = pre_ref[:, lanes]
        x = pre * jax.nn.sigmoid(pre)
        xs_low = (x * spread_pair(step, pair)).astype(bf16)
        d_mixed = d_mixed_ref[:, lanes]
        dy_low = d_mixed.astype(bf16)
        zero = jnp.zeros_like(dy_low)
        parts = []
        for side in range(2):
            head = 2 * pair + side
            own = jnp.where(first_half if side == 0 else ~first_half, dy_low, zero)
            decays = decay_block(cum, cum_t, head, bias)
            d_products = d_products + decays * nt(own, xs_low)
            parts.append(tn((decays * products).astype(bf16), dy_low))
        d_xs = jnp.where(first_half, parts[0], parts[1])
        d_xs_ref[:, lanes] = d_xs
        within = within_ref[:, lanes] - spread_pair(skips, pair) * x
        through = dy_low.astype(f32) * within - xs_low.astype(f32) * d_xs
        start_low = start_ref[lanes, :]
        carried = d_mixed * spread_pair(entry, pair)
        d_c = d_c + mm(carried.astype(bf16), start_low)
        d_cum = d_cum + head_sums(through + carried * nt(c_low, start_low), pair)
        skip_grad_ref[:, lanes] = jnp.sum(d_mixed * x, axis=0, keepdims=True)
    d_products = d_products.astype(bf16)
    d_bc_ref[:, :STATE] = tn(d_products, c_low)
    d_bc_ref[:, STATE:] = d_c + mm(d_products, b_low)
    d_cum_ref[...] = d_cum


def carry_back_body(
    d_mixed_ref,
    pre_ref,
    joined_ref,
    d_xs_ref,
    d_bc_in_ref,
    d_cum_ref,
    start_ref,
    adjoint_ref,
    b_ref,
    step_ref,
    cum_ref,
    sig_ref,
    decay_ref,
    seg_ref,
    decay_log_ref,
    skip_ref,
    taps_ref,
    d_bc_ref,
    d_ext_ref,
    d_step_ref,
    conv_ref,
    small_ref,
    ext_ref,
    pad_ref,
):
    _, documents = documents_of(seg_ref)
    tap_masks = tap_masks_of(documents, ext_ref)
    pad_ref[...] = jnp.zeros_like(pad_ref)
    skips = skip_ref[...]
    cum = cum_ref[...]
    step = step_ref[...]
    b_low = b_ref[...]
    end = end_decay(cum, documents)
    gains = jnp.exp(cum[ROWS - 1 : ROWS, :])
    lane = lane_index((1, LANES))
    d_b = d_bc_in_ref[:, :STATE]
    d_cum = d_cum_ref[...]
    d_step = jnp.zeros((ROWS, LANES), f32)
    d_last = jnp.zeros((8, LANES), f32)
    d_whole = jnp.zeros((1, LANES), f32)
    for pair in range(PAIRS):
        lanes = slice(pair * LANES, (pair + 1) * LANES)
        pre = pre_ref[:, lanes]
        sig = jax.nn.sigmoid(pre)
        x = pre * sig
        steps = spread_pair(step, pair)
        ends = spread_pair(end, pair)
        xs = x * steps
        adjoint_low = adjoint_ref[lanes, :]
        d_ended = nt(b_low, adjoint_low) * ends
        d_b = d_b + mm((xs * ends).astype(bf16), adjoint_low)
        at_end = xs * d_ended
        d_cum = d_cum - head_sums(at_end, pair)
        d_xs = d_xs_ref[:, lanes] + d_ended
        d_step = d_step + head_sums(x * d_xs, pair)
        end_sum = jnp.sum(at_end, axis=0, keepdims=True)
        d_last = d_last + head_sums(jnp.broadcast_to(end_sum, (8, LANES)), pair)
        meeting = start_ref[lanes, :].astype(f32) * adjoint_low.astype(f32)
        for side in range(2):
            whole_sum = jnp.sum(
                jnp.sum(meeting[side * HEAD : (side + 1) * HEAD, :], axis=0, keepdims=True),
                axis=1,
                keepdims=True,
            )
            d_whole = d_whole + jnp.where(lane == 2 * pair + side, whole_sum, 0.0)
        d_act = steps * d_xs + spread_pair(skips, pair) * d_mixed_ref[:, lanes]
        d_pre = d_act * (sig + x * (1.0 - sig))
        d_ext_ref[:, lanes] = conv_back(
            d_pre, joined_ref, lanes, lanes, taps_ref[:, lanes], tap_masks, pad_ref, conv_ref
        ).astype(bf16)
    d_bc_ref[:, :STATE] = d_b.astype(bf16)
    d_bc_ref[:, STATE:] = d_bc_in_ref[:, STATE:].astype(bf16)
    tri = (row_index((ROWS, ROWS)) <= lane_index((ROWS, ROWS))).astype(f32)
    d_decay = exact(tri, d_cum) + (d_last[0:1, :] + gains * d_whole)
    d_raw = (d_step + d_decay * to_lanes(-jnp.exp(decay_log_ref[...]))) * sig_ref[...]
    d_step_ref[...] = d_raw.astype(bf16)
    small_ref[...] = jnp.concatenate(
        [
            jnp.sum(d_raw, axis=0, keepdims=True),
            jnp.sum(d_decay * decay_ref[...], axis=0, keepdims=True),
            jnp.zeros((6, LANES), f32),
        ],
        axis=0,
    )


def bc_back_body(
    own_ref, other_ref, pre_ref, joined_ref, seg_ref, taps_ref, d_ext_ref, conv_ref, ext_ref, pad_ref
):
    _, documents = documents_of(seg_ref)
    tap_masks = tap_masks_of(documents, ext_ref)
    pad_ref[...] = jnp.zeros_like(pad_ref)
    for half in range(2):
        lanes = slice(half * LANES, (half + 1) * LANES)
        source = slice(LOCAL + half * LANES, LOCAL + (half + 1) * LANES)
        pre = pre_ref[:, source]
        sig = jax.nn.sigmoid(pre)
        d_act = own_ref[:, lanes].astype(f32) + other_ref[:, lanes].astype(f32)
        d_pre = d_act * (sig + pre * sig * (1.0 - sig))
        d_ext_ref[:, lanes] = conv_back(
            d_pre, joined_ref, source, lanes, taps_ref[:, lanes], tap_masks, pad_ref, conv_ref
        ).astype(bf16)


def terms_body(dx_ref, dz_ref, dst_ref, dbc_ref, win_ref, wst_ref, wbc_ref, out_ref):
    first = lax.axis_index("tensor") == 0
    dbc = dbc_ref[...]
    wbc = wbc_ref[...]
    half = jnp.where(first, dbc[:, :STATE], dbc[:, STATE:])
    weights = jnp.where(first, wbc[:, :STATE], wbc[:, STATE:])
    both = nt(dx_ref[...], win_ref[:, :LOCAL]) + nt(half, weights)
    out_ref[:HALO, :] = both[:HALO, :].astype(bf16)
    own = nt(dz_ref[...], win_ref[:, LOCAL:]) + mm(dst_ref[:, :HEADS], wst_ref[...])
    out_ref[HALO:, :] = (both[HALO:, :] + own).astype(bf16)


def hidden_body(
    hidden_ref, terms_ref, other_ref, returned_ref, gain_ref, out_grad_ref, grad_ref, gain_grad_ref
):
    values = hidden_ref[...].astype(f32)
    scale = lax.rsqrt(jnp.sum(values * values, axis=1, keepdims=True) / D + EPSILON)
    d_normed = terms_ref[HALO:, :].astype(f32) + other_ref[HALO:, :].astype(f32)
    tail = jnp.concatenate(
        [jnp.zeros((ROWS - HALO, D), f32), returned_ref[...].astype(f32)], axis=0
    )
    d_normed = d_normed + tail
    first = lax.axis_index("tensor") == 0
    half = D // 2
    grads = jnp.sum(d_normed * values * scale, axis=0, keepdims=True)
    gain_grad_ref[...] = jnp.where(first, grads[:, :half], grads[:, half:])
    scaled = d_normed * gain_ref[...]
    dots = jnp.sum(values * scaled, axis=1, keepdims=True)
    result = scale * scaled - values * (scale * scale * scale * dots / D)
    own = jnp.where(first, result[:, :half], result[:, half:])
    grad_ref[...] = (out_grad_ref[...].astype(f32) + own).astype(bf16)


def x_grad_body(normed_ref, dx_ref, grad_ref):
    grad_ref[...] = tn(normed_ref[...], dx_ref[...]).astype(bf16)


def bundle_body(
    normed_ref,
    dbc_ref,
    dst_ref,
    conv_ref,
    bc_conv_ref,
    gate_gain_ref,
    norm_gain_ref,
    skip_ref,
    small_ref,
    bundle_ref,
):
    half = D // 2
    first = lax.axis_index("tensor") == 0
    share = jnp.where(first, normed_ref[:, :half], normed_ref[:, half:])
    bundle_ref[:half, :] = tn(share, dbc_ref[...]).astype(bf16)
    steps = tn(dst_ref[...], normed_ref[HALO:, :])
    for part in range(4):
        at = half + part * HEADS
        bundle_ref[at : at + HEADS, :] = steps[:HEADS, part * 256 : part * 256 + 256].astype(bf16)
    row = half + 4 * HEADS
    pieces = []
    for part in range(4):
        pieces.append(conv_ref[:, part * 256 : part * 256 + 256])
    pieces.append(bc_conv_ref[...])
    lone = [gate_gain_ref[:, part * 256 : part * 256 + 256] for part in range(4)]
    lone += [norm_gain_ref[:, part * 256 : part * 256 + 256] for part in range(2)]
    lone += [jnp.concatenate([small_ref[0:1, :], small_ref[1:2, :]], axis=1)]
    lone += [jnp.zeros((1, 256), f32)]
    pieces.append(jnp.concatenate(lone, axis=0))
    skips = skip_ref[...]
    pieces.append(
        jnp.concatenate(
            [skips[:, part * 256 : part * 256 + 256] for part in range(4)]
            + [jnp.zeros((4, 256), f32)],
            axis=0,
        )
    )
    pieces.append(jnp.zeros((8, 256), f32))
    bundle_ref[row : row + 64, :] = jnp.concatenate(pieces, axis=0).astype(bf16)
    bundle_ref[row + 64 :, :] = jnp.zeros((half - 4 * HEADS - 64, 256), bf16)


def total_body(x_ref, few_ref, out_ref):
    for received_ref, lanes in ((x_ref, slice(0, LOCAL)), (few_ref, slice(LOCAL, LOCAL + 256))):
        total = jnp.zeros(received_ref.shape[1:], f32)
        for k in range(DEVICES):
            total = total + received_ref[k].astype(f32)
        total = total.astype(bf16)
        for k in range(DEVICES):
            out_ref[k, :, lanes] = total


def few_body(
    final_ref,
    bc_ref,
    step_ref,
    conv_ref,
    conv_bias_ref,
    bc_conv_ref,
    bc_conv_bias_ref,
    gate_gain_ref,
    norm_gain_ref,
    skip_ref,
    step_bias_ref,
    decay_log_ref,
):
    half = D // 2
    grads = final_ref[:half, LOCAL:].astype(f32)
    bc_ref[:, 0, :] = grads[:, :STATE]
    bc_ref[:, 1, :] = grads[:, STATE:]
    rest = final_ref[half : half + 128, LOCAL:].astype(f32)
    for part in range(4):
        step_ref[:, part * 256 : part * 256 + 256] = rest[part * HEADS : (part + 1) * HEADS]
    conv = jnp.concatenate([rest[64 + part * 8 : 72 + part * 8] for part in range(4)], axis=1)
    conv_ref[...] = conv[:4]
    conv_bias_ref[...] = conv[4:5]
    bc = rest[96:104]
    for side in range(2):
        lanes = slice(side * STATE, (side + 1) * STATE)
        bc_conv_ref[:, side, :] = bc[:4, lanes]
        bc_conv_bias_ref[side : side + 1, :] = bc[4:5, lanes]
    lone = rest[104:112]
    gate_gain_ref[...] = jnp.concatenate([lone[part : part + 1] for part in range(4)], axis=1)
    norm_gain_ref[...] = jnp.concatenate([lone[part : part + 1] for part in range(4, 6)], axis=1)
    step_bias_ref[...] = lone[6:7, :HEADS]
    decay_log_ref[...] = lone[6:7, LANES : LANES + HEADS]
    skips = rest[112:116]
    total = jnp.zeros((1, LANES), f32)
    lane = lane_index((1, LANES))
    for head in range(HEADS):
        at = (head % 4) * HEAD
        own = jnp.sum(
            skips[head // 4 : head // 4 + 1, at : at + HEAD], axis=1, keepdims=True
        )
        total = total + jnp.where(lane == head, own, 0.0)
    skip_ref[...] = total[:, :HEADS]


PARTS = 4


def x_rows_body(final_ref, grad_in_ref, wide_ref, sem):
    wide_ref[...] = final_ref[...].astype(f32)
    copy = pltpu.make_async_copy(wide_ref, grad_in_ref.at[:, 0, :], sem)
    copy.start()
    copy.wait()


def early_rows_body(
    _, gate_ref, out_ref, grad_in_ref, grad_out_ref, low_ref, wide_ref, in_sems, out_sems
):
    size = D // PARTS
    loads, stores = [], []
    for part in range(PARTS):
        rows = slice(part * size, (part + 1) * size)
        for which, source in enumerate((gate_ref, out_ref)):
            loads.append(
                pltpu.make_async_copy(
                    source.at[rows, :], low_ref.at[which, rows, :], in_sems.at[which, part]
                )
            )
    for load in loads:
        load.start()
    for part in range(PARTS):
        rows = slice(part * size, (part + 1) * size)
        for which in range(2):
            target = grad_out_ref.at[rows, :] if which else grad_in_ref.at[rows, 1, :]
            loads[2 * part + which].wait()
            wide_ref[which, rows, :] = low_ref[which, rows, :].astype(f32)
            stores.append(
                pltpu.make_async_copy(
                    wide_ref.at[which, rows, :], target, out_sems.at[which, part]
                )
            )
            stores[-1].start()
    for store in stores:
        store.wait()


def swapped(values):
    return lax.ppermute(values, "tensor", [(0, 1), (1, 0)])


def shards(
    hidden_in,
    segment_ids,
    norm_gain,
    in_weight,
    bc_weight,
    step_weight,
    conv_weight,
    conv_bias,
    bc_conv_weight,
    bc_conv_bias,
    step_bias,
    decay_log,
    skip_gain,
    gate_gain,
    out_weight,
    out_grad,
):
    side = lax.axis_index("tensor")
    width = hidden_in.shape[1]
    gathered = lax.all_gather(hidden_in, "tensor", axis=1, tiled=True)
    halo = lax.ppermute(gathered[ROWS - HALO :], CONTEXT, [(i, i + 1) for i in range(15)])
    win = in_weight.reshape(D, 2 * LOCAL)
    wbc = bc_weight.reshape(D, 2 * STATE)
    bc_taps = bc_conv_weight.reshape(4, 2 * STATE)
    segs = segment_ids[None]
    skip = skip_gain[None]
    step_rows = step_weight.T
    gain_row = gate_gain[None]
    ext_scratch = pltpu.VMEM((ROWS + 8, LANES), f32)
    pad_scratch = pltpu.VMEM((4, ROWS + 48, LANES), f32)
    (
        normed_ext,
        joined,
        pre,
        b_low,
        c_low,
        step,
        cum,
        sig,
        decay,
        state,
    ) = kernel_call(
        front_body,
        [
            ((EXT, D), bf16),
            ((EXT, LOCAL + 2 * STATE), f32),
            ((ROWS, LOCAL + 2 * STATE), f32),
            ((ROWS, STATE), bf16),
            ((ROWS, STATE), bf16),
            ((ROWS, LANES), f32),
            ((ROWS, LANES), f32),
            ((ROWS, LANES), f32),
            ((ROWS, LANES), f32),
            ((HEADS, CHUNK, STATE), bf16),
        ],
        (
            gathered,
            halo,
            norm_gain[None],
            win,
            wbc,
            step_rows,
            conv_weight,
            conv_bias[None],
            bc_taps,
            bc_conv_bias.reshape(1, 2 * STATE),
            segs,
            step_bias[None],
            decay_log[None],
        ),
        scratch=[ext_scratch, pltpu.VMEM((LANES, D), bf16)],
        blocks={3: ((D, LOCAL), (0, 0))},
    )
    late_grad, state = lax.optimization_barrier((out_grad, state))
    cotangent = lax.all_gather(late_grad, "tensor", axis=1, tiled=True)
    dg = nt(cotangent, out_weight)
    pieces = lax.all_to_all(state, CONTEXT, 0, 0, tiled=True)
    (gate,) = kernel_call(
        gate_proj_body,
        [((ROWS, LOCAL), f32)],
        (normed_ext, win),
        blocks={1: ((D, LOCAL), (0, 1))},
    )
    (within,) = kernel_call(
        within_body,
        [((ROWS, LOCAL), f32)],
        (pre, step, cum, b_low, c_low, segs, skip),
        cost=12_000_000,
    )
    pieces, dg = lax.optimization_barrier((pieces, dg))
    (starts,) = kernel_call(scan_body, [((16, HEAD, STATE), bf16)], (pieces,))
    start = lax.all_to_all(starts, CONTEXT, 0, 0, tiled=True).reshape(LOCAL, STATE)
    mixed, sums = kernel_call(
        mixed_body,
        [((ROWS, LOCAL), f32), ((ROWS, LANES), f32)],
        (within, start, c_low, cum, segs, gate, dg, gain_row),
    )
    gnorm, d_mixed, d_gate, grad_gate_gain, d_start, grad_out, grad_gate = kernel_call(
        gate_body,
        [
            ((ROWS, LOCAL), bf16),
            ((ROWS, LOCAL), f32),
            ((ROWS, LOCAL), bf16),
            ((1, LOCAL), f32),
            ((HEADS, HEAD, STATE), bf16),
            ((LOCAL, D), bf16),
            ((D, LOCAL), bf16),
        ],
        (sums, swapped(sums), mixed, gate, dg, gain_row, c_low, cum, segs, cotangent, normed_ext),
    )
    grad_out, grad_gate = lax.psum((grad_out, grad_gate), EVERYONE)
    def later(
        d_start,
        gnorm,
        d_mixed,
        d_gate,
        grad_gate_gain,
        start,
        pieces,
        within,
        normed_ext,
        joined,
        pre,
        gathered,
        win,
    ):
        received = lax.all_to_all(d_start, CONTEXT, 0, 0, tiled=True)
        (adjoints,) = kernel_call(
            scan_back_body, [((16, HEAD, STATE), bf16)], (pieces, received)
        )
        adjoint = lax.all_to_all(adjoints, CONTEXT, 0, 0, tiled=True).reshape(LOCAL, STATE)
        out_terms = mm(gnorm, out_weight).astype(bf16)
        kept = lax.dynamic_slice_in_dim(out_terms, side * width, width, 1)
        given = lax.dynamic_slice_in_dim(out_terms, (1 - side) * width, width, 1)
        hidden_out = (
            hidden_in.astype(f32) + kept.astype(f32) + swapped(given).astype(f32)
        ).astype(bf16)
        d_xs, d_bc_part, d_cum, skip_grads = kernel_call(
            back_body,
            [
                ((ROWS, LOCAL), f32),
                ((ROWS, 2 * STATE), f32),
                ((ROWS, LANES), f32),
                ((1, LOCAL), f32),
            ],
            (d_mixed, pre, within, start, b_low, c_low, step, cum, segs, skip),
            cost=20_000_000,
        )
        d_bc, d_ext, d_step, conv_grads, small = kernel_call(
            carry_back_body,
            [
                ((ROWS, 2 * STATE), bf16),
                ((EXT, LOCAL), bf16),
                ((ROWS, LANES), bf16),
                ((8, LOCAL), f32),
                ((8, LANES), f32),
            ],
            (
                d_mixed,
                pre,
                joined,
                d_xs,
                d_bc_part,
                d_cum,
                start,
                adjoint,
                b_low,
                step,
                cum,
                sig,
                decay,
                segs,
                decay_log[None],
                skip,
                conv_weight,
            ),
            scratch=[ext_scratch, pad_scratch],
        )
        (grad_x,) = kernel_call(x_grad_body, [((D, LOCAL), bf16)], (normed_ext, d_ext))
        scattered_x = lax.all_to_all(
            grad_x.reshape(DEVICES, 16, LOCAL), EVERYONE, 0, 0, tiled=True
        )
        d_bc_ext, bc_conv_grads = kernel_call(
            bc_back_body,
            [((EXT, 2 * STATE), bf16), ((8, 2 * STATE), f32)],
            (d_bc, swapped(d_bc), pre, joined, segs, bc_taps),
            scratch=[ext_scratch, pad_scratch],
            cost=BC_COST,
        )
        (terms,) = kernel_call(
            terms_body,
            [((EXT, D), bf16)],
            (d_ext, d_gate, d_step, d_bc_ext, win, step_rows, wbc),
            cost=TERMS_COST,
        )
        other_terms = swapped(terms)
        halo_terms = (terms[:HALO].astype(f32) + other_terms[:HALO].astype(f32)).astype(bf16)
        returned = lax.ppermute(halo_terms, CONTEXT, [(i + 1, i) for i in range(15)])
        hidden_grad, grad_norm = kernel_call(
            hidden_body,
            [((ROWS, width), bf16), ((1, width), f32)],
            (gathered, terms, other_terms, returned, norm_gain[None], out_grad),
            cost=HIDDEN_COST,
        )
        (bundle,) = kernel_call(
            bundle_body,
            [((D, 256), bf16)],
            (
                normed_ext,
                d_bc_ext,
                d_step,
                conv_grads,
                bc_conv_grads,
                grad_gate_gain,
                grad_norm,
                skip_grads,
                small,
            ),
            cost=BUNDLE_COST,
        )
        bundle, scattered_x = lax.optimization_barrier((bundle, scattered_x))
        scattered = lax.all_to_all(
            bundle.reshape(DEVICES, 16, 256), EVERYONE, 0, 0, tiled=True
        )
        (spread,) = kernel_call(
            total_body, [((DEVICES, 16, LOCAL + 256), bf16)], (scattered_x, scattered)
        )
        final = lax.all_to_all(spread, EVERYONE, 0, 0, tiled=True).reshape(D, LOCAL + 256)
        return hidden_out, hidden_grad, final

    def nothing(*_):
        return (
            jnp.zeros((ROWS, width), bf16),
            jnp.zeros((ROWS, width), bf16),
            jnp.zeros((D, LOCAL + 256), bf16),
        )

    hidden_out, hidden_grad, final = lax.cond(
        segment_ids[0] >= 0,
        later,
        nothing,
        d_start,
        gnorm,
        d_mixed,
        d_gate,
        grad_gate_gain,
        start,
        pieces,
        within,
        normed_ext,
        joined,
        pre,
        gathered,
        win,
    )
    half = D // 2
    (
        grad_bc,
        grad_step,
        grad_conv,
        grad_conv_bias,
        grad_bc_conv,
        grad_bc_conv_bias,
        total_gate_gain,
        total_norm_gain,
        grad_skip,
        grad_step_bias,
        grad_decay_log,
    ) = kernel_call(
        few_body,
        [
            ((half, 2, STATE), f32),
            ((HEADS, D), f32),
            ((4, LOCAL), f32),
            ((1, LOCAL), f32),
            ((4, 2, STATE), f32),
            ((2, STATE), f32),
            ((1, LOCAL), f32),
            ((1, half), f32),
            ((1, HEADS), f32),
            ((1, HEADS), f32),
            ((1, HEADS), f32),
        ],
        (final,),
    )
    anywhere = pl.BlockSpec(memory_space=pl.ANY)
    params = pltpu.CompilerParams(vmem_limit_bytes=60 * 1024 * 1024)
    grad_in = pl.pallas_call(
        x_rows_body,
        grid=(1,),
        out_shape=jax.ShapeDtypeStruct((D, 2, LOCAL), f32),
        in_specs=[whole((D, LOCAL))],
        out_specs=anywhere,
        scratch_shapes=[pltpu.VMEM((D, LOCAL), f32), pltpu.SemaphoreType.DMA],
        compiler_params=params,
    )(final)
    grad_in, grad_out = pl.pallas_call(
        early_rows_body,
        out_shape=[
            jax.ShapeDtypeStruct((D, 2, LOCAL), f32),
            jax.ShapeDtypeStruct((LOCAL, D), f32),
        ],
        in_specs=[anywhere] * 3,
        out_specs=[anywhere] * 2,
        scratch_shapes=[
            pltpu.VMEM((2, D, LOCAL), bf16),
            pltpu.VMEM((2, D, LOCAL), f32),
            pltpu.SemaphoreType.DMA((2, PARTS)),
            pltpu.SemaphoreType.DMA((2, PARTS)),
        ],
        input_output_aliases={0: 0},
        compiler_params=params,
    )(grad_in, grad_gate, grad_out)
    return (
        hidden_out,
        hidden_grad,
        total_norm_gain[0],
        grad_in,
        grad_bc,
        grad_step.T,
        grad_conv,
        grad_conv_bias[0],
        grad_bc_conv,
        grad_bc_conv_bias,
        grad_step_bias[0],
        grad_decay_log[0],
        grad_skip[0],
        total_gate_gain[0],
        grad_out,
    )


def solution(mesh):
    torus = Mesh(
        mesh.devices.reshape(mesh.shape["tensor"], mesh.shape["dp"], 4, 4),
        ("tensor", "dp", "context_0", "context_1"),
    )
    rows = ("dp", "context_0", "context_1")
    in_specs = (
        P(rows, "tensor"),
        P(rows),
        P(),
        P(None, None, "tensor"),
        P(),
        P(None, "tensor"),
        P(None, "tensor"),
        P("tensor"),
        P(),
        P(),
        P(),
        P("tensor"),
        P("tensor"),
        P("tensor"),
        P("tensor", None),
        P(rows, "tensor"),
    )
    out_specs = (
        P(rows, "tensor"),
        P(rows, "tensor"),
        P("tensor"),
        P(None, None, "tensor"),
        P("tensor", None, None),
        P(None, "tensor"),
        P(None, "tensor"),
        P("tensor"),
        P(),
        P(),
        P("tensor"),
        P("tensor"),
        P("tensor"),
        P("tensor"),
        P("tensor", None),
    )
    return jax.shard_map(
        shards, mesh=torus, in_specs=in_specs, out_specs=out_specs, check_vma=False
    )
```

```python
import jax
import jax.numpy as jnp
from jax import lax
from jax.experimental import pallas as pl
from jax.experimental.pallas import tpu as pltpu
from jax.sharding import Mesh
from jax.sharding import PartitionSpec as P

D = 1024
HEAD = 64
STATE = 128
INNER = 2048
ROWS = 256
HEADS = 16
LOCAL = 1024
HALO = 16
EXT = ROWS + HALO
LANES = 128
PAIRS = LOCAL // LANES
CHUNK = 80
DEVICES = 64
CONTEXT = ("context_0", "context_1")
EVERYONE = ("dp", "context_0", "context_1")
EPSILON = 1e-05
BC_COST = 10_000_000
TERMS_COST = 15_000_000
HIDDEN_COST = 9_000_000
BUNDLE_COST = 8_000_000
f32 = jnp.float32
bf16 = jnp.bfloat16
HIGHEST = lax.Precision.HIGHEST


def mm(a, b):
    return lax.dot_general(a, b, (((1,), (0,)), ((), ())), preferred_element_type=f32)


def nt(a, b):
    return lax.dot_general(a, b, (((1,), (1,)), ((), ())), preferred_element_type=f32)


def tn(a, b):
    return lax.dot_general(a, b, (((0,), (0,)), ((), ())), preferred_element_type=f32)


def exact(a, b):
    return lax.dot_general(
        a, b, (((1,), (0,)), ((), ())), precision=HIGHEST, preferred_element_type=f32
    )


def whole(shape, index=None):
    index = index or (0,) * len(shape)
    return pl.BlockSpec(shape, lambda i: index, pipeline_mode=pl.Buffered(1))


def kernel_call(body, outs, args, scratch=(), cost=0, vmem=24, blocks={}):
    return pl.pallas_call(
        body,
        grid=(1,),
        out_shape=[jax.ShapeDtypeStruct(shape, kind) for shape, kind in outs],
        in_specs=[whole(*blocks.get(i, (a.shape,))) for i, a in enumerate(args)],
        out_specs=[whole(shape) for shape, _ in outs],
        scratch_shapes=list(scratch),
        compiler_params=pltpu.CompilerParams(vmem_limit_bytes=vmem * 1024 * 1024),
        cost_estimate=pl.CostEstimate(flops=0, bytes_accessed=cost, transcendentals=0),
    )(*args)


def lane_index(shape):
    return lax.broadcasted_iota(jnp.int32, shape, 1)


def row_index(shape):
    return lax.broadcasted_iota(jnp.int32, shape, 0)


def spread_pair(columns, pair):
    rows = columns.shape[0]
    first = jnp.broadcast_to(columns[:, 2 * pair : 2 * pair + 1], (rows, LANES))
    second = jnp.broadcast_to(columns[:, 2 * pair + 1 : 2 * pair + 2], (rows, LANES))
    return jnp.where(lane_index((rows, LANES)) < HEAD, first, second)


def pair_mask(documents, seg_row):
    shape = (ROWS, ROWS)
    causal = row_index(shape) >= lane_index(shape)
    columns = jnp.concatenate([documents, documents], axis=1)
    return jnp.where((columns == seg_row) & causal, 0.0, -1e30).astype(f32)


def decay_block(cum, cum_t, head, bias):
    return jnp.exp(cum[:, head : head + 1] - cum_t[head : head + 1, :] + bias)


def document_before():
    piece = lax.axis_index("context_0") * 4 + lax.axis_index("context_1")
    return jnp.where(piece > 0, 2.0, 0.0).astype(f32)


def documents_of(seg_ref):
    seg_row = seg_ref[...].astype(f32) + 1.0
    return seg_row, jnp.broadcast_to(seg_row, (LANES, ROWS)).T


def tap_masks_of(documents, ext_ref):
    ext_ref[:8, :] = jnp.full((8, LANES), document_before(), f32)
    ext_ref[8:, :] = documents
    return [(ext_ref[5 + k : 5 + k + ROWS, :] == documents).astype(f32) for k in range(3)]


def end_decay(cum, documents):
    last = (documents == documents[ROWS - 1 : ROWS, :]).astype(f32)
    return jnp.exp(cum[ROWS - 1 : ROWS, :] - cum) * last


def entry_decay(cum, documents):
    return jnp.exp(cum) * (documents == document_before()).astype(f32)


def to_lanes(values):
    rows, count = values.shape
    return jnp.concatenate([values, jnp.zeros((rows, LANES - count), f32)], axis=1)


def front_body(
    hidden_ref,
    halo_ref,
    gain_ref,
    win_ref,
    wbc_ref,
    wst_ref,
    taps_ref,
    bias_ref,
    bc_taps_ref,
    bc_bias_ref,
    seg_ref,
    step_bias_ref,
    decay_log_ref,
    normed_ref,
    joined_ref,
    pre_ref,
    b_ref,
    c_ref,
    step_ref,
    cum_ref,
    sig_ref,
    decay_ref,
    state_ref,
    ext_ref,
    wide_ref,
):
    gain = gain_ref[...]
    for source, start, rows in ((halo_ref, 0, HALO), (hidden_ref, HALO, ROWS)):
        values = source[...].astype(f32)
        scale = lax.rsqrt(jnp.sum(values * values, axis=1, keepdims=True) / D + EPSILON)
        normed_ref[start : start + rows, :] = (values * scale * gain).astype(bf16)
    normed_ext = normed_ref[...]
    normed = normed_ref[HALO:, :]
    joined_ref[:, :LOCAL] = mm(normed_ext, win_ref[...])
    joined_ref[:, LOCAL:] = mm(normed_ext, wbc_ref[...])
    wide_ref[...] = jnp.zeros_like(wide_ref)
    wide_ref[:HEADS, :] = wst_ref[...]
    both = step_bias_ref[...]
    first = lax.axis_index("tensor") == 0
    local_bias = jnp.where(first, both[:, :HEADS], both[:, HEADS:])
    raw = nt(normed, wide_ref[...]) + to_lanes(local_bias)
    step = jnp.maximum(raw, 0.0) + jnp.log1p(jnp.exp(-jnp.abs(raw)))
    decay = step * to_lanes(-jnp.exp(decay_log_ref[...]))
    tri = (row_index((ROWS, ROWS)) >= lane_index((ROWS, ROWS))).astype(f32)
    cum = exact(tri, decay)
    step_ref[...] = step
    cum_ref[...] = cum
    sig_ref[...] = jax.nn.sigmoid(raw)
    decay_ref[...] = decay
    _, documents = documents_of(seg_ref)
    tap_masks = tap_masks_of(documents, ext_ref)

    def conv(at, taps, bias):
        lanes = slice(at, at + LANES)
        total = jnp.broadcast_to(bias, (ROWS, LANES))
        for k in range(4):
            part = joined_ref[HALO - 3 + k : HALO - 3 + k + ROWS, lanes] * taps[k : k + 1]
            total = total + (part * tap_masks[k] if k < 3 else part)
        pre_ref[:, lanes] = total
        return total * jax.nn.sigmoid(total)

    b_low = conv(LOCAL, bc_taps_ref[:, :STATE], bc_bias_ref[:, :STATE]).astype(bf16)
    c_low = conv(LOCAL + STATE, bc_taps_ref[:, STATE:], bc_bias_ref[:, STATE:]).astype(bf16)
    b_ref[...] = b_low
    c_ref[...] = c_low
    gains = jnp.exp(cum[ROWS - 1 : ROWS, :])
    ended = step * end_decay(cum, documents)
    for pair in range(PAIRS):
        lanes = slice(pair * LANES, (pair + 1) * LANES)
        x = conv(pair * LANES, taps_ref[:, lanes], bias_ref[:, lanes])
        state = tn((x * spread_pair(ended, pair)).astype(bf16), b_low).astype(bf16)
        for side in range(2):
            head = 2 * pair + side
            state_ref[head, :HEAD, :] = state[side * HEAD : (side + 1) * HEAD, :]
            state_ref[head, HEAD:, :] = jnp.broadcast_to(
                gains[:, head : head + 1], (CHUNK - HEAD, STATE)
            ).astype(bf16)


def gate_proj_body(normed_ref, win_ref, gate_ref):
    gate_ref[...] = mm(normed_ref[HALO:, :], win_ref[...])


def within_body(pre_ref, step_ref, cum_ref, b_ref, c_ref, seg_ref, skip_ref, within_ref):
    seg_row, documents = documents_of(seg_ref)
    products = nt(c_ref[...], b_ref[...])
    bias = pair_mask(documents, seg_row)
    step = step_ref[...]
    cum = cum_ref[...]
    cum_t = cum.T
    skip = skip_ref[...]
    first_half = lane_index((ROWS, LANES)) < HEAD
    for pair in range(PAIRS):
        lanes = slice(pair * LANES, (pair + 1) * LANES)
        pre = pre_ref[:, lanes]
        x = pre * jax.nn.sigmoid(pre)
        xs_low = (x * spread_pair(step, pair)).astype(bf16)
        sums = []
        for head in (2 * pair, 2 * pair + 1):
            block = (decay_block(cum, cum_t, head, bias) * products).astype(bf16)
            sums.append(mm(block, xs_low))
        within_ref[:, lanes] = (
            jnp.where(first_half, sums[0], sums[1]) + spread_pair(skip, pair) * x
        )


def scan_body(pieces_ref, start_ref):
    state = jnp.zeros((HEAD, STATE), f32)
    for k in range(16):
        start_ref[k] = state.astype(bf16)
        if k < 15:
            gain = pieces_ref[k, HEAD : HEAD + 16, :].astype(f32)[0:1, :]
            state = state * gain + pieces_ref[k, :HEAD, :].astype(f32)


def scan_back_body(pieces_ref, grads_ref, adjoint_ref):
    state = jnp.zeros((HEAD, STATE), f32)
    for k in reversed(range(16)):
        adjoint_ref[k] = state.astype(bf16)
        if k > 0:
            gain = pieces_ref[k, HEAD : HEAD + 16, :].astype(f32)[0:1, :]
            state = state * gain + grads_ref[k].astype(f32)


def mixed_body(
    within_ref, start_ref, c_ref, cum_ref, seg_ref, gate_ref, dg_ref, gain_ref, mixed_ref, sums_ref
):
    entry = entry_decay(cum_ref[...], documents_of(seg_ref)[1])
    c_low = c_ref[...]
    squares = jnp.zeros((ROWS, LANES), f32)
    dots = jnp.zeros((ROWS, LANES), f32)
    for pair in range(PAIRS):
        lanes = slice(pair * LANES, (pair + 1) * LANES)
        carried = nt(c_low, start_ref[lanes, :])
        mixed = within_ref[:, lanes] + spread_pair(entry, pair) * carried
        mixed_ref[:, lanes] = mixed
        gate = gate_ref[:, lanes]
        gated = mixed * (gate * jax.nn.sigmoid(gate))
        squares = squares + gated * gated
        dots = dots + gated * gain_ref[:, lanes] * dg_ref[:, lanes]
    lane = lane_index((ROWS, LANES))
    sums_ref[...] = jnp.where(
        lane == 0,
        jnp.sum(squares, axis=1, keepdims=True),
        jnp.where(lane == 1, jnp.sum(dots, axis=1, keepdims=True), 0.0),
    )


def gate_body(
    sums_ref,
    other_ref,
    mixed_ref,
    gate_ref,
    dg_ref,
    gain_ref,
    c_ref,
    cum_ref,
    seg_ref,
    cotangent_ref,
    normed_ref,
    gnorm_ref,
    d_mixed_ref,
    d_gate_ref,
    grad_gain_ref,
    d_start_ref,
    grad_out_ref,
    grad_gate_ref,
):
    normed_t = normed_ref[HALO:, :].T
    cotangent = cotangent_ref[...]
    sums = sums_ref[...] + other_ref[...]
    rate = lax.rsqrt(sums[:, 0:1] / INNER + EPSILON)
    back = rate * rate * rate * sums[:, 1:2] / INNER
    rate = jnp.broadcast_to(rate, (ROWS, LANES))
    back = jnp.broadcast_to(back, (ROWS, LANES))
    entry = entry_decay(cum_ref[...], documents_of(seg_ref)[1])
    c_low = c_ref[...]
    for pair in range(PAIRS):
        lanes = slice(pair * LANES, (pair + 1) * LANES)
        mixed = mixed_ref[:, lanes]
        gate = gate_ref[:, lanes]
        gain = gain_ref[:, lanes]
        dg = dg_ref[:, lanes]
        sig = jax.nn.sigmoid(gate)
        silu = gate * sig
        gated = mixed * silu
        scaled = gated * rate
        gnorm_ref[:, lanes] = (scaled * gain).astype(bf16)
        grad_gain_ref[:, lanes] = jnp.sum(dg * scaled, axis=0, keepdims=True)
        d_gated = rate * gain * dg - gated * back
        d_mixed = d_gated * silu
        d_mixed_ref[:, lanes] = d_mixed
        d_gate_ref[:, lanes] = (d_gated * mixed * (sig + silu * (1.0 - sig))).astype(bf16)
        d_state = tn((d_mixed * spread_pair(entry, pair)).astype(bf16), c_low).astype(bf16)
        for side in range(2):
            d_start_ref[2 * pair + side] = d_state[side * HEAD : (side + 1) * HEAD, :]
        if pair % 2 == 1:
            group = slice((pair - 1) * LANES, (pair + 1) * LANES)
            grad_out_ref[group, :] = tn(gnorm_ref[:, group], cotangent).astype(bf16)
            grad_gate_ref[:, group] = mm(normed_t, d_gate_ref[:, group]).astype(bf16)


def head_sums(values, pair):
    shape = (LANES, LANES)
    into = lane_index(shape) == 2 * pair + (row_index(shape) >= HEAD).astype(jnp.int32)
    into = into.astype(bf16)
    high = values.astype(bf16)
    low = (values - high.astype(f32)).astype(bf16)
    return mm(high, into) + mm(low, into)


def conv_back(d_pre, joined_ref, source, lanes, taps, masks, pad_ref, into):
    total = None
    sums = []
    for k in range(4):
        joined = joined_ref[HALO - 3 + k : HALO - 3 + k + ROWS, source]
        part = d_pre * masks[k] if k < 3 else d_pre
        sums.append(jnp.sum(part * joined, axis=0, keepdims=True))
        pad_ref[k, 24 : 24 + ROWS, :] = part * taps[k : k + 1]
        moved = pad_ref[k, 24 - 13 - k : 24 - 13 - k + EXT, :]
        total = moved if total is None else total + moved
    sums.append(jnp.sum(d_pre, axis=0, keepdims=True))
    into[:, lanes] = jnp.concatenate(sums + [jnp.zeros((3, LANES), f32)], axis=0)
    return total


def back_body(
    d_mixed_ref,
    pre_ref,
    within_ref,
    start_ref,
    b_ref,
    c_ref,
    step_ref,
    cum_ref,
    seg_ref,
    skip_ref,
    d_xs_ref,
    d_bc_ref,
    d_cum_ref,
    skip_grad_ref,
):
    seg_row, documents = documents_of(seg_ref)
    skips = skip_ref[...]
    cum = cum_ref[...]
    cum_t = cum.T
    step = step_ref[...]
    b_low = b_ref[...]
    c_low = c_ref[...]
    products = nt(c_low, b_low)
    bias = pair_mask(documents, seg_row)
    entry = entry_decay(cum, documents)
    first_half = lane_index((ROWS, LANES)) < HEAD
    d_products = jnp.zeros((ROWS, ROWS), f32)
    d_c = jnp.zeros((ROWS, STATE), f32)
    d_cum = jnp.zeros((ROWS, LANES), f32)
    for pair in range(PAIRS):
        lanes = slice(pair * LANES, (pair + 1) * LANES)
        pre = pre_ref[:, lanes]
        x = pre * jax.nn.sigmoid(pre)
        xs_low = (x * spread_pair(step, pair)).astype(bf16)
        d_mixed = d_mixed_ref[:, lanes]
        dy_low = d_mixed.astype(bf16)
        zero = jnp.zeros_like(dy_low)
        parts = []
        for side in range(2):
            head = 2 * pair + side
            own = jnp.where(first_half if side == 0 else ~first_half, dy_low, zero)
            decays = decay_block(cum, cum_t, head, bias)
            d_products = d_products + decays * nt(own, xs_low)
            parts.append(tn((decays * products).astype(bf16), dy_low))
        d_xs = jnp.where(first_half, parts[0], parts[1])
        d_xs_ref[:, lanes] = d_xs
        within = within_ref[:, lanes] - spread_pair(skips, pair) * x
        through = dy_low.astype(f32) * within - xs_low.astype(f32) * d_xs
        start_low = start_ref[lanes, :]
        carried = d_mixed * spread_pair(entry, pair)
        d_c = d_c + mm(carried.astype(bf16), start_low)
        d_cum = d_cum + head_sums(through + carried * nt(c_low, start_low), pair)
        skip_grad_ref[:, lanes] = jnp.sum(d_mixed * x, axis=0, keepdims=True)
    d_products = d_products.astype(bf16)
    d_bc_ref[:, :STATE] = tn(d_products, c_low)
    d_bc_ref[:, STATE:] = d_c + mm(d_products, b_low)
    d_cum_ref[...] = d_cum


def carry_back_body(
    d_mixed_ref,
    pre_ref,
    joined_ref,
    d_xs_ref,
    d_bc_in_ref,
    d_cum_ref,
    start_ref,
    adjoint_ref,
    b_ref,
    step_ref,
    cum_ref,
    sig_ref,
    decay_ref,
    seg_ref,
    decay_log_ref,
    skip_ref,
    taps_ref,
    d_bc_ref,
    d_ext_ref,
    d_step_ref,
    conv_ref,
    small_ref,
    ext_ref,
    pad_ref,
):
    _, documents = documents_of(seg_ref)
    tap_masks = tap_masks_of(documents, ext_ref)
    pad_ref[...] = jnp.zeros_like(pad_ref)
    skips = skip_ref[...]
    cum = cum_ref[...]
    step = step_ref[...]
    b_low = b_ref[...]
    end = end_decay(cum, documents)
    gains = jnp.exp(cum[ROWS - 1 : ROWS, :])
    lane = lane_index((1, LANES))
    d_b = d_bc_in_ref[:, :STATE]
    d_cum = d_cum_ref[...]
    d_step = jnp.zeros((ROWS, LANES), f32)
    d_last = jnp.zeros((8, LANES), f32)
    d_whole = jnp.zeros((1, LANES), f32)
    for pair in range(PAIRS):
        lanes = slice(pair * LANES, (pair + 1) * LANES)
        pre = pre_ref[:, lanes]
        sig = jax.nn.sigmoid(pre)
        x = pre * sig
        steps = spread_pair(step, pair)
        ends = spread_pair(end, pair)
        xs = x * steps
        adjoint_low = adjoint_ref[lanes, :]
        d_ended = nt(b_low, adjoint_low) * ends
        d_b = d_b + mm((xs * ends).astype(bf16), adjoint_low)
        at_end = xs * d_ended
        d_cum = d_cum - head_sums(at_end, pair)
        d_xs = d_xs_ref[:, lanes] + d_ended
        d_step = d_step + head_sums(x * d_xs, pair)
        end_sum = jnp.sum(at_end, axis=0, keepdims=True)
        d_last = d_last + head_sums(jnp.broadcast_to(end_sum, (8, LANES)), pair)
        meeting = start_ref[lanes, :].astype(f32) * adjoint_low.astype(f32)
        for side in range(2):
            whole_sum = jnp.sum(
                jnp.sum(meeting[side * HEAD : (side + 1) * HEAD, :], axis=0, keepdims=True),
                axis=1,
                keepdims=True,
            )
            d_whole = d_whole + jnp.where(lane == 2 * pair + side, whole_sum, 0.0)
        d_act = steps * d_xs + spread_pair(skips, pair) * d_mixed_ref[:, lanes]
        d_pre = d_act * (sig + x * (1.0 - sig))
        d_ext_ref[:, lanes] = conv_back(
            d_pre, joined_ref, lanes, lanes, taps_ref[:, lanes], tap_masks, pad_ref, conv_ref
        ).astype(bf16)
    d_bc_ref[:, :STATE] = d_b.astype(bf16)
    d_bc_ref[:, STATE:] = d_bc_in_ref[:, STATE:].astype(bf16)
    tri = (row_index((ROWS, ROWS)) <= lane_index((ROWS, ROWS))).astype(f32)
    d_decay = exact(tri, d_cum) + (d_last[0:1, :] + gains * d_whole)
    d_raw = (d_step + d_decay * to_lanes(-jnp.exp(decay_log_ref[...]))) * sig_ref[...]
    d_step_ref[...] = d_raw.astype(bf16)
    small_ref[...] = jnp.concatenate(
        [
            jnp.sum(d_raw, axis=0, keepdims=True),
            jnp.sum(d_decay * decay_ref[...], axis=0, keepdims=True),
            jnp.zeros((6, LANES), f32),
        ],
        axis=0,
    )


def bc_back_body(
    own_ref, other_ref, pre_ref, joined_ref, seg_ref, taps_ref, d_ext_ref, conv_ref, ext_ref, pad_ref
):
    _, documents = documents_of(seg_ref)
    tap_masks = tap_masks_of(documents, ext_ref)
    pad_ref[...] = jnp.zeros_like(pad_ref)
    for half in range(2):
        lanes = slice(half * LANES, (half + 1) * LANES)
        source = slice(LOCAL + half * LANES, LOCAL + (half + 1) * LANES)
        pre = pre_ref[:, source]
        sig = jax.nn.sigmoid(pre)
        d_act = own_ref[:, lanes].astype(f32) + other_ref[:, lanes].astype(f32)
        d_pre = d_act * (sig + pre * sig * (1.0 - sig))
        d_ext_ref[:, lanes] = conv_back(
            d_pre, joined_ref, source, lanes, taps_ref[:, lanes], tap_masks, pad_ref, conv_ref
        ).astype(bf16)


def terms_body(dx_ref, dz_ref, dst_ref, dbc_ref, win_ref, wst_ref, wbc_ref, out_ref):
    first = lax.axis_index("tensor") == 0
    dbc = dbc_ref[...]
    wbc = wbc_ref[...]
    half = jnp.where(first, dbc[:, :STATE], dbc[:, STATE:])
    weights = jnp.where(first, wbc[:, :STATE], wbc[:, STATE:])
    both = nt(dx_ref[...], win_ref[:, :LOCAL]) + nt(half, weights)
    out_ref[:HALO, :] = both[:HALO, :].astype(bf16)
    own = nt(dz_ref[...], win_ref[:, LOCAL:]) + mm(dst_ref[:, :HEADS], wst_ref[...])
    out_ref[HALO:, :] = (both[HALO:, :] + own).astype(bf16)


def hidden_body(
    hidden_ref, terms_ref, other_ref, returned_ref, gain_ref, out_grad_ref, grad_ref, gain_grad_ref
):
    values = hidden_ref[...].astype(f32)
    scale = lax.rsqrt(jnp.sum(values * values, axis=1, keepdims=True) / D + EPSILON)
    d_normed = terms_ref[HALO:, :].astype(f32) + other_ref[HALO:, :].astype(f32)
    tail = jnp.concatenate(
        [jnp.zeros((ROWS - HALO, D), f32), returned_ref[...].astype(f32)], axis=0
    )
    d_normed = d_normed + tail
    first = lax.axis_index("tensor") == 0
    half = D // 2
    grads = jnp.sum(d_normed * values * scale, axis=0, keepdims=True)
    gain_grad_ref[...] = jnp.where(first, grads[:, :half], grads[:, half:])
    scaled = d_normed * gain_ref[...]
    dots = jnp.sum(values * scaled, axis=1, keepdims=True)
    result = scale * scaled - values * (scale * scale * scale * dots / D)
    own = jnp.where(first, result[:, :half], result[:, half:])
    grad_ref[...] = (out_grad_ref[...].astype(f32) + own).astype(bf16)


def x_grad_body(normed_ref, dx_ref, grad_ref):
    grad_ref[...] = tn(normed_ref[...], dx_ref[...]).astype(bf16)


def bundle_body(
    normed_ref,
    dbc_ref,
    dst_ref,
    conv_ref,
    bc_conv_ref,
    gate_gain_ref,
    norm_gain_ref,
    skip_ref,
    small_ref,
    bundle_ref,
):
    half = D // 2
    first = lax.axis_index("tensor") == 0
    share = jnp.where(first, normed_ref[:, :half], normed_ref[:, half:])
    bundle_ref[:half, :] = tn(share, dbc_ref[...]).astype(bf16)
    steps = tn(dst_ref[...], normed_ref[HALO:, :])
    for part in range(4):
        at = half + part * HEADS
        bundle_ref[at : at + HEADS, :] = steps[:HEADS, part * 256 : part * 256 + 256].astype(bf16)
    row = half + 4 * HEADS
    pieces = []
    for part in range(4):
        pieces.append(conv_ref[:, part * 256 : part * 256 + 256])
    pieces.append(bc_conv_ref[...])
    lone = [gate_gain_ref[:, part * 256 : part * 256 + 256] for part in range(4)]
    lone += [norm_gain_ref[:, part * 256 : part * 256 + 256] for part in range(2)]
    lone += [jnp.concatenate([small_ref[0:1, :], small_ref[1:2, :]], axis=1)]
    lone += [jnp.zeros((1, 256), f32)]
    pieces.append(jnp.concatenate(lone, axis=0))
    skips = skip_ref[...]
    pieces.append(
        jnp.concatenate(
            [skips[:, part * 256 : part * 256 + 256] for part in range(4)]
            + [jnp.zeros((4, 256), f32)],
            axis=0,
        )
    )
    pieces.append(jnp.zeros((8, 256), f32))
    bundle_ref[row : row + 64, :] = jnp.concatenate(pieces, axis=0).astype(bf16)
    bundle_ref[row + 64 :, :] = jnp.zeros((half - 4 * HEADS - 64, 256), bf16)


def total_body(x_ref, few_ref, out_ref):
    for received_ref, lanes in ((x_ref, slice(0, LOCAL)), (few_ref, slice(LOCAL, LOCAL + 256))):
        total = jnp.zeros(received_ref.shape[1:], f32)
        for k in range(DEVICES):
            total = total + received_ref[k].astype(f32)
        total = total.astype(bf16)
        for k in range(DEVICES):
            out_ref[k, :, lanes] = total


def few_body(
    final_ref,
    bc_ref,
    step_ref,
    conv_ref,
    conv_bias_ref,
    bc_conv_ref,
    bc_conv_bias_ref,
    gate_gain_ref,
    norm_gain_ref,
    skip_ref,
    step_bias_ref,
    decay_log_ref,
):
    half = D // 2
    grads = final_ref[:half, LOCAL:].astype(f32)
    bc_ref[:, 0, :] = grads[:, :STATE]
    bc_ref[:, 1, :] = grads[:, STATE:]
    rest = final_ref[half : half + 128, LOCAL:].astype(f32)
    for part in range(4):
        step_ref[:, part * 256 : part * 256 + 256] = rest[part * HEADS : (part + 1) * HEADS]
    conv = jnp.concatenate([rest[64 + part * 8 : 72 + part * 8] for part in range(4)], axis=1)
    conv_ref[...] = conv[:4]
    conv_bias_ref[...] = conv[4:5]
    bc = rest[96:104]
    for side in range(2):
        lanes = slice(side * STATE, (side + 1) * STATE)
        bc_conv_ref[:, side, :] = bc[:4, lanes]
        bc_conv_bias_ref[side : side + 1, :] = bc[4:5, lanes]
    lone = rest[104:112]
    gate_gain_ref[...] = jnp.concatenate([lone[part : part + 1] for part in range(4)], axis=1)
    norm_gain_ref[...] = jnp.concatenate([lone[part : part + 1] for part in range(4, 6)], axis=1)
    step_bias_ref[...] = lone[6:7, :HEADS]
    decay_log_ref[...] = lone[6:7, LANES : LANES + HEADS]
    skips = rest[112:116]
    total = jnp.zeros((1, LANES), f32)
    lane = lane_index((1, LANES))
    for head in range(HEADS):
        at = (head % 4) * HEAD
        own = jnp.sum(
            skips[head // 4 : head // 4 + 1, at : at + HEAD], axis=1, keepdims=True
        )
        total = total + jnp.where(lane == head, own, 0.0)
    skip_ref[...] = total[:, :HEADS]


PARTS = 4


def x_rows_body(final_ref, grad_in_ref, wide_ref, sem):
    wide_ref[...] = final_ref[...].astype(f32)
    copy = pltpu.make_async_copy(wide_ref, grad_in_ref.at[:, 0, :], sem)
    copy.start()
    copy.wait()


def early_rows_body(
    _, gate_ref, out_ref, grad_in_ref, grad_out_ref, low_ref, wide_ref, in_sems, out_sems
):
    size = D // PARTS
    loads, stores = [], []
    for part in range(PARTS):
        rows = slice(part * size, (part + 1) * size)
        for which, source in enumerate((gate_ref, out_ref)):
            loads.append(
                pltpu.make_async_copy(
                    source.at[rows, :], low_ref.at[which, rows, :], in_sems.at[which, part]
                )
            )
    for load in loads:
        load.start()
    for part in range(PARTS):
        rows = slice(part * size, (part + 1) * size)
        for which in range(2):
            target = grad_out_ref.at[rows, :] if which else grad_in_ref.at[rows, 1, :]
            loads[2 * part + which].wait()
            wide_ref[which, rows, :] = low_ref[which, rows, :].astype(f32)
            stores.append(
                pltpu.make_async_copy(
                    wide_ref.at[which, rows, :], target, out_sems.at[which, part]
                )
            )
            stores[-1].start()
    for store in stores:
        store.wait()


def swapped(values):
    return lax.ppermute(values, "tensor", [(0, 1), (1, 0)])


def shards(
    hidden_in,
    segment_ids,
    norm_gain,
    in_weight,
    bc_weight,
    step_weight,
    conv_weight,
    conv_bias,
    bc_conv_weight,
    bc_conv_bias,
    step_bias,
    decay_log,
    skip_gain,
    gate_gain,
    out_weight,
    out_grad,
):
    side = lax.axis_index("tensor")
    width = hidden_in.shape[1]
    gathered = lax.all_gather(hidden_in, "tensor", axis=1, tiled=True)
    halo = lax.ppermute(gathered[ROWS - HALO :], CONTEXT, [(i, i + 1) for i in range(15)])
    win = in_weight.reshape(D, 2 * LOCAL)
    wbc = bc_weight.reshape(D, 2 * STATE)
    bc_taps = bc_conv_weight.reshape(4, 2 * STATE)
    segs = segment_ids[None]
    skip = skip_gain[None]
    step_rows = step_weight.T
    gain_row = gate_gain[None]
    ext_scratch = pltpu.VMEM((ROWS + 8, LANES), f32)
    pad_scratch = pltpu.VMEM((4, ROWS + 48, LANES), f32)
    (
        normed_ext,
        joined,
        pre,
        b_low,
        c_low,
        step,
        cum,
        sig,
        decay,
        state,
    ) = kernel_call(
        front_body,
        [
            ((EXT, D), bf16),
            ((EXT, LOCAL + 2 * STATE), f32),
            ((ROWS, LOCAL + 2 * STATE), f32),
            ((ROWS, STATE), bf16),
            ((ROWS, STATE), bf16),
            ((ROWS, LANES), f32),
            ((ROWS, LANES), f32),
            ((ROWS, LANES), f32),
            ((ROWS, LANES), f32),
            ((HEADS, CHUNK, STATE), bf16),
        ],
        (
            gathered,
            halo,
            norm_gain[None],
            win,
            wbc,
            step_rows,
            conv_weight,
            conv_bias[None],
            bc_taps,
            bc_conv_bias.reshape(1, 2 * STATE),
            segs,
            step_bias[None],
            decay_log[None],
        ),
        scratch=[ext_scratch, pltpu.VMEM((LANES, D), bf16)],
        blocks={3: ((D, LOCAL), (0, 0))},
    )
    late_grad, state = lax.optimization_barrier((out_grad, state))
    cotangent = lax.all_gather(late_grad, "tensor", axis=1, tiled=True)
    dg = nt(cotangent, out_weight)
    pieces = lax.all_to_all(state, CONTEXT, 0, 0, tiled=True)
    (gate,) = kernel_call(
        gate_proj_body,
        [((ROWS, LOCAL), f32)],
        (normed_ext, win),
        blocks={1: ((D, LOCAL), (0, 1))},
    )
    (within,) = kernel_call(
        within_body,
        [((ROWS, LOCAL), f32)],
        (pre, step, cum, b_low, c_low, segs, skip),
        cost=12_000_000,
    )
    pieces, dg = lax.optimization_barrier((pieces, dg))
    (starts,) = kernel_call(scan_body, [((16, HEAD, STATE), bf16)], (pieces,))
    start = lax.all_to_all(starts, CONTEXT, 0, 0, tiled=True).reshape(LOCAL, STATE)
    mixed, sums = kernel_call(
        mixed_body,
        [((ROWS, LOCAL), f32), ((ROWS, LANES), f32)],
        (within, start, c_low, cum, segs, gate, dg, gain_row),
    )
    gnorm, d_mixed, d_gate, grad_gate_gain, d_start, grad_out, grad_gate = kernel_call(
        gate_body,
        [
            ((ROWS, LOCAL), bf16),
            ((ROWS, LOCAL), f32),
            ((ROWS, LOCAL), bf16),
            ((1, LOCAL), f32),
            ((HEADS, HEAD, STATE), bf16),
            ((LOCAL, D), bf16),
            ((D, LOCAL), bf16),
        ],
        (sums, swapped(sums), mixed, gate, dg, gain_row, c_low, cum, segs, cotangent, normed_ext),
    )
    grad_out, grad_gate = lax.psum((grad_out, grad_gate), EVERYONE)
    def later(
        d_start,
        gnorm,
        d_mixed,
        d_gate,
        grad_gate_gain,
        start,
        pieces,
        within,
        normed_ext,
        joined,
        pre,
        gathered,
        win,
    ):
        received = lax.all_to_all(d_start, CONTEXT, 0, 0, tiled=True)
        (adjoints,) = kernel_call(
            scan_back_body, [((16, HEAD, STATE), bf16)], (pieces, received)
        )
        adjoint = lax.all_to_all(adjoints, CONTEXT, 0, 0, tiled=True).reshape(LOCAL, STATE)
        out_terms = mm(gnorm, out_weight).astype(bf16)
        kept = lax.dynamic_slice_in_dim(out_terms, side * width, width, 1)
        given = lax.dynamic_slice_in_dim(out_terms, (1 - side) * width, width, 1)
        hidden_out = (
            hidden_in.astype(f32) + kept.astype(f32) + swapped(given).astype(f32)
        ).astype(bf16)
        d_xs, d_bc_part, d_cum, skip_grads = kernel_call(
            back_body,
            [
                ((ROWS, LOCAL), f32),
                ((ROWS, 2 * STATE), f32),
                ((ROWS, LANES), f32),
                ((1, LOCAL), f32),
            ],
            (d_mixed, pre, within, start, b_low, c_low, step, cum, segs, skip),
            cost=20_000_000,
        )
        d_bc, d_ext, d_step, conv_grads, small = kernel_call(
            carry_back_body,
            [
                ((ROWS, 2 * STATE), bf16),
                ((EXT, LOCAL), bf16),
                ((ROWS, LANES), bf16),
                ((8, LOCAL), f32),
                ((8, LANES), f32),
            ],
            (
                d_mixed,
                pre,
                joined,
                d_xs,
                d_bc_part,
                d_cum,
                start,
                adjoint,
                b_low,
                step,
                cum,
                sig,
                decay,
                segs,
                decay_log[None],
                skip,
                conv_weight,
            ),
            scratch=[ext_scratch, pad_scratch],
        )
        (grad_x,) = kernel_call(x_grad_body, [((D, LOCAL), bf16)], (normed_ext, d_ext))
        scattered_x = lax.all_to_all(
            grad_x.reshape(DEVICES, 16, LOCAL), EVERYONE, 0, 0, tiled=True
        )
        d_bc_ext, bc_conv_grads = kernel_call(
            bc_back_body,
            [((EXT, 2 * STATE), bf16), ((8, 2 * STATE), f32)],
            (d_bc, swapped(d_bc), pre, joined, segs, bc_taps),
            scratch=[ext_scratch, pad_scratch],
            cost=BC_COST,
        )
        (terms,) = kernel_call(
            terms_body,
            [((EXT, D), bf16)],
            (d_ext, d_gate, d_step, d_bc_ext, win, step_rows, wbc),
            cost=TERMS_COST,
        )
        other_terms = swapped(terms)
        halo_terms = (terms[:HALO].astype(f32) + other_terms[:HALO].astype(f32)).astype(bf16)
        returned = lax.ppermute(halo_terms, CONTEXT, [(i + 1, i) for i in range(15)])
        hidden_grad, grad_norm = kernel_call(
            hidden_body,
            [((ROWS, width), bf16), ((1, width), f32)],
            (gathered, terms, other_terms, returned, norm_gain[None], out_grad),
            cost=HIDDEN_COST,
        )
        (bundle,) = kernel_call(
            bundle_body,
            [((D, 256), bf16)],
            (
                normed_ext,
                d_bc_ext,
                d_step,
                conv_grads,
                bc_conv_grads,
                grad_gate_gain,
                grad_norm,
                skip_grads,
                small,
            ),
            cost=BUNDLE_COST,
        )
        bundle, scattered_x = lax.optimization_barrier((bundle, scattered_x))
        scattered = lax.all_to_all(
            bundle.reshape(DEVICES, 16, 256), EVERYONE, 0, 0, tiled=True
        )
        (spread,) = kernel_call(
            total_body, [((DEVICES, 16, LOCAL + 256), bf16)], (scattered_x, scattered)
        )
        final = lax.all_to_all(spread, EVERYONE, 0, 0, tiled=True).reshape(D, LOCAL + 256)
        return hidden_out, hidden_grad, final

    def nothing(*_):
        return (
            jnp.zeros((ROWS, width), bf16),
            jnp.zeros((ROWS, width), bf16),
            jnp.zeros((D, LOCAL + 256), bf16),
        )

    hidden_out, hidden_grad, final = lax.cond(
        segment_ids[0] >= 0,
        later,
        nothing,
        d_start,
        gnorm,
        d_mixed,
        d_gate,
        grad_gate_gain,
        start,
        pieces,
        within,
        normed_ext,
        joined,
        pre,
        gathered,
        win,
    )
    half = D // 2
    (
        grad_bc,
        grad_step,
        grad_conv,
        grad_conv_bias,
        grad_bc_conv,
        grad_bc_conv_bias,
        total_gate_gain,
        total_norm_gain,
        grad_skip,
        grad_step_bias,
        grad_decay_log,
    ) = kernel_call(
        few_body,
        [
            ((half, 2, STATE), f32),
            ((HEADS, D), f32),
            ((4, LOCAL), f32),
            ((1, LOCAL), f32),
            ((4, 2, STATE), f32),
            ((2, STATE), f32),
            ((1, LOCAL), f32),
            ((1, half), f32),
            ((1, HEADS), f32),
            ((1, HEADS), f32),
            ((1, HEADS), f32),
        ],
        (final,),
    )
    anywhere = pl.BlockSpec(memory_space=pl.ANY)
    params = pltpu.CompilerParams(vmem_limit_bytes=60 * 1024 * 1024)
    grad_in = pl.pallas_call(
        x_rows_body,
        grid=(1,),
        out_shape=jax.ShapeDtypeStruct((D, 2, LOCAL), f32),
        in_specs=[whole((D, LOCAL))],
        out_specs=anywhere,
        scratch_shapes=[pltpu.VMEM((D, LOCAL), f32), pltpu.SemaphoreType.DMA],
        compiler_params=params,
    )(final)
    grad_in, grad_out = pl.pallas_call(
        early_rows_body,
        out_shape=[
            jax.ShapeDtypeStruct((D, 2, LOCAL), f32),
            jax.ShapeDtypeStruct((LOCAL, D), f32),
        ],
        in_specs=[anywhere] * 3,
        out_specs=[anywhere] * 2,
        scratch_shapes=[
            pltpu.VMEM((2, D, LOCAL), bf16),
            pltpu.VMEM((2, D, LOCAL), f32),
            pltpu.SemaphoreType.DMA((2, PARTS)),
            pltpu.SemaphoreType.DMA((2, PARTS)),
        ],
        input_output_aliases={0: 0},
        compiler_params=params,
    )(grad_in, grad_gate, grad_out)
    return (
        hidden_out,
        hidden_grad,
        total_norm_gain[0],
        grad_in,
        grad_bc,
        grad_step.T,
        grad_conv,
        grad_conv_bias[0],
        grad_bc_conv,
        grad_bc_conv_bias,
        grad_step_bias[0],
        grad_decay_log[0],
        grad_skip[0],
        total_gate_gain[0],
        grad_out,
    )


def solution(mesh):
    torus = Mesh(
        mesh.devices.reshape(mesh.shape["tensor"], mesh.shape["dp"], 4, 4),
        ("tensor", "dp", "context_0", "context_1"),
    )
    rows = ("dp", "context_0", "context_1")
    in_specs = (
        P(rows, "tensor"),
        P(rows),
        P(),
        P(None, None, "tensor"),
        P(),
        P(None, "tensor"),
        P(None, "tensor"),
        P("tensor"),
        P(),
        P(),
        P(),
        P("tensor"),
        P("tensor"),
        P("tensor"),
        P("tensor", None),
        P(rows, "tensor"),
    )
    out_specs = (
        P(rows, "tensor"),
        P(rows, "tensor"),
        P("tensor"),
        P(None, None, "tensor"),
        P("tensor", None, None),
        P(None, "tensor"),
        P(None, "tensor"),
        P("tensor"),
        P(),
        P(),
        P("tensor"),
        P("tensor"),
        P("tensor"),
        P("tensor"),
        P("tensor", None),
    )
    return jax.shard_map(
        shards, mesh=torus, in_specs=in_specs, out_specs=out_specs, check_vma=False
    )
```

```python
import jax
import jax.numpy as jnp
from jax import lax
from jax.experimental import pallas as pl
from jax.experimental.pallas import tpu as pltpu
from jax.sharding import Mesh
from jax.sharding import PartitionSpec as P

D = 1024
HEAD = 64
STATE = 128
INNER = 2048
ROWS = 256
HEADS = 16
LOCAL = 1024
HALO = 16
EXT = ROWS + HALO
LANES = 128
PAIRS = LOCAL // LANES
CHUNK = 80
DEVICES = 64
CONTEXT = ("context_0", "context_1")
EVERYONE = ("dp", "context_0", "context_1")
EPSILON = 1e-05
BC_COST = 10_000_000
TERMS_COST = 15_000_000
HIDDEN_COST = 9_000_000
BUNDLE_COST = 8_000_000
f32 = jnp.float32
bf16 = jnp.bfloat16
HIGHEST = lax.Precision.HIGHEST


def mm(a, b):
    return lax.dot_general(a, b, (((1,), (0,)), ((), ())), preferred_element_type=f32)


def nt(a, b):
    return lax.dot_general(a, b, (((1,), (1,)), ((), ())), preferred_element_type=f32)


def tn(a, b):
    return lax.dot_general(a, b, (((0,), (0,)), ((), ())), preferred_element_type=f32)


def exact(a, b):
    return lax.dot_general(
        a, b, (((1,), (0,)), ((), ())), precision=HIGHEST, preferred_element_type=f32
    )


def whole(shape, index=None):
    index = index or (0,) * len(shape)
    return pl.BlockSpec(shape, lambda i: index, pipeline_mode=pl.Buffered(1))


def kernel_call(body, outs, args, scratch=(), cost=0, vmem=24, blocks={}):
    return pl.pallas_call(
        body,
        grid=(1,),
        out_shape=[jax.ShapeDtypeStruct(shape, kind) for shape, kind in outs],
        in_specs=[whole(*blocks.get(i, (a.shape,))) for i, a in enumerate(args)],
        out_specs=[whole(shape) for shape, _ in outs],
        scratch_shapes=list(scratch),
        compiler_params=pltpu.CompilerParams(vmem_limit_bytes=vmem * 1024 * 1024),
        cost_estimate=pl.CostEstimate(flops=0, bytes_accessed=cost, transcendentals=0),
    )(*args)


def lane_index(shape):
    return lax.broadcasted_iota(jnp.int32, shape, 1)


def row_index(shape):
    return lax.broadcasted_iota(jnp.int32, shape, 0)


def spread_pair(columns, pair):
    rows = columns.shape[0]
    first = jnp.broadcast_to(columns[:, 2 * pair : 2 * pair + 1], (rows, LANES))
    second = jnp.broadcast_to(columns[:, 2 * pair + 1 : 2 * pair + 2], (rows, LANES))
    return jnp.where(lane_index((rows, LANES)) < HEAD, first, second)


def pair_mask(documents, seg_row):
    shape = (ROWS, ROWS)
    causal = row_index(shape) >= lane_index(shape)
    columns = jnp.concatenate([documents, documents], axis=1)
    return jnp.where((columns == seg_row) & causal, 0.0, -1e30).astype(f32)


def decay_block(cum, cum_t, head, bias):
    return jnp.exp(cum[:, head : head + 1] - cum_t[head : head + 1, :] + bias)


def document_before():
    piece = lax.axis_index("context_0") * 4 + lax.axis_index("context_1")
    return jnp.where(piece > 0, 2.0, 0.0).astype(f32)


def documents_of(seg_ref):
    seg_row = seg_ref[...].astype(f32) + 1.0
    return seg_row, jnp.broadcast_to(seg_row, (LANES, ROWS)).T


def tap_masks_of(documents, ext_ref):
    ext_ref[:8, :] = jnp.full((8, LANES), document_before(), f32)
    ext_ref[8:, :] = documents
    return [(ext_ref[5 + k : 5 + k + ROWS, :] == documents).astype(f32) for k in range(3)]


def end_decay(cum, documents):
    last = (documents == documents[ROWS - 1 : ROWS, :]).astype(f32)
    return jnp.exp(cum[ROWS - 1 : ROWS, :] - cum) * last


def entry_decay(cum, documents):
    return jnp.exp(cum) * (documents == document_before()).astype(f32)


def to_lanes(values):
    rows, count = values.shape
    return jnp.concatenate([values, jnp.zeros((rows, LANES - count), f32)], axis=1)


def front_body(
    hidden_ref,
    halo_ref,
    gain_ref,
    win_ref,
    wbc_ref,
    wst_ref,
    taps_ref,
    bias_ref,
    bc_taps_ref,
    bc_bias_ref,
    seg_ref,
    step_bias_ref,
    decay_log_ref,
    normed_ref,
    joined_ref,
    pre_ref,
    b_ref,
    c_ref,
    step_ref,
    cum_ref,
    sig_ref,
    decay_ref,
    state_ref,
    ext_ref,
    wide_ref,
):
    gain = gain_ref[...]
    for source, start, rows in ((halo_ref, 0, HALO), (hidden_ref, HALO, ROWS)):
        values = source[...].astype(f32)
        scale = lax.rsqrt(jnp.sum(values * values, axis=1, keepdims=True) / D + EPSILON)
        normed_ref[start : start + rows, :] = (values * scale * gain).astype(bf16)
    normed_ext = normed_ref[...]
    normed = normed_ref[HALO:, :]
    joined_ref[:, :LOCAL] = mm(normed_ext, win_ref[...])
    joined_ref[:, LOCAL:] = mm(normed_ext, wbc_ref[...])
    wide_ref[...] = jnp.zeros_like(wide_ref)
    wide_ref[:HEADS, :] = wst_ref[...]
    both = step_bias_ref[...]
    first = lax.axis_index("tensor") == 0
    local_bias = jnp.where(first, both[:, :HEADS], both[:, HEADS:])
    raw = nt(normed, wide_ref[...]) + to_lanes(local_bias)
    step = jnp.maximum(raw, 0.0) + jnp.log1p(jnp.exp(-jnp.abs(raw)))
    decay = step * to_lanes(-jnp.exp(decay_log_ref[...]))
    tri = (row_index((ROWS, ROWS)) >= lane_index((ROWS, ROWS))).astype(f32)
    cum = exact(tri, decay)
    step_ref[...] = step
    cum_ref[...] = cum
    sig_ref[...] = jax.nn.sigmoid(raw)
    decay_ref[...] = decay
    _, documents = documents_of(seg_ref)
    tap_masks = tap_masks_of(documents, ext_ref)

    def conv(at, taps, bias):
        lanes = slice(at, at + LANES)
        total = jnp.broadcast_to(bias, (ROWS, LANES))
        for k in range(4):
            part = joined_ref[HALO - 3 + k : HALO - 3 + k + ROWS, lanes] * taps[k : k + 1]
            total = total + (part * tap_masks[k] if k < 3 else part)
        pre_ref[:, lanes] = total
        return total * jax.nn.sigmoid(total)

    b_low = conv(LOCAL, bc_taps_ref[:, :STATE], bc_bias_ref[:, :STATE]).astype(bf16)
    c_low = conv(LOCAL + STATE, bc_taps_ref[:, STATE:], bc_bias_ref[:, STATE:]).astype(bf16)
    b_ref[...] = b_low
    c_ref[...] = c_low
    gains = jnp.exp(cum[ROWS - 1 : ROWS, :])
    ended = step * end_decay(cum, documents)
    for pair in range(PAIRS):
        lanes = slice(pair * LANES, (pair + 1) * LANES)
        x = conv(pair * LANES, taps_ref[:, lanes], bias_ref[:, lanes])
        state = tn((x * spread_pair(ended, pair)).astype(bf16), b_low).astype(bf16)
        for side in range(2):
            head = 2 * pair + side
            state_ref[head, :HEAD, :] = state[side * HEAD : (side + 1) * HEAD, :]
            state_ref[head, HEAD:, :] = jnp.broadcast_to(
                gains[:, head : head + 1], (CHUNK - HEAD, STATE)
            ).astype(bf16)


def gate_proj_body(normed_ref, win_ref, gate_ref):
    gate_ref[...] = mm(normed_ref[HALO:, :], win_ref[...])


def within_body(pre_ref, step_ref, cum_ref, b_ref, c_ref, seg_ref, skip_ref, within_ref):
    seg_row, documents = documents_of(seg_ref)
    products = nt(c_ref[...], b_ref[...])
    bias = pair_mask(documents, seg_row)
    step = step_ref[...]
    cum = cum_ref[...]
    cum_t = cum.T
    skip = skip_ref[...]
    first_half = lane_index((ROWS, LANES)) < HEAD
    for pair in range(PAIRS):
        lanes = slice(pair * LANES, (pair + 1) * LANES)
        pre = pre_ref[:, lanes]
        x = pre * jax.nn.sigmoid(pre)
        xs_low = (x * spread_pair(step, pair)).astype(bf16)
        sums = []
        for head in (2 * pair, 2 * pair + 1):
            block = (decay_block(cum, cum_t, head, bias) * products).astype(bf16)
            sums.append(mm(block, xs_low))
        within_ref[:, lanes] = (
            jnp.where(first_half, sums[0], sums[1]) + spread_pair(skip, pair) * x
        )


def scan_body(pieces_ref, start_ref):
    state = jnp.zeros((HEAD, STATE), f32)
    for k in range(16):
        start_ref[k] = state.astype(bf16)
        if k < 15:
            gain = pieces_ref[k, HEAD : HEAD + 16, :].astype(f32)[0:1, :]
            state = state * gain + pieces_ref[k, :HEAD, :].astype(f32)


def scan_back_body(pieces_ref, grads_ref, adjoint_ref):
    state = jnp.zeros((HEAD, STATE), f32)
    for k in reversed(range(16)):
        adjoint_ref[k] = state.astype(bf16)
        if k > 0:
            gain = pieces_ref[k, HEAD : HEAD + 16, :].astype(f32)[0:1, :]
            state = state * gain + grads_ref[k].astype(f32)


def mixed_body(
    within_ref, start_ref, c_ref, cum_ref, seg_ref, gate_ref, dg_ref, gain_ref, mixed_ref, sums_ref
):
    entry = entry_decay(cum_ref[...], documents_of(seg_ref)[1])
    c_low = c_ref[...]
    squares = jnp.zeros((ROWS, LANES), f32)
    dots = jnp.zeros((ROWS, LANES), f32)
    for pair in range(PAIRS):
        lanes = slice(pair * LANES, (pair + 1) * LANES)
        carried = nt(c_low, start_ref[lanes, :])
        mixed = within_ref[:, lanes] + spread_pair(entry, pair) * carried
        mixed_ref[:, lanes] = mixed
        gate = gate_ref[:, lanes]
        gated = mixed * (gate * jax.nn.sigmoid(gate))
        squares = squares + gated * gated
        dots = dots + gated * gain_ref[:, lanes] * dg_ref[:, lanes]
    lane = lane_index((ROWS, LANES))
    sums_ref[...] = jnp.where(
        lane == 0,
        jnp.sum(squares, axis=1, keepdims=True),
        jnp.where(lane == 1, jnp.sum(dots, axis=1, keepdims=True), 0.0),
    )


def gate_body(
    sums_ref,
    other_ref,
    mixed_ref,
    gate_ref,
    dg_ref,
    gain_ref,
    c_ref,
    cum_ref,
    seg_ref,
    cotangent_ref,
    gnorm_ref,
    d_mixed_ref,
    d_gate_ref,
    grad_gain_ref,
    d_start_ref,
    grad_out_ref,
):
    cotangent = cotangent_ref[...]
    sums = sums_ref[...] + other_ref[...]
    rate = lax.rsqrt(sums[:, 0:1] / INNER + EPSILON)
    back = rate * rate * rate * sums[:, 1:2] / INNER
    rate = jnp.broadcast_to(rate, (ROWS, LANES))
    back = jnp.broadcast_to(back, (ROWS, LANES))
    entry = entry_decay(cum_ref[...], documents_of(seg_ref)[1])
    c_low = c_ref[...]
    for pair in range(PAIRS):
        lanes = slice(pair * LANES, (pair + 1) * LANES)
        mixed = mixed_ref[:, lanes]
        gate = gate_ref[:, lanes]
        gain = gain_ref[:, lanes]
        dg = dg_ref[:, lanes]
        sig = jax.nn.sigmoid(gate)
        silu = gate * sig
        gated = mixed * silu
        scaled = gated * rate
        gnorm_ref[:, lanes] = (scaled * gain).astype(bf16)
        grad_gain_ref[:, lanes] = jnp.sum(dg * scaled, axis=0, keepdims=True)
        d_gated = rate * gain * dg - gated * back
        d_mixed = d_gated * silu
        d_mixed_ref[:, lanes] = d_mixed
        d_gate_ref[:, lanes] = (d_gated * mixed * (sig + silu * (1.0 - sig))).astype(bf16)
        d_state = tn((d_mixed * spread_pair(entry, pair)).astype(bf16), c_low).astype(bf16)
        for side in range(2):
            d_start_ref[2 * pair + side] = d_state[side * HEAD : (side + 1) * HEAD, :]
        if pair % 2 == 1:
            group = slice((pair - 1) * LANES, (pair + 1) * LANES)
            grad_out_ref[group, :] = tn(gnorm_ref[:, group], cotangent).astype(bf16)


def gate_grad_body(normed_ref, d_gate_ref, grad_ref):
    grad_ref[...] = tn(normed_ref[HALO:, :], d_gate_ref[...]).astype(bf16)


def head_sums(values, pair):
    shape = (LANES, LANES)
    into = lane_index(shape) == 2 * pair + (row_index(shape) >= HEAD).astype(jnp.int32)
    into = into.astype(bf16)
    high = values.astype(bf16)
    low = (values - high.astype(f32)).astype(bf16)
    return mm(high, into) + mm(low, into)


def conv_back(d_pre, joined_ref, source, lanes, taps, masks, pad_ref, into):
    total = None
    sums = []
    for k in range(4):
        joined = joined_ref[HALO - 3 + k : HALO - 3 + k + ROWS, source]
        part = d_pre * masks[k] if k < 3 else d_pre
        sums.append(jnp.sum(part * joined, axis=0, keepdims=True))
        pad_ref[k, 24 : 24 + ROWS, :] = part * taps[k : k + 1]
        moved = pad_ref[k, 24 - 13 - k : 24 - 13 - k + EXT, :]
        total = moved if total is None else total + moved
    sums.append(jnp.sum(d_pre, axis=0, keepdims=True))
    into[:, lanes] = jnp.concatenate(sums + [jnp.zeros((3, LANES), f32)], axis=0)
    return total


def back_body(
    d_mixed_ref,
    pre_ref,
    within_ref,
    start_ref,
    b_ref,
    c_ref,
    step_ref,
    cum_ref,
    seg_ref,
    skip_ref,
    d_xs_ref,
    d_bc_ref,
    d_cum_ref,
    skip_grad_ref,
):
    seg_row, documents = documents_of(seg_ref)
    skips = skip_ref[...]
    cum = cum_ref[...]
    cum_t = cum.T
    step = step_ref[...]
    b_low = b_ref[...]
    c_low = c_ref[...]
    products = nt(c_low, b_low)
    bias = pair_mask(documents, seg_row)
    entry = entry_decay(cum, documents)
    first_half = lane_index((ROWS, LANES)) < HEAD
    d_products = jnp.zeros((ROWS, ROWS), f32)
    d_c = jnp.zeros((ROWS, STATE), f32)
    d_cum = jnp.zeros((ROWS, LANES), f32)
    for pair in range(PAIRS):
        lanes = slice(pair * LANES, (pair + 1) * LANES)
        pre = pre_ref[:, lanes]
        x = pre * jax.nn.sigmoid(pre)
        xs_low = (x * spread_pair(step, pair)).astype(bf16)
        d_mixed = d_mixed_ref[:, lanes]
        dy_low = d_mixed.astype(bf16)
        zero = jnp.zeros_like(dy_low)
        parts = []
        for side in range(2):
            head = 2 * pair + side
            own = jnp.where(first_half if side == 0 else ~first_half, dy_low, zero)
            decays = decay_block(cum, cum_t, head, bias)
            d_products = d_products + decays * nt(own, xs_low)
            parts.append(tn((decays * products).astype(bf16), dy_low))
        d_xs = jnp.where(first_half, parts[0], parts[1])
        d_xs_ref[:, lanes] = d_xs
        within = within_ref[:, lanes] - spread_pair(skips, pair) * x
        through = dy_low.astype(f32) * within - xs_low.astype(f32) * d_xs
        start_low = start_ref[lanes, :]
        carried = d_mixed * spread_pair(entry, pair)
        d_c = d_c + mm(carried.astype(bf16), start_low)
        d_cum = d_cum + head_sums(through + carried * nt(c_low, start_low), pair)
        skip_grad_ref[:, lanes] = jnp.sum(d_mixed * x, axis=0, keepdims=True)
    d_products = d_products.astype(bf16)
    d_bc_ref[:, :STATE] = tn(d_products, c_low)
    d_bc_ref[:, STATE:] = d_c + mm(d_products, b_low)
    d_cum_ref[...] = d_cum


def carry_back_body(
    d_mixed_ref,
    pre_ref,
    joined_ref,
    d_xs_ref,
    d_bc_in_ref,
    d_cum_ref,
    start_ref,
    adjoint_ref,
    b_ref,
    step_ref,
    cum_ref,
    sig_ref,
    decay_ref,
    seg_ref,
    decay_log_ref,
    skip_ref,
    taps_ref,
    d_bc_ref,
    d_ext_ref,
    d_step_ref,
    conv_ref,
    small_ref,
    ext_ref,
    pad_ref,
):
    _, documents = documents_of(seg_ref)
    tap_masks = tap_masks_of(documents, ext_ref)
    pad_ref[...] = jnp.zeros_like(pad_ref)
    skips = skip_ref[...]
    cum = cum_ref[...]
    step = step_ref[...]
    b_low = b_ref[...]
    end = end_decay(cum, documents)
    gains = jnp.exp(cum[ROWS - 1 : ROWS, :])
    lane = lane_index((1, LANES))
    d_b = d_bc_in_ref[:, :STATE]
    d_cum = d_cum_ref[...]
    d_step = jnp.zeros((ROWS, LANES), f32)
    d_last = jnp.zeros((8, LANES), f32)
    d_whole = jnp.zeros((1, LANES), f32)
    for pair in range(PAIRS):
        lanes = slice(pair * LANES, (pair + 1) * LANES)
        pre = pre_ref[:, lanes]
        sig = jax.nn.sigmoid(pre)
        x = pre * sig
        steps = spread_pair(step, pair)
        ends = spread_pair(end, pair)
        xs = x * steps
        adjoint_low = adjoint_ref[lanes, :]
        d_ended = nt(b_low, adjoint_low) * ends
        d_b = d_b + mm((xs * ends).astype(bf16), adjoint_low)
        at_end = xs * d_ended
        d_cum = d_cum - head_sums(at_end, pair)
        d_xs = d_xs_ref[:, lanes] + d_ended
        d_step = d_step + head_sums(x * d_xs, pair)
        end_sum = jnp.sum(at_end, axis=0, keepdims=True)
        d_last = d_last + head_sums(jnp.broadcast_to(end_sum, (8, LANES)), pair)
        meeting = start_ref[lanes, :].astype(f32) * adjoint_low.astype(f32)
        for side in range(2):
            whole_sum = jnp.sum(
                jnp.sum(meeting[side * HEAD : (side + 1) * HEAD, :], axis=0, keepdims=True),
                axis=1,
                keepdims=True,
            )
            d_whole = d_whole + jnp.where(lane == 2 * pair + side, whole_sum, 0.0)
        d_act = steps * d_xs + spread_pair(skips, pair) * d_mixed_ref[:, lanes]
        d_pre = d_act * (sig + x * (1.0 - sig))
        d_ext_ref[:, lanes] = conv_back(
            d_pre, joined_ref, lanes, lanes, taps_ref[:, lanes], tap_masks, pad_ref, conv_ref
        ).astype(bf16)
    d_bc_ref[:, :STATE] = d_b.astype(bf16)
    d_bc_ref[:, STATE:] = d_bc_in_ref[:, STATE:].astype(bf16)
    tri = (row_index((ROWS, ROWS)) <= lane_index((ROWS, ROWS))).astype(f32)
    d_decay = exact(tri, d_cum) + (d_last[0:1, :] + gains * d_whole)
    d_raw = (d_step + d_decay * to_lanes(-jnp.exp(decay_log_ref[...]))) * sig_ref[...]
    d_step_ref[...] = d_raw.astype(bf16)
    small_ref[...] = jnp.concatenate(
        [
            jnp.sum(d_raw, axis=0, keepdims=True),
            jnp.sum(d_decay * decay_ref[...], axis=0, keepdims=True),
            jnp.zeros((6, LANES), f32),
        ],
        axis=0,
    )


def bc_back_body(
    own_ref, other_ref, pre_ref, joined_ref, seg_ref, taps_ref, d_ext_ref, conv_ref, ext_ref, pad_ref
):
    _, documents = documents_of(seg_ref)
    tap_masks = tap_masks_of(documents, ext_ref)
    pad_ref[...] = jnp.zeros_like(pad_ref)
    for half in range(2):
        lanes = slice(half * LANES, (half + 1) * LANES)
        source = slice(LOCAL + half * LANES, LOCAL + (half + 1) * LANES)
        pre = pre_ref[:, source]
        sig = jax.nn.sigmoid(pre)
        d_act = own_ref[:, lanes].astype(f32) + other_ref[:, lanes].astype(f32)
        d_pre = d_act * (sig + pre * sig * (1.0 - sig))
        d_ext_ref[:, lanes] = conv_back(
            d_pre, joined_ref, source, lanes, taps_ref[:, lanes], tap_masks, pad_ref, conv_ref
        ).astype(bf16)


def terms_body(dx_ref, dz_ref, dst_ref, dbc_ref, win_ref, wst_ref, wbc_ref, out_ref):
    first = lax.axis_index("tensor") == 0
    dbc = dbc_ref[...]
    wbc = wbc_ref[...]
    half = jnp.where(first, dbc[:, :STATE], dbc[:, STATE:])
    weights = jnp.where(first, wbc[:, :STATE], wbc[:, STATE:])
    both = nt(dx_ref[...], win_ref[:, :LOCAL]) + nt(half, weights)
    out_ref[:HALO, :] = both[:HALO, :].astype(bf16)
    own = nt(dz_ref[...], win_ref[:, LOCAL:]) + mm(dst_ref[:, :HEADS], wst_ref[...])
    out_ref[HALO:, :] = (both[HALO:, :] + own).astype(bf16)


def hidden_body(
    hidden_ref, terms_ref, other_ref, returned_ref, gain_ref, out_grad_ref, grad_ref, gain_grad_ref
):
    values = hidden_ref[...].astype(f32)
    scale = lax.rsqrt(jnp.sum(values * values, axis=1, keepdims=True) / D + EPSILON)
    d_normed = terms_ref[HALO:, :].astype(f32) + other_ref[HALO:, :].astype(f32)
    tail = jnp.concatenate(
        [jnp.zeros((ROWS - HALO, D), f32), returned_ref[...].astype(f32)], axis=0
    )
    d_normed = d_normed + tail
    first = lax.axis_index("tensor") == 0
    half = D // 2
    grads = jnp.sum(d_normed * values * scale, axis=0, keepdims=True)
    gain_grad_ref[...] = jnp.where(first, grads[:, :half], grads[:, half:])
    scaled = d_normed * gain_ref[...]
    dots = jnp.sum(values * scaled, axis=1, keepdims=True)
    result = scale * scaled - values * (scale * scale * scale * dots / D)
    own = jnp.where(first, result[:, :half], result[:, half:])
    grad_ref[...] = (out_grad_ref[...].astype(f32) + own).astype(bf16)


def x_grad_body(normed_ref, dx_ref, grad_ref):
    grad_ref[...] = tn(normed_ref[...], dx_ref[...]).astype(bf16)


def bundle_body(
    normed_ref,
    dbc_ref,
    dst_ref,
    conv_ref,
    bc_conv_ref,
    gate_gain_ref,
    norm_gain_ref,
    skip_ref,
    small_ref,
    bundle_ref,
):
    half = D // 2
    first = lax.axis_index("tensor") == 0
    share = jnp.where(first, normed_ref[:, :half], normed_ref[:, half:])
    bundle_ref[:half, :] = tn(share, dbc_ref[...]).astype(bf16)
    steps = tn(dst_ref[...], normed_ref[HALO:, :])
    for part in range(4):
        at = half + part * HEADS
        bundle_ref[at : at + HEADS, :] = steps[:HEADS, part * 256 : part * 256 + 256].astype(bf16)
    row = half + 4 * HEADS
    pieces = []
    for part in range(4):
        pieces.append(conv_ref[:, part * 256 : part * 256 + 256])
    pieces.append(bc_conv_ref[...])
    lone = [gate_gain_ref[:, part * 256 : part * 256 + 256] for part in range(4)]
    lone += [norm_gain_ref[:, part * 256 : part * 256 + 256] for part in range(2)]
    lone += [jnp.concatenate([small_ref[0:1, :], small_ref[1:2, :]], axis=1)]
    lone += [jnp.zeros((1, 256), f32)]
    pieces.append(jnp.concatenate(lone, axis=0))
    skips = skip_ref[...]
    pieces.append(
        jnp.concatenate(
            [skips[:, part * 256 : part * 256 + 256] for part in range(4)]
            + [jnp.zeros((4, 256), f32)],
            axis=0,
        )
    )
    pieces.append(jnp.zeros((8, 256), f32))
    bundle_ref[row : row + 64, :] = jnp.concatenate(pieces, axis=0).astype(bf16)
    bundle_ref[row + 64 :, :] = jnp.zeros((half - 4 * HEADS - 64, 256), bf16)


def total_body(x_ref, few_ref, out_ref):
    for received_ref, lanes in ((x_ref, slice(0, LOCAL)), (few_ref, slice(LOCAL, LOCAL + 256))):
        total = jnp.zeros(received_ref.shape[1:], f32)
        for k in range(DEVICES):
            total = total + received_ref[k].astype(f32)
        total = total.astype(bf16)
        for k in range(DEVICES):
            out_ref[k, :, lanes] = total


def few_body(
    final_ref,
    bc_ref,
    step_ref,
    conv_ref,
    conv_bias_ref,
    bc_conv_ref,
    bc_conv_bias_ref,
    gate_gain_ref,
    norm_gain_ref,
    skip_ref,
    step_bias_ref,
    decay_log_ref,
):
    half = D // 2
    grads = final_ref[:half, LOCAL:].astype(f32)
    bc_ref[:, 0, :] = grads[:, :STATE]
    bc_ref[:, 1, :] = grads[:, STATE:]
    rest = final_ref[half : half + 128, LOCAL:].astype(f32)
    for part in range(4):
        step_ref[:, part * 256 : part * 256 + 256] = rest[part * HEADS : (part + 1) * HEADS]
    conv = jnp.concatenate([rest[64 + part * 8 : 72 + part * 8] for part in range(4)], axis=1)
    conv_ref[...] = conv[:4]
    conv_bias_ref[...] = conv[4:5]
    bc = rest[96:104]
    for side in range(2):
        lanes = slice(side * STATE, (side + 1) * STATE)
        bc_conv_ref[:, side, :] = bc[:4, lanes]
        bc_conv_bias_ref[side : side + 1, :] = bc[4:5, lanes]
    lone = rest[104:112]
    gate_gain_ref[...] = jnp.concatenate([lone[part : part + 1] for part in range(4)], axis=1)
    norm_gain_ref[...] = jnp.concatenate([lone[part : part + 1] for part in range(4, 6)], axis=1)
    step_bias_ref[...] = lone[6:7, :HEADS]
    decay_log_ref[...] = lone[6:7, LANES : LANES + HEADS]
    skips = rest[112:116]
    total = jnp.zeros((1, LANES), f32)
    lane = lane_index((1, LANES))
    for head in range(HEADS):
        at = (head % 4) * HEAD
        own = jnp.sum(
            skips[head // 4 : head // 4 + 1, at : at + HEAD], axis=1, keepdims=True
        )
        total = total + jnp.where(lane == head, own, 0.0)
    skip_ref[...] = total[:, :HEADS]


PARTS = 8


def x_rows_body(final_ref, grad_in_ref, wide_ref, sem):
    wide_ref[...] = final_ref[...].astype(f32)
    copy = pltpu.make_async_copy(wide_ref, grad_in_ref.at[:, 0, :], sem)
    copy.start()
    copy.wait()


def early_rows_body(
    _, gate_ref, out_ref, grad_in_ref, grad_out_ref, low_ref, wide_ref, in_sems, out_sems
):
    size = D // PARTS
    loads, stores = [], []
    for part in range(PARTS):
        rows = slice(part * size, (part + 1) * size)
        for which, source in enumerate((gate_ref, out_ref)):
            loads.append(
                pltpu.make_async_copy(
                    source.at[rows, :], low_ref.at[which, rows, :], in_sems.at[which, part]
                )
            )
    for load in loads:
        load.start()
    for part in range(PARTS):
        rows = slice(part * size, (part + 1) * size)
        for which in range(2):
            target = grad_out_ref.at[rows, :] if which else grad_in_ref.at[rows, 1, :]
            loads[2 * part + which].wait()
            wide_ref[which, rows, :] = low_ref[which, rows, :].astype(f32)
            stores.append(
                pltpu.make_async_copy(
                    wide_ref.at[which, rows, :], target, out_sems.at[which, part]
                )
            )
            stores[-1].start()
    for store in stores:
        store.wait()


def swapped(values):
    return lax.ppermute(values, "tensor", [(0, 1), (1, 0)])


def shards(
    hidden_in,
    segment_ids,
    norm_gain,
    in_weight,
    bc_weight,
    step_weight,
    conv_weight,
    conv_bias,
    bc_conv_weight,
    bc_conv_bias,
    step_bias,
    decay_log,
    skip_gain,
    gate_gain,
    out_weight,
    out_grad,
):
    side = lax.axis_index("tensor")
    width = hidden_in.shape[1]
    gathered = lax.all_gather(hidden_in, "tensor", axis=1, tiled=True)
    halo = lax.ppermute(gathered[ROWS - HALO :], CONTEXT, [(i, i + 1) for i in range(15)])
    win = in_weight.reshape(D, 2 * LOCAL)
    wbc = bc_weight.reshape(D, 2 * STATE)
    bc_taps = bc_conv_weight.reshape(4, 2 * STATE)
    segs = segment_ids[None]
    skip = skip_gain[None]
    step_rows = step_weight.T
    gain_row = gate_gain[None]
    ext_scratch = pltpu.VMEM((ROWS + 8, LANES), f32)
    pad_scratch = pltpu.VMEM((4, ROWS + 48, LANES), f32)
    (
        normed_ext,
        joined,
        pre,
        b_low,
        c_low,
        step,
        cum,
        sig,
        decay,
        state,
    ) = kernel_call(
        front_body,
        [
            ((EXT, D), bf16),
            ((EXT, LOCAL + 2 * STATE), f32),
            ((ROWS, LOCAL + 2 * STATE), f32),
            ((ROWS, STATE), bf16),
            ((ROWS, STATE), bf16),
            ((ROWS, LANES), f32),
            ((ROWS, LANES), f32),
            ((ROWS, LANES), f32),
            ((ROWS, LANES), f32),
            ((HEADS, CHUNK, STATE), bf16),
        ],
        (
            gathered,
            halo,
            norm_gain[None],
            win,
            wbc,
            step_rows,
            conv_weight,
            conv_bias[None],
            bc_taps,
            bc_conv_bias.reshape(1, 2 * STATE),
            segs,
            step_bias[None],
            decay_log[None],
        ),
        scratch=[ext_scratch, pltpu.VMEM((LANES, D), bf16)],
        blocks={3: ((D, LOCAL), (0, 0))},
    )
    late_grad, state = lax.optimization_barrier((out_grad, state))
    cotangent = lax.all_gather(late_grad, "tensor", axis=1, tiled=True)
    dg = nt(cotangent, out_weight)
    pieces = lax.all_to_all(state, CONTEXT, 0, 0, tiled=True)
    (gate,) = kernel_call(
        gate_proj_body,
        [((ROWS, LOCAL), f32)],
        (normed_ext, win),
        blocks={1: ((D, LOCAL), (0, 1))},
    )
    (within,) = kernel_call(
        within_body,
        [((ROWS, LOCAL), f32)],
        (pre, step, cum, b_low, c_low, segs, skip),
        cost=12_000_000,
    )
    pieces, dg = lax.optimization_barrier((pieces, dg))
    (starts,) = kernel_call(scan_body, [((16, HEAD, STATE), bf16)], (pieces,))
    start = lax.all_to_all(starts, CONTEXT, 0, 0, tiled=True).reshape(LOCAL, STATE)
    mixed, sums = kernel_call(
        mixed_body,
        [((ROWS, LOCAL), f32), ((ROWS, LANES), f32)],
        (within, start, c_low, cum, segs, gate, dg, gain_row),
    )
    gnorm, d_mixed, d_gate, grad_gate_gain, d_start, grad_out = kernel_call(
        gate_body,
        [
            ((ROWS, LOCAL), bf16),
            ((ROWS, LOCAL), f32),
            ((ROWS, LOCAL), bf16),
            ((1, LOCAL), f32),
            ((HEADS, HEAD, STATE), bf16),
            ((LOCAL, D), bf16),
        ],
        (sums, swapped(sums), mixed, gate, dg, gain_row, c_low, cum, segs, cotangent),
    )
    (grad_gate,) = kernel_call(gate_grad_body, [((D, LOCAL), bf16)], (normed_ext, d_gate))
    grad_out, grad_gate = lax.psum((grad_out, grad_gate), EVERYONE)
    def later(
        d_start,
        gnorm,
        d_mixed,
        d_gate,
        grad_gate_gain,
        start,
        pieces,
        within,
        normed_ext,
        joined,
        pre,
        gathered,
        win,
    ):
        received = lax.all_to_all(d_start, CONTEXT, 0, 0, tiled=True)
        (adjoints,) = kernel_call(
            scan_back_body, [((16, HEAD, STATE), bf16)], (pieces, received)
        )
        adjoint = lax.all_to_all(adjoints, CONTEXT, 0, 0, tiled=True).reshape(LOCAL, STATE)
        out_terms = mm(gnorm, out_weight).astype(bf16)
        kept = lax.dynamic_slice_in_dim(out_terms, side * width, width, 1)
        given = lax.dynamic_slice_in_dim(out_terms, (1 - side) * width, width, 1)
        hidden_out = (
            hidden_in.astype(f32) + kept.astype(f32) + swapped(given).astype(f32)
        ).astype(bf16)
        d_xs, d_bc_part, d_cum, skip_grads = kernel_call(
            back_body,
            [
                ((ROWS, LOCAL), f32),
                ((ROWS, 2 * STATE), f32),
                ((ROWS, LANES), f32),
                ((1, LOCAL), f32),
            ],
            (d_mixed, pre, within, start, b_low, c_low, step, cum, segs, skip),
            cost=20_000_000,
        )
        d_bc, d_ext, d_step, conv_grads, small = kernel_call(
            carry_back_body,
            [
                ((ROWS, 2 * STATE), bf16),
                ((EXT, LOCAL), bf16),
                ((ROWS, LANES), bf16),
                ((8, LOCAL), f32),
                ((8, LANES), f32),
            ],
            (
                d_mixed,
                pre,
                joined,
                d_xs,
                d_bc_part,
                d_cum,
                start,
                adjoint,
                b_low,
                step,
                cum,
                sig,
                decay,
                segs,
                decay_log[None],
                skip,
                conv_weight,
            ),
            scratch=[ext_scratch, pad_scratch],
        )
        (grad_x,) = kernel_call(x_grad_body, [((D, LOCAL), bf16)], (normed_ext, d_ext))
        scattered_x = lax.all_to_all(
            grad_x.reshape(DEVICES, 16, LOCAL), EVERYONE, 0, 0, tiled=True
        )
        d_bc_ext, bc_conv_grads = kernel_call(
            bc_back_body,
            [((EXT, 2 * STATE), bf16), ((8, 2 * STATE), f32)],
            (d_bc, swapped(d_bc), pre, joined, segs, bc_taps),
            scratch=[ext_scratch, pad_scratch],
            cost=BC_COST,
        )
        (terms,) = kernel_call(
            terms_body,
            [((EXT, D), bf16)],
            (d_ext, d_gate, d_step, d_bc_ext, win, step_rows, wbc),
            cost=TERMS_COST,
        )
        other_terms = swapped(terms)
        halo_terms = (terms[:HALO].astype(f32) + other_terms[:HALO].astype(f32)).astype(bf16)
        returned = lax.ppermute(halo_terms, CONTEXT, [(i + 1, i) for i in range(15)])
        hidden_grad, grad_norm = kernel_call(
            hidden_body,
            [((ROWS, width), bf16), ((1, width), f32)],
            (gathered, terms, other_terms, returned, norm_gain[None], out_grad),
            cost=HIDDEN_COST,
        )
        (bundle,) = kernel_call(
            bundle_body,
            [((D, 256), bf16)],
            (
                normed_ext,
                d_bc_ext,
                d_step,
                conv_grads,
                bc_conv_grads,
                grad_gate_gain,
                grad_norm,
                skip_grads,
                small,
            ),
            cost=BUNDLE_COST,
        )
        bundle, scattered_x = lax.optimization_barrier((bundle, scattered_x))
        scattered = lax.all_to_all(
            bundle.reshape(DEVICES, 16, 256), EVERYONE, 0, 0, tiled=True
        )
        (spread,) = kernel_call(
            total_body, [((DEVICES, 16, LOCAL + 256), bf16)], (scattered_x, scattered)
        )
        final = lax.all_to_all(spread, EVERYONE, 0, 0, tiled=True).reshape(D, LOCAL + 256)
        return hidden_out, hidden_grad, final

    def nothing(*_):
        return (
            jnp.zeros((ROWS, width), bf16),
            jnp.zeros((ROWS, width), bf16),
            jnp.zeros((D, LOCAL + 256), bf16),
        )

    hidden_out, hidden_grad, final = lax.cond(
        segment_ids[0] >= 0,
        later,
        nothing,
        d_start,
        gnorm,
        d_mixed,
        d_gate,
        grad_gate_gain,
        start,
        pieces,
        within,
        normed_ext,
        joined,
        pre,
        gathered,
        win,
    )
    half = D // 2
    (
        grad_bc,
        grad_step,
        grad_conv,
        grad_conv_bias,
        grad_bc_conv,
        grad_bc_conv_bias,
        total_gate_gain,
        total_norm_gain,
        grad_skip,
        grad_step_bias,
        grad_decay_log,
    ) = kernel_call(
        few_body,
        [
            ((half, 2, STATE), f32),
            ((HEADS, D), f32),
            ((4, LOCAL), f32),
            ((1, LOCAL), f32),
            ((4, 2, STATE), f32),
            ((2, STATE), f32),
            ((1, LOCAL), f32),
            ((1, half), f32),
            ((1, HEADS), f32),
            ((1, HEADS), f32),
            ((1, HEADS), f32),
        ],
        (final,),
    )
    anywhere = pl.BlockSpec(memory_space=pl.ANY)
    params = pltpu.CompilerParams(vmem_limit_bytes=60 * 1024 * 1024)
    grad_in = pl.pallas_call(
        x_rows_body,
        grid=(1,),
        out_shape=jax.ShapeDtypeStruct((D, 2, LOCAL), f32),
        in_specs=[whole((D, LOCAL))],
        out_specs=anywhere,
        scratch_shapes=[pltpu.VMEM((D, LOCAL), f32), pltpu.SemaphoreType.DMA],
        compiler_params=params,
    )(final)
    grad_in, grad_out = pl.pallas_call(
        early_rows_body,
        out_shape=[
            jax.ShapeDtypeStruct((D, 2, LOCAL), f32),
            jax.ShapeDtypeStruct((LOCAL, D), f32),
        ],
        in_specs=[anywhere] * 3,
        out_specs=[anywhere] * 2,
        scratch_shapes=[
            pltpu.VMEM((2, D, LOCAL), bf16),
            pltpu.VMEM((2, D, LOCAL), f32),
            pltpu.SemaphoreType.DMA((2, PARTS)),
            pltpu.SemaphoreType.DMA((2, PARTS)),
        ],
        input_output_aliases={0: 0},
        compiler_params=params,
    )(grad_in, grad_gate, grad_out)
    return (
        hidden_out,
        hidden_grad,
        total_norm_gain[0],
        grad_in,
        grad_bc,
        grad_step.T,
        grad_conv,
        grad_conv_bias[0],
        grad_bc_conv,
        grad_bc_conv_bias,
        grad_step_bias[0],
        grad_decay_log[0],
        grad_skip[0],
        total_gate_gain[0],
        grad_out,
    )


def solution(mesh):
    torus = Mesh(
        mesh.devices.reshape(mesh.shape["tensor"], mesh.shape["dp"], 4, 4),
        ("tensor", "dp", "context_0", "context_1"),
    )
    rows = ("dp", "context_0", "context_1")
    in_specs = (
        P(rows, "tensor"),
        P(rows),
        P(),
        P(None, None, "tensor"),
        P(),
        P(None, "tensor"),
        P(None, "tensor"),
        P("tensor"),
        P(),
        P(),
        P(),
        P("tensor"),
        P("tensor"),
        P("tensor"),
        P("tensor", None),
        P(rows, "tensor"),
    )
    out_specs = (
        P(rows, "tensor"),
        P(rows, "tensor"),
        P("tensor"),
        P(None, None, "tensor"),
        P("tensor", None, None),
        P(None, "tensor"),
        P(None, "tensor"),
        P("tensor"),
        P(),
        P(),
        P("tensor"),
        P("tensor"),
        P("tensor"),
        P("tensor"),
        P("tensor", None),
    )
    return jax.shard_map(
        shards, mesh=torus, in_specs=in_specs, out_specs=out_specs, check_vma=False
    )
```
